32 devices in a mesh: dp: 2 (over core), fsdp: 16 (over z, y, x).
Axes of the slice: x: 2, y: 2, z: 4, core: 2. Of those that a mesh axis runs over, the one named last changes fastest.
Arguments:
- tokens: bfloat16 [32768, 1024], P(('dp', 'fsdp')), may hold values from -18 to 18
- condition: bfloat16 [128, 768], P(('dp', 'fsdp')), may hold values from -6 to 6
- shapes: int32 [128, 2], P(('dp', 'fsdp')), may hold values from 8 to 32, as said below
- cotangent: bfloat16 [32768, 1024], P(('dp', 'fsdp')), may hold values from -6 to 6
- ada_weight: float32 [2, 768, 1024], P(None, 'fsdp'), may hold values from -0.109375 to 0.109375
- ada_first: float32 [2, 768, 1024], P(None, 'fsdp'), may hold values from -0.00018310547 to 0.00018310547
- ada_second: float32 [2, 768, 1024], P(None, 'fsdp'), may hold values from 3.2885286e-09 to 1.3154114e-08
- qkv_weight: float32 [1024, 3072], P('fsdp'), may hold values from -0.1875 to 0.1875
- qkv_first: float32 [1024, 3072], P('fsdp'), may hold values from -0.00018310547 to 0.00018310547
- qkv_second: float32 [1024, 3072], P('fsdp'), may hold values from 3.2885286e-09 to 1.3154114e-08
- out_weight: float32 [1024, 1024], P('fsdp'), may hold values from -1.5 to 1.5
- out_first: float32 [1024, 1024], P('fsdp'), may hold values from -4.5776367e-05 to 4.5776367e-05
- out_second: float32 [1024, 1024], P('fsdp'), may hold values from 1.9731172e-10 to 7.892469e-10
- up_weight: float32 [1024, 6144], P('fsdp'), may hold values from -0.1875 to 0.1875
- up_first: float32 [1024, 6144], P('fsdp'), may hold values from -6.1035156e-05 to 6.1035156e-05
- up_second: float32 [1024, 6144], P('fsdp'), may hold values from 3.2885286e-10 to 1.3154114e-09
- down_weight: float32 [3072, 1024], P('fsdp'), may hold values from -0.109375 to 0.109375
- down_first: float32 [3072, 1024], P('fsdp'), may hold values from -0.00018310547 to 0.00018310547
- down_second: float32 [3072, 1024], P('fsdp'), may hold values from 3.2885286e-09 to 1.3154114e-08
- head_scale: float32 [16], replicated, may hold values from 5 to 20
- scale_first: float32 [16], replicated, may hold values from -0.00018310547 to 0.00018310547
- scale_second: float32 [16], replicated, may hold values from 3.2885286e-09 to 1.3154114e-08
Outputs:
- block_output: bfloat16 [32768, 1024], P(('dp', 'fsdp'))
- input_grad: bfloat16 [32768, 1024], P(('dp', 'fsdp'))
- grad_norm: float32 [], replicated
- new_ada: float32 [2, 768, 1024], P(None, 'fsdp')
- new_ada_first: float32 [2, 768, 1024], P(None, 'fsdp')
- new_ada_second: float32 [2, 768, 1024], P(None, 'fsdp')
- new_qkv: float32 [1024, 3072], P('fsdp')
- new_qkv_first: float32 [1024, 3072], P('fsdp')
- new_qkv_second: float32 [1024, 3072], P('fsdp')
- new_out: float32 [1024, 1024], P('fsdp')
- new_out_first: float32 [1024, 1024], P('fsdp')
- new_out_second: float32 [1024, 1024], P('fsdp')
- new_up: float32 [1024, 6144], P('fsdp')
- new_up_first: float32 [1024, 6144], P('fsdp')
- new_up_second: float32 [1024, 6144], P('fsdp')
- new_down: float32 [3072, 1024], P('fsdp')
- new_down_first: float32 [3072, 1024], P('fsdp')
- new_down_second: float32 [3072, 1024], P('fsdp')
- new_scale: float32 [16], replicated
- new_scale_first: float32 [16], replicated
- new_scale_second: float32 [16], replicated
The draws below stay inside these ranges and needn't reach their ends.
Inputs may be any that keep to these rules, and one draw needn't show every extreme that they name: `shapes`: each row is an image's bucket (height, width) with height = 256 // width, so that its valid tokens height * width never exceed 256; the first image is a full 16 x 16 bucket.
All inputs are finite; a program needn't handle non-finite values.
Results may differ from the reference program's by a relative error of at most 0.02.
Values may be sent and summed in bfloat16 or wider, within the bound.
No kernel may reach another device: no remote copies, remote signals or barrier semaphores. Data moves between devices by JAX's collectives and lax.ppermute only.
A program may use at most 256 MiB of HBM per device.

```python
import math
import jax
import jax.numpy as jnp
from jax import lax

D = 1024
H = 16
FF = 3072
COND = 768
SIDE = 16
STEP = 10
SEQ = 256
IMAGES = 128
TOKENS = 32768
PARAMS = 15204368


def draw_tokens(key, part):
    key = jax.random.fold_in(key, 11)
    rising = jnp.arange(D, dtype=jnp.float32) / (D - 1)
    base = jnp.clip(jax.random.normal(key, (TOKENS, D), jnp.float32), -6.0, 6.0)
    values = base * jnp.exp(rising * math.log(2.0))
    return values.astype(jnp.bfloat16)


def draw_shapes(key, part):
    key = jax.random.fold_in(key, 23)
    widths = jax.random.randint(key, (IMAGES,), SIDE // 2, 2 * SIDE + 1).astype(jnp.int32)
    widths = widths.at[0].set(SIDE)
    heights = SEQ // widths
    return jnp.stack([heights, widths], axis=1).astype(jnp.int32)


def steps_of(stream_key, shape, pieces, least, high):
    gain, own = 1.0, jax.random.fold_in(stream_key, 6)
    for axis_at, parts in pieces:
        steps = jnp.exp(jax.random.uniform(jax.random.fold_in(own, axis_at), (parts,), jnp.float32, least / len(pieces), high / len(pieces)))
        gain = gain * jnp.repeat(steps, shape[axis_at] // parts).reshape([-1 if axis == axis_at else 1 for axis in range(len(shape))])
    return gain


def scatter_about(own_key, dims, spread, limit, cuts=(), held_as=jnp.bfloat16):
    entries = jax.random.normal(own_key, dims, jnp.float32) * spread
    if len(cuts) > 0:
        entries = steps_of(own_key, dims, cuts, -0.22, 0.18) * entries
    return jnp.clip(entries, min=-limit, max=limit).astype(held_as)


def setup_inputs(seed: int = 0) -> dict:
    keys = jax.random.split(jax.random.key(seed), 23)
    tokens = draw_tokens(jax.random.fold_in(keys[22], 71), 0)
    condition = scatter_about(keys[1], (IMAGES, COND), 1.0, 6.0, ((0, 32),))
    shapes = draw_shapes(jax.random.fold_in(keys[22], 71), 0)
    cotangent = scatter_about(keys[3], (TOKENS, D), 1.0, 6.0, ((0, 32),))
    ada_weight = scatter_about(keys[4], (2, COND, D), (4 * COND) ** -0.5, 0.109375, ((1, 16),), jnp.float32)
    ada_first = scatter_about(keys[5], (2, COND, D), (0.11 * PARAMS ** -0.5), 0.00018310547, ((1, 16),), jnp.float32)
    ada_second = jnp.clip(jnp.exp(math.log(1.315411424229751e-08) - 1.3862944 * jax.random.uniform(keys[6], (2, COND, D), jnp.float32) ** steps_of(keys[6], (2, COND, D), ((1, 16),), -0.2, 0.2)), 3.2885285605743775e-09, 1.315411424229751e-08)
    qkv_weight = scatter_about(keys[7], (D, 3 * D), D ** -0.5, 0.1875, ((0, 16),), jnp.float32)
    qkv_first = scatter_about(keys[8], (D, 3 * D), (0.11 * PARAMS ** -0.5), 0.00018310547, ((0, 16),), jnp.float32)
    qkv_second = jnp.clip(jnp.exp(math.log(1.315411424229751e-08) - 1.3862944 * jax.random.uniform(keys[9], (D, 3 * D), jnp.float32) ** steps_of(keys[9], (D, 3 * D), ((0, 16),), -0.2, 0.2)), 3.2885285605743775e-09, 1.315411424229751e-08)
    out_weight = scatter_about(keys[10], (D, D), (4 * D // SEQ) ** -0.5, 1.5, ((0, 16),), jnp.float32)
    out_first = scatter_about(keys[11], (D, D), (0.03 * PARAMS ** -0.5), 4.57763671875e-05, ((0, 16),), jnp.float32)
    out_second = jnp.clip(jnp.exp(math.log(7.892468900649874e-10) - 1.3862944 * jax.random.uniform(keys[12], (D, D), jnp.float32) ** steps_of(keys[12], (D, D), ((0, 16),), -0.2, 0.2)), 1.9731172251624685e-10, 7.892468900649874e-10)
    up_weight = scatter_about(keys[13], (D, 2 * FF), D ** -0.5, 0.1875, ((0, 16),), jnp.float32)
    up_first = scatter_about(keys[14], (D, 2 * FF), (0.04 * PARAMS ** -0.5), 6.103515625e-05, ((0, 16),), jnp.float32)
    up_second = jnp.clip(jnp.exp(math.log(1.3154114464342115e-09) - 1.3862944 * jax.random.uniform(keys[15], (D, 2 * FF), jnp.float32) ** steps_of(keys[15], (D, 2 * FF), ((0, 16),), -0.2, 0.2)), 3.2885286160855287e-10, 1.3154114464342115e-09)
    down_weight = scatter_about(keys[16], (FF, D), FF ** -0.5, 0.109375, ((0, 16),), jnp.float32)
    down_first = scatter_about(keys[17], (FF, D), (0.11 * PARAMS ** -0.5), 0.00018310547, ((0, 16),), jnp.float32)
    down_second = jnp.clip(jnp.exp(math.log(1.315411424229751e-08) - 1.3862944 * jax.random.uniform(keys[18], (FF, D), jnp.float32) ** steps_of(keys[18], (FF, D), ((0, 16),), -0.2, 0.2)), 3.2885285605743775e-09, 1.315411424229751e-08)
    head_scale = jnp.clip(jnp.exp(jax.random.uniform(keys[19], (H,), jnp.float32, math.log(5.0), math.log(20.0))), 5.0, 20.0)
    scale_first = scatter_about(keys[20], (H,), (0.11 * PARAMS ** -0.5), 0.00018310547, (), jnp.float32)
    scale_second = jnp.clip(jnp.exp(jax.random.uniform(keys[21], (H,), jnp.float32, math.log(3.2885285605743775e-09), math.log(1.315411424229751e-08))), 3.2885285605743775e-09, 1.315411424229751e-08)
    return dict(tokens=tokens, condition=condition, shapes=shapes, cotangent=cotangent, ada_weight=ada_weight, ada_first=ada_first, ada_second=ada_second, qkv_weight=qkv_weight, qkv_first=qkv_first, qkv_second=qkv_second, out_weight=out_weight, out_first=out_first, out_second=out_second, up_weight=up_weight, up_first=up_first, up_second=up_second, down_weight=down_weight, down_first=down_first, down_second=down_second, head_scale=head_scale, scale_first=scale_first, scale_second=scale_second)


@jax.custom_vjp
def low(v):
    return lax.optimization_barrier(v.astype(jnp.bfloat16)).astype(jnp.float32)

@jax.custom_vjp
def low_back(v):
    return v

def low_keep(v):
    return (low(v), None)

def low_pass(kept, grad):
    return (grad,)

def back_keep(v):
    return (v, None)

def back_low(kept, grad):
    return (low(grad),)
low.defvjp(low_keep, low_pass)
low_back.defvjp(back_keep, back_low)
NORM_EPS = 1e-06
COSINE_EPS = 1e-06
MASK_FILL = -1e+30
ROPE_BASE = 100.0
CLIP = 1.0
RATE = 0.02
OUTPUT_RATE = 0.2
SCALE_RATE = 8.0
BETA_ONE = 0.9
BETA_TWO = 0.95
ADAM_EPS = 1e-08
DECAY = 0.01
PRECISE = lax.Precision.HIGHEST

def rope_tables(shapes, seq_len, head_dim):
    heights = shapes[:, 0:1]
    widths = shapes[:, 1:2]
    slot_index = jnp.arange(seq_len, dtype=jnp.int32)[None, :]
    row_index = slot_index // widths
    col_index = slot_index % widths
    valid_keys = slot_index < heights * widths
    freq_count = head_dim // 8
    frequency = ROPE_BASE ** (-jnp.arange(freq_count, dtype=jnp.float32) / freq_count)
    angles = jnp.concatenate([row_index.astype(jnp.float32)[..., None] * frequency, col_index.astype(jnp.float32)[..., None] * frequency], axis=-1)
    return (jnp.cos(angles), jnp.sin(angles), valid_keys)

def ada_norm(values, scales):
    inverse = lax.rsqrt(lax.optimization_barrier(jnp.mean(values * values, axis=-1, keepdims=True)) + NORM_EPS)
    return values * inverse * scales[:, None, :]

def turn(values, cosine, sine_table):
    quarter = values.shape[-1] // 4
    first_half = values[..., :quarter]
    second = values[..., quarter:2 * quarter]
    cos_wide = cosine[:, :, None, :]
    sin_wide = sine_table[:, :, None, :]
    return jnp.concatenate([first_half * cos_wide - second * sin_wide, first_half * sin_wide + second * cos_wide, values[..., 2 * quarter:]], axis=-1)

def prepare(queries, keys_in, head_scale, cosine, sine_table):
    root_scale = jnp.sqrt(head_scale)[None, None, :, None]
    queries = queries * root_scale * lax.rsqrt(lax.optimization_barrier(jnp.sum(queries * queries, axis=-1, keepdims=True)) + COSINE_EPS)
    keys_in = keys_in * root_scale * lax.rsqrt(lax.optimization_barrier(jnp.sum(keys_in * keys_in, axis=-1, keepdims=True)) + COSINE_EPS)
    return (turn(queries, cosine, sine_table), turn(keys_in, cosine, sine_table))

def group_forward(inputs, condition, shapes, low_weights, head_scale):
    ada_low, qkv_low, out_low, up_low, down_low = low_weights
    image_count, seq_len, model_width = inputs.shape
    head_count = head_scale.shape[0]
    head_dim = model_width // head_count
    hidden_units = down_low.shape[0]
    cosine, sine_table, valid_keys = rope_tables(shapes, seq_len, head_dim)
    scale_one = 1.0 + jnp.dot(condition, ada_low[0], precision=PRECISE)
    act_one = low(ada_norm(inputs, scale_one))
    projected = low_back(jnp.einsum('bsd,de->bse', act_one, qkv_low, precision=PRECISE))
    projected = projected.reshape(image_count, seq_len, 3, head_count, head_dim)
    turned_q, turned_k = prepare(projected[:, :, 0], projected[:, :, 1], head_scale, cosine, sine_table)
    q_low = low(turned_q)
    k_low = low(turned_k)
    v_low = low(projected[:, :, 2])
    scores = low_back(jnp.einsum('bqhd,bkhd->bhqk', q_low, k_low, precision=PRECISE))
    scores = jnp.where(valid_keys[:, None, None, :], scores, MASK_FILL)
    top_score = lax.optimization_barrier(jnp.max(scores, axis=-1, keepdims=True))
    exponent = jnp.exp(scores - top_score)
    probabilities = low(exponent / lax.optimization_barrier(jnp.sum(exponent, axis=-1, keepdims=True)))
    mixed_out = jnp.einsum('bhqk,bkhd->bqhd', probabilities, v_low, precision=PRECISE)
    mixed_out = low(low_back(mixed_out.reshape(image_count, seq_len, model_width)))
    middle = inputs + low_back(jnp.einsum('bse,ed->bsd', mixed_out, out_low, precision=PRECISE))
    scale_two = 1.0 + jnp.dot(condition, ada_low[1], precision=PRECISE)
    act_two = low(ada_norm(middle, scale_two))
    gate_up = low_back(jnp.einsum('bsd,de->bse', act_two, up_low, precision=PRECISE))
    hidden_act = jax.nn.gelu(gate_up[..., :hidden_units], approximate=False) * gate_up[..., hidden_units:]
    hidden_act = low(low_back(hidden_act))
    return middle + low_back(jnp.einsum('bsf,fd->bsd', hidden_act, down_low, precision=PRECISE))

def adamw(weight, first_moment, second_moment, gradient, factor, rate, decay):
    clipped = gradient * factor
    new_first = BETA_ONE * first_moment + (1.0 - BETA_ONE) * clipped
    new_second = BETA_TWO * second_moment + (1.0 - BETA_TWO) * clipped * clipped
    denominator = jnp.sqrt(new_second / (1.0 - BETA_TWO ** STEP)) + ADAM_EPS
    new_weight = weight * (1.0 - rate * decay) - rate * (new_first / (1.0 - BETA_ONE ** STEP)) / denominator
    return (new_weight, new_first, new_second)

def reference(tokens, condition, shapes, cotangent, ada_weight, ada_first, ada_second, qkv_weight, qkv_first, qkv_second, out_weight, out_first, out_second, up_weight, up_first, up_second, down_weight, down_first, down_second, head_scale, scale_first, scale_second):
    image_total = shapes.shape[0]
    group_size = math.gcd(image_total, max(1, 4096 // SEQ))
    group_count = image_total // group_size
    cond_groups = condition.astype(jnp.float32).reshape(group_count, group_size, COND)
    shape_groups = shapes.reshape(group_count, group_size, 2)

    def forward(inputs, ada_w, qkv_w, out_w, up_w, down_w, scale_w):
        low_weights = (low(ada_w), low(qkv_w), low(out_w), low(up_w), low(down_w))

        def one_group(group_parts):
            return group_forward(group_parts[0], group_parts[1], group_parts[2], low_weights, scale_w)
        outputs = lax.map(jax.checkpoint(one_group), (inputs.reshape(group_count, group_size, SEQ, D), cond_groups, shape_groups))
        return outputs.reshape(image_total * SEQ, D)
    result, pullback = jax.vjp(forward, tokens.astype(jnp.float32), ada_weight, qkv_weight, out_weight, up_weight, down_weight, head_scale)
    grads = pullback(cotangent.astype(jnp.float32))
    total = jnp.sum(grads[1] * grads[1]) + jnp.sum(grads[2] * grads[2]) + jnp.sum(grads[3] * grads[3])
    total = total + jnp.sum(grads[4] * grads[4]) + jnp.sum(grads[5] * grads[5]) + jnp.sum(grads[6] * grads[6])
    grad_norm = jnp.sqrt(total)
    factor = jnp.minimum(1.0, CLIP / (grad_norm + 1e-06))
    ada_new = adamw(ada_weight, ada_first, ada_second, grads[1], factor, RATE, DECAY)
    qkv_new = adamw(qkv_weight, qkv_first, qkv_second, grads[2], factor, RATE, DECAY)
    out_new = adamw(out_weight, out_first, out_second, grads[3], factor, OUTPUT_RATE, DECAY)
    up_new = adamw(up_weight, up_first, up_second, grads[4], factor, RATE, DECAY)
    down_new = adamw(down_weight, down_first, down_second, grads[5], factor, RATE, DECAY)
    scale_new = adamw(head_scale, scale_first, scale_second, grads[6], factor, SCALE_RATE, 0.0)
    return (result.astype(jnp.bfloat16), grads[0].astype(jnp.bfloat16), grad_norm, ada_new[0], ada_new[1], ada_new[2], qkv_new[0], qkv_new[1], qkv_new[2], out_new[0], out_new[1], out_new[2], up_new[0], up_new[1], up_new[2], down_new[0], down_new[1], down_new[2], scale_new[0], scale_new[1], scale_new[2])
```

```python
import functools
import math

import jax
import jax.numpy as jnp
import numpy as np
from jax import lax
from jax.experimental import pallas as pl
from jax.experimental.pallas import tpu as pltpu
from jax.sharding import PartitionSpec as P

FF = 3072
STEP = 10


NORM_EPS = 1e-06
COSINE_EPS = 1e-06
ROPE_BASE = 100.0
CLIP = 1.0
RATE = 0.02
OUTPUT_RATE = 0.2
SCALE_RATE = 8.0
BETA_ONE = 0.9
BETA_TWO = 0.95
ADAM_EPS = 1e-08
DECAY = 0.01
PRECISE = lax.Precision.HIGHEST
AXES = ("dp", "fsdp")
LOW = jnp.bfloat16
WIDE = jnp.float32


class Net:
    def __init__(self, size, dp_size):
        self.size = size
        self.dp_size = dp_size
        self.sub = size // 16
        self.core = lax.axis_index("dp")
        self.me = lax.axis_index("fsdp") // self.sub
        self.gather_order = ((8, 4, 1, 2), (8, 4, 2, 1))
        self.scatter_order = ((1, 2, 4, 8), (2, 1, 4, 8))

    def exchange(self, array, bits):
        pairs = []
        for core in range(self.dp_size):
            for place in range(self.size):
                target = place ^ (bits[core % 2] * self.sub)
                pairs.append((core * self.size + place, core * self.size + target))
        return lax.ppermute(array, AXES, pairs)

    def swap(self, array):
        pairs = []
        for core in range(self.dp_size):
            for place in range(self.size):
                pairs.append((core * self.size + place, (core ^ 1) * self.size + place))
        return lax.ppermute(array, AXES, pairs)

    def origins(self, order, sibling=False):
        tables = []
        for core in range(2):
            bits = order[core ^ 1] if sibling else order[core]
            table = []
            for index in range(16):
                value = 0
                for stage in range(4):
                    if index >> stage & 1:
                        value ^= bits[stage]
                table.append(value)
            tables.append(table)
        table = jnp.asarray(tables, jnp.int32)[self.core]
        return table ^ self.me

    def join_sub(self, shard):
        if self.sub == 1:
            return shard
        groups = [list(range(g * self.sub, (g + 1) * self.sub)) for g in range(16)]
        return lax.all_gather(shard, "fsdp", axis=0, tiled=True, axis_index_groups=groups)

    def gather(self, half):
        low, high = self.gather_order
        held = half[None]
        for stage in range(3):
            other = self.exchange(held, (low[stage], high[stage]))
            held = jnp.concatenate([held, other], axis=0)
        far = self.exchange(held, (low[3], high[3]))
        return held, far, self.swap(held), self.swap(far)

    def scatter(self, held):
        low, high = self.scatter_order
        for stage in range(4):
            count = held.shape[0] // 2
            other = self.exchange(held[count:], (low[stage], high[stage]))
            held = (held[:count].astype(WIDE) + other.astype(WIDE)).astype(LOW)
        return held[0]

    def table(self, order):
        return jnp.concatenate(
            [self.origins(order), self.origins(order, True), self.core[None]]
        ).astype(jnp.int32)

    def split_sub(self, gradient):
        if self.sub == 1:
            return gradient
        groups = [list(range(g * self.sub, (g + 1) * self.sub)) for g in range(16)]
        gathered = lax.all_gather(gradient, "fsdp", axis=0, axis_index_groups=groups)
        rows = gradient.shape[0] // self.sub
        place = lax.axis_index("fsdp") % self.sub
        return lax.dynamic_slice_in_dim(jnp.sum(gathered, axis=0), place * rows, rows, axis=0)

    def gather_small(self, rows):
        if self.sub > 1:
            return lax.all_gather(rows, AXES, axis=0, tiled=True)
        for bit in (8, 4, 2, 1):
            rows = jnp.concatenate([rows, self.exchange(rows, (bit, bit))], axis=0)
        return jnp.concatenate([rows, self.swap(rows)], axis=0)

    def total(self, value):
        if self.sub > 1:
            return lax.psum(value, "fsdp")
        value = jnp.broadcast_to(value, (1, 128))
        for bit in (1, 2, 4, 8):
            value = value + self.exchange(value, (bit, bit))
        return value[0, 0]


def half_rows(shard, core):
    rows = shard.shape[0] // 2
    return lax.dynamic_slice_in_dim(shard, core * rows, rows, axis=0).astype(LOW)


def owner_start(table_ref, index, rows, side):
    return pl.multiple_of(table_ref[index] * (2 * rows) + side * rows, 16)


def load_weight(table_ref, pieces, full_ref, sems):
    core = table_ref[32]
    rows = pieces[0].shape[1]
    copies = []
    for number, piece in enumerate(pieces):
        side = core if number < 2 else 1 - core
        for index in range(8):
            start = owner_start(table_ref, number * 8 + index, rows, side)
            copies.append(
                pltpu.make_async_copy(
                    piece.at[index], full_ref.at[pl.ds(start, rows)], sems.at[number, index]
                )
            )
    return copies


def fetch(copies):
    for copy in copies:
        copy.start()
    for copy in copies:
        copy.wait()


ANY = pl.BlockSpec(memory_space=pl.ANY)
SMEM = pl.BlockSpec(memory_space=pltpu.SMEM)
NT = (((1,), (1,)), ((), ()))
VMEM_LIMIT = 56 * 1024 * 1024


def params(dims):
    return pltpu.CompilerParams(
        dimension_semantics=("arbitrary",) * dims, vmem_limit_bytes=VMEM_LIMIT
    )


def mul(a, b):
    return jnp.dot(a, b, preferred_element_type=WIDE)


def mul_nt(a, b):
    return lax.dot_general(a, b, NT, preferred_element_type=WIDE)


def whole(shape):
    return pl.BlockSpec(shape, lambda *_: (0,) * len(shape))


def rotate(values, cos_rep, up_rep, down_rep, sign):
    ahead = pltpu.roll(values, values.shape[-1] - 16, 1)
    behind = pltpu.roll(values, 16, 1)
    turned = ahead * up_rep + behind * down_rep
    return values * cos_rep + (turned if sign > 0 else -turned)


def front_kernel(
    table_ref, x_ref, scale_ref, p0, p1, p2, p3, sums_ref, spread_ref, root_ref,
    cos_ref, up_ref, down_ref, act_ref, q_ref, k_ref, v_ref, pack_ref, w_ref, sems,
):
    @pl.when(pl.program_id(0) == 0)
    def _():
        fetch(load_weight(table_ref, (p0, p1, p2, p3), w_ref, sems))

    width = x_ref.shape[1]
    x = x_ref[...].astype(WIDE)
    inverse = lax.rsqrt(jnp.mean(x * x, axis=-1, keepdims=True) + NORM_EPS)
    act = (x * inverse * scale_ref[0]).astype(LOW)
    act_ref[...] = act
    v_ref[...] = mul(act, w_ref[:, 2 * width :]).astype(LOW)
    q = mul(act, w_ref[:, :width])
    k = mul(act, w_ref[:, width : 2 * width])
    sums = mul((q * q).astype(LOW), sums_ref[0]) + mul((k * k).astype(LOW), sums_ref[1])
    factor = lax.rsqrt(sums + COSINE_EPS)
    high = factor.astype(LOW)
    low = (factor - high.astype(WIDE)).astype(LOW)
    lane = lax.broadcasted_iota(jnp.int32, factor.shape, 1)
    pack = jnp.where(lane < 32, high.astype(WIDE), jnp.where(lane < 64, low.astype(WIDE), 0.0))
    pack = pack.astype(LOW)
    pack_ref[...] = pack
    q = q * mul(pack, spread_ref[0]) * root_ref[...]
    k = k * mul(pack, spread_ref[1]) * root_ref[...]
    cos_rep, up_rep, down_rep = cos_ref[...], up_ref[...], down_ref[...]
    for pair in range(width // 128):
        lanes = slice(pair * 128, pair * 128 + 128)
        q_ref[:, lanes] = rotate(q[:, lanes], cos_rep, up_rep, down_rep, 1).astype(LOW)
        k_ref[:, lanes] = rotate(k[:, lanes], cos_rep, up_rep, down_rep, 1).astype(LOW)


def front(table, x, scale, pieces, sums, spread, root, turns, images):
    tokens, width = x.shape
    seq = tokens // images
    row = pl.BlockSpec((seq, width), lambda i: (i, 0))
    narrow = pl.BlockSpec((seq, 128), lambda i: (i, 0))
    full = jax.ShapeDtypeStruct((tokens, width), LOW)
    return pl.pallas_call(
        front_kernel,
        grid=(images,),
        in_specs=[SMEM, row, pl.BlockSpec((1, 1, width), lambda i: (i, 0, 0)), ANY, ANY, ANY, ANY,
                  whole(sums.shape), whole(spread.shape), whole(root.shape), narrow, narrow, narrow],
        out_specs=[row, row, row, row, narrow],
        out_shape=[full, full, full, full, jax.ShapeDtypeStruct((tokens, 128), LOW)],
        scratch_shapes=[pltpu.VMEM((width, 3 * width), LOW), pltpu.SemaphoreType.DMA((4, 8))],
        compiler_params=params(1),
        cost_estimate=pl.CostEstimate(flops=6 * tokens * width * width, bytes_accessed=20 << 20, transcendentals=0),
        name="front",
    )(table, x, scale, *pieces, sums, spread, root, *turns)


def attend_kernel(q_ref, k_ref, v_ref, valid_ref, o_ref, lse_ref):
    seq, width = q_ref.shape
    valid = valid_ref[...]
    lane = lax.broadcasted_iota(jnp.int32, (seq, 128), 1)
    first = lane < 64
    totals = jnp.zeros((seq, 128), WIDE)
    zero = jnp.zeros((seq, 128), LOW)
    for pair in range(width // 128):
        lanes = slice(pair * 128, pair * 128 + 128)
        q, k = q_ref[:, lanes], k_ref[:, lanes]
        v = v_ref[:, lanes] * valid
        mixed = None
        for half in range(2):
            pick = first if half == 0 else jnp.logical_not(first)
            scores = mul_nt(jnp.where(pick, q, zero), k)
            weights = jnp.exp(scores).astype(LOW)
            right = jnp.concatenate([jnp.where(pick, v, zero), valid], axis=1)
            both = mul(weights, right)
            total = both[:, 128:]
            part = both[:, :128] / total
            mixed = part if mixed is None else mixed + part
            totals = jnp.where(lane == 2 * pair + half, total, totals)
        o_ref[:, lanes] = mixed.astype(LOW)
    lane_ok = lane < width // 64
    lse = jnp.log(jnp.where(lane_ok, totals, 1.0))
    lse_ref[0] = lse.T[: width // 64]


def attend(q, k, v, valid, images):
    tokens, width = q.shape
    seq = tokens // images
    row = pl.BlockSpec((seq, width), lambda i: (i, 0))
    heads = width // 64
    return pl.pallas_call(
        attend_kernel,
        grid=(images,),
        in_specs=[row, row, row, pl.BlockSpec((seq, 128), lambda i: (i, 0))],
        out_specs=[row, pl.BlockSpec((1, heads, seq), lambda i: (i, 0, 0))],
        out_shape=[jax.ShapeDtypeStruct((tokens, width), LOW),
                   jax.ShapeDtypeStruct((images, heads, seq), WIDE)],
        compiler_params=params(1),
        cost_estimate=pl.CostEstimate(flops=16 * tokens * seq * width, bytes_accessed=8 << 20, transcendentals=0),
        name="attend",
    )(q, k, v, valid)


def middle_kernel(table_ref, o_ref, x_ref, scale_ref, p0, p1, p2, p3, mid_ref, act_ref, w_ref, sems):
    @pl.when(pl.program_id(0) == 0)
    def _():
        fetch(load_weight(table_ref, (p0, p1, p2, p3), w_ref, sems))

    mid = x_ref[...].astype(WIDE) + mul(o_ref[...], w_ref[...])
    mid_ref[...] = mid
    inverse = lax.rsqrt(jnp.mean(mid * mid, axis=-1, keepdims=True) + NORM_EPS)
    act_ref[...] = (mid * inverse * scale_ref[0]).astype(LOW)


def middle_block(table, o, x, scale, pieces, images):
    tokens, width = x.shape
    seq = tokens // images
    row = pl.BlockSpec((seq, width), lambda i: (i, 0))
    return pl.pallas_call(
        middle_kernel,
        grid=(images,),
        in_specs=[SMEM, row, row, pl.BlockSpec((1, 1, width), lambda i: (i, 0, 0)), ANY, ANY, ANY, ANY],
        out_specs=[row, row],
        out_shape=[jax.ShapeDtypeStruct((tokens, width), WIDE), jax.ShapeDtypeStruct((tokens, width), LOW)],
        scratch_shapes=[pltpu.VMEM((width, width), LOW), pltpu.SemaphoreType.DMA((4, 8))],
        compiler_params=params(1),
        cost_estimate=pl.CostEstimate(flops=2 * tokens * width * width, bytes_accessed=12 << 20, transcendentals=0),
        name="middle",
    )(table, o, x, scale, *pieces)


def gate_kernel(table_ref, act_ref, dy_ref, u0, u1, u2, u3, d0, d1, d2, d3,
                hid_ref, dgu_ref, up_ref, down_ref, sems, sems_down):
    step = pl.program_id(1)

    @pl.when((pl.program_id(0) == 0) & (step == 0))
    def _():
        fetch(
            load_weight(table_ref, (u0, u1, u2, u3), up_ref, sems)
            + load_weight(table_ref, (d0, d1, d2, d3), down_ref, sems_down)
        )

    hidden = hid_ref.shape[1]
    size = 512
    at = pl.multiple_of(step * size, size)
    above = pl.multiple_of(hidden + step * size, size)
    act = act_ref[...]
    gate = mul(act, up_ref[:, pl.ds(at, size)])
    upper = mul(act, up_ref[:, pl.ds(above, size)])
    grad = mul_nt(dy_ref[...], down_ref[pl.ds(at, size), :]).astype(LOW).astype(WIDE)
    cdf = 0.5 * (1.0 + lax.erf(gate * math.sqrt(0.5)))
    bell = jnp.exp(-0.5 * gate * gate) * (1.0 / math.sqrt(2.0 * math.pi))
    gelu = gate * cdf
    hid_ref[:, pl.ds(at, size)] = (gelu * upper).astype(LOW)
    dgu_ref[:, pl.ds(at, size)] = (grad * upper * (cdf + gate * bell)).astype(LOW)
    dgu_ref[:, pl.ds(above, size)] = (grad * gelu).astype(LOW)


def gate_block(table, act, dy, up_pieces, down_pieces, images):
    tokens, width = act.shape
    seq = tokens // images
    hidden = 32 * down_pieces[0].shape[1]
    row = pl.BlockSpec((seq, width), lambda i, j: (i, 0))
    return pl.pallas_call(
        gate_kernel,
        grid=(images, hidden // 512),
        in_specs=[SMEM, row, row] + [ANY] * 8,
        out_specs=[pl.BlockSpec((seq, hidden), lambda i, j: (i, 0)),
                   pl.BlockSpec((seq, 2 * hidden), lambda i, j: (i, 0))],
        out_shape=[jax.ShapeDtypeStruct((tokens, hidden), LOW),
                   jax.ShapeDtypeStruct((tokens, 2 * hidden), LOW)],
        scratch_shapes=[pltpu.VMEM((width, 2 * hidden), LOW), pltpu.VMEM((hidden, width), LOW),
                        pltpu.SemaphoreType.DMA((4, 8)), pltpu.SemaphoreType.DMA((4, 8))],
        compiler_params=params(2),
        cost_estimate=pl.CostEstimate(flops=6 * tokens * width * hidden, bytes_accessed=40 << 20, transcendentals=0),
        name="geglu",
    )(table, act, dy, *up_pieces, *down_pieces)


def branch_kernel(table_ref, dgu_ref, dy_ref, mid_ref, scale_ref, u0, u1, u2, u3, o0, o1, o2, o3,
                  dmid_ref, db_ref, do_ref, dscale_ref, up_ref, out_ref, acc_ref, sems, sems_out):
    step = pl.program_id(1)

    @pl.when((pl.program_id(0) == 0) & (step == 0))
    def _():
        fetch(
            load_weight(table_ref, (u0, u1, u2, u3), up_ref, sems)
            + load_weight(table_ref, (o0, o1, o2, o3), out_ref, sems_out)
        )

    size = dgu_ref.shape[1]
    at = pl.multiple_of(step * size, size)
    part = mul_nt(dgu_ref[...], up_ref[:, pl.ds(at, size)])

    @pl.when(step == 0)
    def _():
        acc_ref[...] = part

    @pl.when(step > 0)
    def _():
        acc_ref[...] += part

    @pl.when(step == pl.num_programs(1) - 1)
    def _():
        grad = acc_ref[...]
        mid = mid_ref[...]
        inverse = lax.rsqrt(jnp.mean(mid * mid, axis=-1, keepdims=True) + NORM_EPS)
        normed = mid * inverse
        dscale_ref[0] = jnp.sum(grad * normed, axis=0, keepdims=True)
        grad = grad * scale_ref[0]
        inner = jnp.mean(grad * normed, axis=-1, keepdims=True)
        dmid = dy_ref[...].astype(WIDE) + inverse * (grad - normed * inner)
        dmid_ref[...] = dmid
        low = dmid.astype(LOW)
        db_ref[...] = low
        do_ref[...] = mul_nt(low, out_ref[...]).astype(LOW)


def branch_block(table, dgu, dy, mid, scale, up_pieces, out_pieces, images):
    tokens, width = dy.shape
    seq = tokens // images
    wide = dgu.shape[1]
    size = 1024
    row = pl.BlockSpec((seq, width), lambda i, j: (i, 0))
    one = pl.BlockSpec((1, 1, width), lambda i, j: (i, 0, 0))
    return pl.pallas_call(
        branch_kernel,
        grid=(images, wide // size),
        in_specs=[SMEM, pl.BlockSpec((seq, size), lambda i, j: (i, j)), row, row, one] + [ANY] * 8,
        out_specs=[row, row, row, one],
        out_shape=[jax.ShapeDtypeStruct((tokens, width), WIDE), jax.ShapeDtypeStruct((tokens, width), LOW),
                   jax.ShapeDtypeStruct((tokens, width), LOW), jax.ShapeDtypeStruct((images, 1, width), WIDE)],
        scratch_shapes=[pltpu.VMEM((width, wide), LOW), pltpu.VMEM((width, width), LOW),
                        pltpu.VMEM((seq, width), WIDE),
                        pltpu.SemaphoreType.DMA((4, 8)), pltpu.SemaphoreType.DMA((4, 8))],
        compiler_params=params(2),
        cost_estimate=pl.CostEstimate(flops=2 * tokens * width * (wide + width), bytes_accessed=40 << 20, transcendentals=0),
        name="branch",
    )(table, dgu, dy, mid, scale, *up_pieces, *out_pieces)


def attend_back_kernel(q_ref, k_ref, v_ref, o_ref, do_ref, lse_ref, valid_ref, pack_ref, spread_ref,
                       root_ref, pick_ref, block_ref, cos_ref, up_ref, down_ref, dproj_ref, dhead_ref):
    seq, width = q_ref.shape
    valid = valid_ref[...]
    valid_wide = valid.astype(WIDE)
    first = lax.broadcasted_iota(jnp.int32, (seq, 128), 1) < 64
    zero = jnp.zeros((seq, 128), LOW)
    cos_rep, up_rep, down_rep = cos_ref[...], up_ref[...], down_ref[...]
    product = (do_ref[...].astype(WIDE) * o_ref[...].astype(WIDE)).astype(LOW)
    delta = mul_nt(pick_ref[...], product)
    pack = pack_ref[...]
    block = block_ref[...]
    for pair in range(width // 128):
        lanes = slice(pair * 128, pair * 128 + 128)
        q, k, v, do = q_ref[:, lanes], k_ref[:, lanes], v_ref[:, lanes], do_ref[:, lanes]
        k_turned = (k * valid).T
        dv = dk = None
        dq_parts = []
        for half in range(2):
            head = 2 * pair + half
            pick = first if half == 0 else jnp.logical_not(first)
            q_one = jnp.where(pick, q, zero)
            do_one = jnp.where(pick, do, zero)
            weights = jnp.exp(mul_nt(k, q_one) - lse_ref[0, head : head + 1, :])
            grads = mul_nt(v, do_one)
            dscore = (weights * (grads - delta[head : head + 1, :])).astype(LOW)
            part_v = mul(weights.astype(LOW), do_one)
            part_k = mul(dscore, q_one)
            dv = part_v if dv is None else dv + part_v
            dk = part_k if dk is None else dk + part_k
            dq_parts.append(mul(k_turned[half * 64 : half * 64 + 64], dscore))
        dq = jnp.concatenate(dq_parts, axis=0).T
        dk = dk * valid_wide
        root = root_ref[:, lanes]
        for side, (grad, value) in enumerate(((dq, q), (dk, k))):
            value = value.astype(WIDE)
            inner = mul((grad * value).astype(LOW), block)
            total = jnp.sum(inner, axis=0, keepdims=True)
            if side == 0:
                head_total = total
            else:
                dhead_ref[0, :, lanes] = head_total + total
            factor = mul(pack, spread_ref[side, :, lanes])
            back = factor * (root * grad - value * (inner / root))
            back = rotate(back, cos_rep, up_rep, down_rep, -1)
            dproj_ref[:, side * width + pair * 128 : side * width + pair * 128 + 128] = back.astype(LOW)
        dproj_ref[:, 2 * width + pair * 128 : 2 * width + pair * 128 + 128] = (dv * valid_wide).astype(LOW)


def attend_back(q, k, v, o, do, lse, valid, pack, spread, root, pick, block, turns, images):
    tokens, width = q.shape
    seq = tokens // images
    heads = width // 64
    row = pl.BlockSpec((seq, width), lambda i: (i, 0))
    narrow = pl.BlockSpec((seq, 128), lambda i: (i, 0))
    return pl.pallas_call(
        attend_back_kernel,
        grid=(images,),
        in_specs=[row, row, row, row, row, pl.BlockSpec((1, heads, seq), lambda i: (i, 0, 0)), narrow, narrow,
                  whole(spread.shape), whole(root.shape), whole(pick.shape), whole(block.shape),
                  narrow, narrow, narrow],
        out_specs=[pl.BlockSpec((seq, 3 * width), lambda i: (i, 0)),
                   pl.BlockSpec((1, 1, width), lambda i: (i, 0, 0))],
        out_shape=[jax.ShapeDtypeStruct((tokens, 3 * width), LOW),
                   jax.ShapeDtypeStruct((images, 1, width), WIDE)],
        compiler_params=params(1),
        cost_estimate=pl.CostEstimate(flops=40 * tokens * seq * width, bytes_accessed=20 << 20, transcendentals=0),
        name="attend_back",
    )(q, k, v, o, do, lse, valid, pack, spread, root, pick, block, *turns)


def input_kernel(table_ref, dproj_ref, x_ref, dmid_ref, scale_ref, p0, p1, p2, p3,
                 out_ref, dscale_ref, w_ref, sems):
    @pl.when(pl.program_id(0) == 0)
    def _():
        fetch(load_weight(table_ref, (p0, p1, p2, p3), w_ref, sems))

    width = x_ref.shape[1]
    grad = mul_nt(dproj_ref[:, :width], w_ref[:, :width])
    grad += mul_nt(dproj_ref[:, width : 2 * width], w_ref[:, width : 2 * width])
    grad += mul_nt(dproj_ref[:, 2 * width :], w_ref[:, 2 * width :])
    x = x_ref[...].astype(WIDE)
    inverse = lax.rsqrt(jnp.mean(x * x, axis=-1, keepdims=True) + NORM_EPS)
    normed = x * inverse
    dscale_ref[0] = jnp.sum(grad * normed, axis=0, keepdims=True)
    grad = grad * scale_ref[0]
    inner = jnp.mean(grad * normed, axis=-1, keepdims=True)
    out_ref[...] = (dmid_ref[...] + inverse * (grad - normed * inner)).astype(LOW)


def input_block(table, dproj, x, dmid, scale, pieces, images):
    tokens, width = x.shape
    seq = tokens // images
    row = pl.BlockSpec((seq, width), lambda i: (i, 0))
    one = pl.BlockSpec((1, 1, width), lambda i: (i, 0, 0))
    return pl.pallas_call(
        input_kernel,
        grid=(images,),
        in_specs=[SMEM, pl.BlockSpec((seq, 3 * width), lambda i: (i, 0)), row, row, one] + [ANY] * 4,
        out_specs=[row, one],
        out_shape=[jax.ShapeDtypeStruct((tokens, width), LOW), jax.ShapeDtypeStruct((images, 1, width), WIDE)],
        scratch_shapes=[pltpu.VMEM((width, 3 * width), LOW), pltpu.SemaphoreType.DMA((4, 8))],
        compiler_params=params(1),
        cost_estimate=pl.CostEstimate(flops=6 * tokens * width * width, bytes_accessed=24 << 20, transcendentals=0),
        name="input_grad",
    )(table, dproj, x, dmid, scale, *pieces)


def result_kernel(table_ref, hid_ref, mid_ref, p0, p1, p2, p3, out_ref, w_ref, sems):
    @pl.when(pl.program_id(0) == 0)
    def _():
        fetch(load_weight(table_ref, (p0, p1, p2, p3), w_ref, sems))

    out_ref[...] = (mid_ref[...] + mul(hid_ref[...], w_ref[...])).astype(LOW)


def result_block(table, hid, mid, pieces, images):
    tokens, width = mid.shape
    seq = tokens // images
    hidden = hid.shape[1]
    row = pl.BlockSpec((seq, width), lambda i: (i, 0))
    return pl.pallas_call(
        result_kernel,
        grid=(images,),
        in_specs=[SMEM, pl.BlockSpec((seq, hidden), lambda i: (i, 0)), row] + [ANY] * 4,
        out_specs=row,
        out_shape=jax.ShapeDtypeStruct((tokens, width), LOW),
        scratch_shapes=[pltpu.VMEM((hidden, width), LOW), pltpu.SemaphoreType.DMA((4, 8))],
        compiler_params=params(1),
        cost_estimate=pl.CostEstimate(flops=2 * tokens * width * hidden, bytes_accessed=20 << 20, transcendentals=0),
        name="result",
    )(table, hid, mid, *pieces)


def weight_kernel(side, add, table_ref, act_ref, grad_ref, *rest):
    if add:
        other_ref, out_ref, turned_ref, left_ref = rest
    else:
        out_ref, turned_ref, left_ref = rest
    rows = left_ref.shape[0] // 16

    @pl.when(pl.program_id(0) == 0)
    def _():
        for start in range(0, act_ref.shape[1], 256):
            turned_ref[start : start + 256, :] = act_ref[:, start : start + 256].T
        core = table_ref[32]
        for index in range(16):
            start = owner_start(table_ref, side * 16 + index, rows, core if side == 0 else 1 - core)
            left_ref[index * rows : index * rows + rows, :] = turned_ref[pl.ds(start, rows), :]

    total = mul(left_ref[...], grad_ref[...])
    if add:
        total = total + other_ref[...].astype(WIDE)
    out_ref[...] = total.astype(LOW)


def weight_half(table, act, grad, side, other=None):
    tokens, depth = act.shape
    columns = grad.shape[1]
    size = 256
    half = depth // 2
    tile = pl.BlockSpec((half, size), lambda j: (0, j))
    extra = () if other is None else (other,)
    return pl.pallas_call(
        functools.partial(weight_kernel, side, other is not None),
        grid=(columns // size,),
        in_specs=[SMEM, whole(act.shape), pl.BlockSpec((tokens, size), lambda j: (0, j))] + [tile] * len(extra),
        out_specs=tile,
        out_shape=jax.ShapeDtypeStruct((half, columns), LOW),
        scratch_shapes=[pltpu.VMEM((depth, tokens), LOW), pltpu.VMEM((half, tokens), LOW)],
        compiler_params=params(1),
        cost_estimate=pl.CostEstimate(flops=tokens * depth * columns, bytes_accessed=(tokens * (depth + columns) + half * columns) * 2, transcendentals=0),
        name="weight_grad",
    )(table, act, grad, *extra)


def rope_tables(shapes, seq_len, head_dim):
    heights = shapes[:, 0:1]
    widths = shapes[:, 1:2]
    slot_index = jnp.arange(seq_len, dtype=jnp.int32)[None, :]
    row_index = slot_index // widths
    col_index = slot_index % widths
    valid_keys = slot_index < heights * widths
    freq_count = head_dim // 8
    frequency = ROPE_BASE ** (-jnp.arange(freq_count, dtype=jnp.float32) / freq_count)
    angles = jnp.concatenate(
        [
            row_index.astype(jnp.float32)[..., None] * frequency,
            col_index.astype(jnp.float32)[..., None] * frequency,
        ],
        axis=-1,
    )
    return (jnp.cos(angles), jnp.sin(angles), valid_keys)


def turn_tables(shapes, seq_len, head_dim):
    cosine, sine, valid = rope_tables(shapes, seq_len, head_dim)
    tokens = cosine.shape[0] * seq_len
    cosine = cosine.reshape(tokens, -1)
    sine = sine.reshape(tokens, -1)
    ones = jnp.ones((tokens, head_dim // 2), WIDE)
    none = jnp.zeros_like(sine)
    blank = jnp.zeros((tokens, head_dim // 2), WIDE)
    cos_rep = jnp.concatenate([cosine, cosine, ones] * 2, axis=1)
    up_rep = jnp.concatenate([-sine, none, blank] * 2, axis=1)
    down_rep = jnp.concatenate([none, sine, blank] * 2, axis=1)
    valid = jnp.broadcast_to(valid.reshape(tokens, 1), (tokens, 128)).astype(LOW)
    return (cos_rep, up_rep, down_rep), valid


def head_matrices(width, head_dim):
    heads = width // head_dim
    owner = np.arange(width) // head_dim
    sums = np.zeros((2, width, 128), np.float32)
    spread = np.zeros((2, 128, width), np.float32)
    for side in range(2):
        for copy in range(2):
            sums[side, np.arange(width), side * heads + copy * 2 * heads + owner] = 1.0
            spread[side, side * heads + copy * 2 * heads + owner, np.arange(width)] = 1.0
    pick = np.zeros((heads, width), np.float32)
    pick[owner, np.arange(width)] = 1.0
    block = np.kron(np.eye(128 // head_dim), np.ones((head_dim, head_dim)))
    return tuple(jnp.asarray(m, LOW) for m in (sums, spread, pick, block))


def adamw(weight, first_moment, second_moment, gradient, factor, rate, decay):
    clipped = gradient * factor
    new_first = BETA_ONE * first_moment + (1.0 - BETA_ONE) * clipped
    new_second = BETA_TWO * second_moment + (1.0 - BETA_TWO) * clipped * clipped
    denominator = jnp.sqrt(new_second / (1.0 - BETA_TWO**STEP)) + ADAM_EPS
    new_weight = (
        weight * (1.0 - rate * decay) - rate * (new_first / (1.0 - BETA_ONE**STEP)) / denominator
    )
    return (new_weight, new_first, new_second)


def local(
    tokens,
    condition,
    shapes,
    cotangent,
    ada_weight,
    ada_first,
    ada_second,
    qkv_weight,
    qkv_first,
    qkv_second,
    out_weight,
    out_first,
    out_second,
    up_weight,
    up_first,
    up_second,
    down_weight,
    down_first,
    down_second,
    head_scale,
    scale_first,
    scale_second,
    *,
    dp_size,
    fsdp_size,
):
    net = Net(fsdp_size, dp_size)
    core = net.core
    images = shapes.shape[0]
    width = tokens.shape[1]
    seq_len = tokens.shape[0] // images
    head_count = head_scale.shape[0]
    head_dim = width // head_count

    table = net.table(net.gather_order)
    scatter_table = net.table(tuple(order[::-1] for order in net.scatter_order))

    ada_rows = ada_weight.shape[1] * net.sub
    ada_flat = net.join_sub(ada_weight.transpose(1, 0, 2).reshape(ada_weight.shape[1], 2 * width))
    ada_pieces = net.gather(
        lax.dynamic_slice_in_dim(ada_flat, core * width, width, axis=1).astype(LOW)
    )
    qkv_pieces = net.gather(half_rows(net.join_sub(qkv_weight), core))
    out_pieces = net.gather(half_rows(net.join_sub(out_weight), core))
    up_pieces = net.gather(half_rows(net.join_sub(up_weight), core))
    down_pieces = net.gather(half_rows(net.join_sub(down_weight), core))

    condition_blocks = condition.reshape(images, 16, ada_rows)

    def project(low, high, order):
        weight = jnp.concatenate([low, high], axis=0)
        cond = jnp.take(condition_blocks, order, axis=1)
        return 1.0 + jnp.einsum("igr,grn->in", cond, weight, preferred_element_type=WIDE)

    scale_own = project(ada_pieces[0], ada_pieces[1], table[:16])
    scale_sib = project(ada_pieces[2], ada_pieces[3], table[16:32])
    scale_one = jnp.where(core == 0, scale_own, scale_sib)[:, None]
    scale_two = jnp.where(core == 0, scale_sib, scale_own)[:, None]

    turns, valid = turn_tables(shapes, seq_len, head_dim)
    sums, spread, pick, block = head_matrices(width, head_dim)
    root = jnp.repeat(jnp.sqrt(head_scale), head_dim)[None]

    act_one, q, k, v, pack = front(
        table, tokens, scale_one, qkv_pieces, sums, spread, root, turns, images
    )
    o, lse = attend(q, k, v, valid, images)
    mid, act_two = middle_block(table, o, tokens, scale_two, out_pieces, images)
    hid, dgu = gate_block(table, act_two, cotangent, up_pieces, down_pieces, images)

    def reduce_blocks(act, grad):
        send = weight_half(scatter_table, act, grad, 1)
        held = weight_half(scatter_table, act, grad, 0, net.swap(send))
        mine = net.scatter(held.reshape(16, held.shape[0] // 16, held.shape[1]))
        other = net.swap(mine)
        gradient = jnp.where(
            core == 0,
            jnp.concatenate([mine, other], axis=0),
            jnp.concatenate([other, mine], axis=0),
        ).astype(WIDE)
        return net.split_sub(gradient)

    grad_down = reduce_blocks(hid, cotangent)
    grad_up = reduce_blocks(act_two, dgu)
    dmid, db, do, dscale_two = branch_block(
        table, dgu, cotangent, mid, scale_two, up_pieces, out_pieces, images
    )
    grad_outw = reduce_blocks(o, db)
    dproj, dhead = attend_back(
        q, k, v, o, do, lse, valid, pack, spread, root, pick, block, turns, images
    )
    grad_qkv = reduce_blocks(act_one, dproj)
    input_grad, dscale_one = input_block(
        table, dproj, tokens, dmid, scale_one, qkv_pieces, images
    )
    block_output = result_block(table, hid, mid, down_pieces, images)

    dhead = jnp.sum(dhead.reshape(images, head_count, head_dim)[:, :, 0], axis=0)
    dhead = jnp.broadcast_to(dhead / (2.0 * head_scale), (images, head_count)) / images
    early = net.gather_small(jnp.concatenate([condition.astype(WIDE), dscale_two[:, 0]], axis=1))
    late = net.gather_small(jnp.concatenate([dscale_one[:, 0], dhead], axis=1))
    own_rows = ada_weight.shape[1]
    cond_own = lax.dynamic_slice_in_dim(
        early[:, : condition.shape[1]], lax.axis_index("fsdp") * own_rows, own_rows, axis=1
    )
    grad_ada = jnp.stack(
        [
            jnp.dot(cond_own.T, late[:, :width], precision=PRECISE),
            jnp.dot(cond_own.T, early[:, condition.shape[1] :], precision=PRECISE),
        ]
    )
    head_grad = jnp.sum(late[:, width:], axis=0)

    owned = (grad_ada, grad_qkv, grad_outw, grad_up, grad_down)
    local_squares = (
        jnp.sum(owned[0] * owned[0]) + jnp.sum(owned[1] * owned[1]) + jnp.sum(owned[2] * owned[2])
    )
    local_squares = local_squares + jnp.sum(owned[3] * owned[3]) + jnp.sum(owned[4] * owned[4])
    total = net.total(local_squares) + jnp.sum(head_grad * head_grad)
    grad_norm = jnp.sqrt(total)
    factor = jnp.minimum(1.0, CLIP / (grad_norm + 1e-06))
    ada_new = adamw(ada_weight, ada_first, ada_second, owned[0], factor, RATE, DECAY)
    qkv_new = adamw(qkv_weight, qkv_first, qkv_second, owned[1], factor, RATE, DECAY)
    out_new = adamw(out_weight, out_first, out_second, owned[2], factor, OUTPUT_RATE, DECAY)
    up_new = adamw(up_weight, up_first, up_second, owned[3], factor, RATE, DECAY)
    down_new = adamw(down_weight, down_first, down_second, owned[4], factor, RATE, DECAY)
    scale_new = adamw(head_scale, scale_first, scale_second, head_grad, factor, SCALE_RATE, 0.0)
    return (
        block_output,
        input_grad,
        grad_norm,
        *ada_new,
        *qkv_new,
        *out_new,
        *up_new,
        *down_new,
        *scale_new,
    )


def solution(mesh):
    tokens = P(("dp", "fsdp"), None)
    ada = P(None, "fsdp", None)
    rows = P("fsdp", None)
    return jax.shard_map(
        functools.partial(local, dp_size=mesh.shape["dp"], fsdp_size=mesh.shape["fsdp"]),
        mesh=mesh,
        in_specs=(tokens,) * 4 + (ada,) * 3 + (rows,) * 12 + (P(),) * 3,
        out_specs=(tokens, tokens, P()) + (ada,) * 3 + (rows,) * 12 + (P(),) * 3,
        check_vma=False,
    )
```

```python
import functools
import math

import jax
import jax.numpy as jnp
import numpy as np
from jax import lax
from jax.experimental import pallas as pl
from jax.experimental.pallas import tpu as pltpu
from jax.sharding import PartitionSpec as P

FF = 3072
STEP = 10


NORM_EPS = 1e-06
COSINE_EPS = 1e-06
ROPE_BASE = 100.0
CLIP = 1.0
RATE = 0.02
OUTPUT_RATE = 0.2
SCALE_RATE = 8.0
BETA_ONE = 0.9
BETA_TWO = 0.95
ADAM_EPS = 1e-08
DECAY = 0.01
PRECISE = lax.Precision.HIGHEST
AXES = ("dp", "fsdp")
LOW = jnp.bfloat16
WIDE = jnp.float32


ORDERS = (((8, 4, 1, 2), (2, 8, 4, 1)), ((8, 4, 2, 1), (1, 8, 4, 2)))


class Net:
    def __init__(self, size, dp_size):
        self.size = size
        self.dp_size = dp_size
        self.sub = size // 16
        self.core = lax.axis_index("dp")
        self.me = lax.axis_index("fsdp") // self.sub
        self.tables = tuple(self.table(order) for order in ORDERS)

    def exchange(self, array, bits):
        pairs = []
        for core in range(self.dp_size):
            for place in range(self.size):
                target = place ^ (bits[core % 2] * self.sub)
                pairs.append((core * self.size + place, core * self.size + target))
        return lax.ppermute(array, AXES, pairs)

    def cross(self, array, parity, stage):
        order = ORDERS[parity]
        return self.exchange(array, (order[0][stage], order[1][stage]))

    def swap(self, array):
        pairs = []
        for core in range(self.dp_size):
            for place in range(self.size):
                pairs.append((core * self.size + place, (core ^ 1) * self.size + place))
        return lax.ppermute(array, AXES, pairs)

    def table(self, order):
        index = lax.iota(jnp.int32, 32)
        side = self.core ^ (index >> 4)
        value = jnp.full((32,), self.me, jnp.int32)
        for stage in range(4):
            bit = jnp.where(side == 0, order[0][stage], order[1][stage])
            value = value ^ ((index >> stage & 1) * bit)
        return jnp.concatenate([value, self.core[None]]).astype(jnp.int32)

    def groups(self):
        return [list(range(g * self.sub, (g + 1) * self.sub)) for g in range(16)]

    def join_sub(self, shard):
        if self.sub == 1:
            return shard
        return lax.all_gather(shard, "fsdp", axis=0, tiled=True, axis_index_groups=self.groups())

    def split_sub(self, gradient):
        gathered = lax.all_gather(gradient, "fsdp", axis=0, axis_index_groups=self.groups())
        rows = gradient.shape[0] // self.sub
        place = lax.axis_index("fsdp") % self.sub
        return lax.dynamic_slice_in_dim(jnp.sum(gathered, axis=0), place * rows, rows, axis=0)

    def total(self, value):
        for bits in ((1, 2, 3), (4, 8, 12)):
            value = value + sum(self.exchange(value, (bit, bit)) for bit in bits)
        return value + self.swap(value)


class Line:
    def __init__(self):
        self.last = None
        self.waits = []

    def call(self, kernel, args, in_specs, prefetch=0, **kwargs):
        deps = []
        if self.last is not None:
            token = self.last
            if self.waits:
                token = lax.optimization_barrier((token, *self.waits))[0]
            deps = [token]
        self.waits = []
        count = len(deps)
        one = not isinstance(kwargs["out_shape"], (list, tuple))
        shapes = [kwargs["out_shape"]] if one else list(kwargs["out_shape"])
        specs = kwargs["out_specs"]
        specs = [specs] if not isinstance(specs, (list, tuple)) else list(specs)
        place = prefetch + len(in_specs) + len(shapes)

        def body(*refs):
            refs = refs[:prefetch] + refs[prefetch + count :]
            refs[place][...] = jnp.zeros((8, 128), WIDE)
            kernel(*refs[:place], *refs[place + 1 :])

        in_specs = [ANY] * count + list(in_specs)
        out_specs = specs + [whole((8, 128)) if "grid" in kwargs else VMEM]
        del kwargs["out_specs"]
        kwargs["out_shape"] = shapes + [jax.ShapeDtypeStruct((8, 128), WIDE)]
        if prefetch:
            kwargs["grid_spec"] = pltpu.PrefetchScalarGridSpec(
                num_scalar_prefetch=prefetch,
                grid=kwargs.pop("grid"),
                in_specs=in_specs,
                out_specs=out_specs,
                scratch_shapes=kwargs.pop("scratch_shapes", []),
            )
        else:
            kwargs["in_specs"] = in_specs
            kwargs["out_specs"] = out_specs
        *outs, self.last = pl.pallas_call(body, **kwargs)(*args[:prefetch], *deps, *args[prefetch:])
        return outs[0] if one else outs

    def pin(self, array):
        if self.last is not None:
            array, _ = lax.optimization_barrier((array, self.last))
        self.waits.append(array)
        return array


class Gather:
    def __init__(self, net, line, parity, half):
        self.net, self.line, self.parity = net, line, parity
        self.held = line.pin(half)
        self.got = net.cross(self.held, parity, 0)

    def second(self):
        self.held = join(self.line, self.held, self.got)
        self.got = self.net.cross(self.held, self.parity, 1)

    def third(self):
        self.held = join(self.line, self.held, self.got)
        self.near = self.net.cross(self.held, self.parity, 2)
        self.far = self.net.cross(self.held, self.parity, 3)

    def fourth(self):
        self.near = self.line.pin(self.near)
        self.last = self.net.cross(self.near, self.parity, 3)
        self.swapped = [self.net.swap(self.held), self.net.swap(self.near)]

    def fifth(self):
        self.far = self.line.pin(self.far)
        self.swapped.append(self.net.swap(self.far))

    def finish(self):
        self.last = self.line.pin(self.last)
        self.swapped = [self.line.pin(array) for array in self.swapped]
        self.swapped.append(self.net.swap(self.last))
        self.pieces = (self.held, self.near, self.far, self.last, *self.swapped)


class Scatter:
    def __init__(self, net, line, parity, keep, send):
        self.net, self.line, self.parity = net, line, parity
        self.keep, self.send = keep, send
        self.part = [None, None, net.swap(send[2]), net.swap(send[3])]

    def first(self):
        two, three = fold_pair(self.line, self.keep[2:], self.part[2:])
        self.part[1] = self.net.swap(self.line.pin(self.send[1]))
        self.part[0] = self.net.swap(self.line.pin(self.send[0]))
        self.got = self.net.cross(three, self.parity, 3)
        self.late = self.net.cross(two, self.parity, 3)

    def second(self):
        self.part[0] = self.line.pin(self.part[0])
        (held,) = fold(self.line, self.keep[1], (self.part[1], self.got), 1)
        self.got = self.net.cross(held, self.parity, 2)

    def third(self):
        self.held, send = fold(self.line, self.keep[0], (self.part[0], self.late, self.got), 2)
        self.got = self.net.cross(send, self.parity, 1)

    def fourth(self):
        self.held, send = fold(self.line, self.held, (self.got,), 2)
        self.got = self.net.cross(send, self.parity, 0)

    def finish(self):
        self.mine, self.square = fold_last(self.line, self.held[0], self.got[0])
        self.other = self.net.swap(self.mine)


class SmallGather:
    def __init__(self, net, line, rows):
        self.net, self.line = net, line
        self.held = line.pin(rows)
        self.send((1, 2, 3))

    def send(self, bits):
        self.got = [self.net.exchange(self.held, (bit, bit)) for bit in bits]

    def step(self):
        got = [self.line.pin(array) for array in self.got]
        self.held = jnp.concatenate([self.held, *got], axis=0)

    def second(self):
        self.step()
        self.send((4, 8, 12))


ANY = pl.BlockSpec(memory_space=pl.ANY)
SMEM = pl.BlockSpec(memory_space=pltpu.SMEM)
VMEM = pl.BlockSpec(memory_space=pltpu.VMEM)
NT = (((1,), (1,)), ((), ()))
TN = (((0,), (0,)), ((), ()))
VMEM_LIMIT = 56 * 1024 * 1024
SMALL_LIMIT = 16 * 1024 * 1024


def load_weight(table_ref, pieces, full_ref, sems):
    core = table_ref[32]
    rows = pieces[0].shape[1]
    copies = []
    for number, piece in enumerate(pieces):
        side = core if number < 4 else 1 - core
        for index in range(4):
            start = pl.multiple_of(table_ref[number * 4 + index] * (2 * rows) + side * rows, 16)
            copies.append(
                pltpu.make_async_copy(
                    piece.at[index], full_ref.at[pl.ds(start, rows)], sems.at[number, index]
                )
            )
    return copies


def part_of(pieces, first, size):
    return tuple(piece.at[:, :, first : first + size] for piece in pieces)


def fetch(copies):
    for copy in copies:
        copy.start()
    for copy in copies:
        copy.wait()


SEMS = pltpu.SemaphoreType.DMA((8, 4))


def params(dims):
    return pltpu.CompilerParams(
        dimension_semantics=("arbitrary",) * dims, vmem_limit_bytes=VMEM_LIMIT
    )


def cost(flops, size):
    return pl.CostEstimate(flops=flops, bytes_accessed=size, transcendentals=0)


def mul(a, b):
    return jnp.dot(a, b, preferred_element_type=WIDE)


def mul_nt(a, b):
    return lax.dot_general(a, b, NT, preferred_element_type=WIDE)


def mul_tn(a, b):
    return lax.dot_general(a, b, TN, preferred_element_type=WIDE)


def whole(shape):
    return pl.BlockSpec(shape, lambda *_: (0,) * len(shape))


def turned_block(width, seq):
    return pl.BlockSpec((width, seq), lambda i: (0, i))


def turned_shape(width, tokens):
    return jax.ShapeDtypeStruct((width, tokens), LOW)


def grouped(images):
    return 2 if images % 2 == 0 else 1


def scaled(values, scale_ref):
    count = scale_ref.shape[0]
    rows = values.shape[0] // count
    parts = [values[i * rows : i * rows + rows] * scale_ref[i] for i in range(count)]
    return parts[0] if count == 1 else jnp.concatenate(parts, axis=0)


def norm_back(grad, values, scale_ref, dscale_ref):
    inverse = lax.rsqrt(jnp.mean(values * values, axis=-1, keepdims=True) + NORM_EPS)
    normed = values * inverse
    product = grad * normed
    count = scale_ref.shape[0]
    rows = values.shape[0] // count
    for i in range(count):
        dscale_ref[i] = jnp.sum(product[i * rows : i * rows + rows], axis=0, keepdims=True)
    grad = scaled(grad, scale_ref)
    inner = jnp.mean(grad * normed, axis=-1, keepdims=True)
    return inverse * (grad - normed * inner)


def rotate(values, cos_rep, up_rep, down_rep, sign):
    ahead = pltpu.roll(values, values.shape[-1] - 16, 1)
    behind = pltpu.roll(values, 16, 1)
    turned = ahead * up_rep + behind * down_rep
    return values * cos_rep + (turned if sign > 0 else -turned)


def join_kernel(a_ref, b_ref, out_ref, sems):
    count = a_ref.shape[0]
    fetch(
        [
            pltpu.make_async_copy(a_ref, out_ref.at[:count], sems.at[0]),
            pltpu.make_async_copy(b_ref, out_ref.at[count:], sems.at[1]),
        ]
    )


def join(line, a, b):
    shape = (2 * a.shape[0],) + a.shape[1:]
    return line.call(
        join_kernel,
        (a, b),
        [ANY, ANY],
        out_specs=VMEM,
        out_shape=jax.ShapeDtypeStruct(shape, a.dtype),
        scratch_shapes=[pltpu.SemaphoreType.DMA((2,))],
        compiler_params=pltpu.CompilerParams(vmem_limit_bytes=SMALL_LIMIT),
        cost_estimate=cost(0, 4 * math.prod(shape)),
        name="join",
    )


def fold_kernel(count, held_ref, *refs):
    outs = refs[count:]
    total = held_ref[...].astype(WIDE)
    for ref in refs[:count]:
        total += ref[...].astype(WIDE)
    size = outs[0].shape[0]
    for number, out in enumerate(outs):
        out[...] = total[number * size : number * size + size].astype(out.dtype)


def fold(line, held, others, parts):
    shape = (held.shape[0] // parts,) + held.shape[1:]
    return line.call(
        functools.partial(fold_kernel, len(others)),
        (held, *others),
        [VMEM] * (1 + len(others)),
        out_specs=[VMEM] * parts,
        out_shape=[jax.ShapeDtypeStruct(shape, held.dtype)] * parts,
        compiler_params=pltpu.CompilerParams(vmem_limit_bytes=SMALL_LIMIT),
        cost_estimate=cost(0, 2 * math.prod(held.shape) * (2 + len(others))),
        name="fold",
    )


def fold_pair_kernel(a_ref, b_ref, c_ref, d_ref, first_ref, second_ref):
    first_ref[...] = (a_ref[...].astype(WIDE) + c_ref[...].astype(WIDE)).astype(LOW)
    second_ref[...] = (b_ref[...].astype(WIDE) + d_ref[...].astype(WIDE)).astype(LOW)


def fold_pair(line, held, others):
    shape = jax.ShapeDtypeStruct(held[0].shape, LOW)
    return line.call(
        fold_pair_kernel,
        (*held, *others),
        [VMEM] * 4,
        out_specs=[VMEM] * 2,
        out_shape=[shape] * 2,
        compiler_params=pltpu.CompilerParams(vmem_limit_bytes=SMALL_LIMIT),
        cost_estimate=cost(0, 12 * math.prod(shape.shape)),
        name="fold_pair",
    )


def fold_last_kernel(held_ref, other_ref, out_ref, square_ref):
    total = (held_ref[...].astype(WIDE) + other_ref[...].astype(WIDE)).astype(LOW)
    out_ref[...] = total
    total = total.astype(WIDE)
    sums = jnp.sum(jnp.sum(total * total, axis=0, keepdims=True), axis=1, keepdims=True)
    square_ref[...] = jnp.broadcast_to(sums, square_ref.shape)


def fold_last(line, held, other):
    return line.call(
        fold_last_kernel,
        (held, other),
        [VMEM, VMEM],
        out_specs=[VMEM, VMEM],
        out_shape=[jax.ShapeDtypeStruct(held.shape, LOW), jax.ShapeDtypeStruct((1, 128), WIDE)],
        compiler_params=pltpu.CompilerParams(vmem_limit_bytes=SMALL_LIMIT),
        cost_estimate=cost(0, 6 * math.prod(held.shape)),
        name="fold_last",
    )


def head_kernel(core_ref, qkv_ref, out_ref, ada_ref, *outs):
    rows, size = qkv_ref.shape[0], ada_ref.shape[2]
    for number, out in enumerate(outs):
        for block in range(4):
            at = (4 * number + block) * size
            values = qkv_ref[:, at : at + size] if at < qkv_ref.shape[1] else out_ref[:, at - qkv_ref.shape[1] : at - qkv_ref.shape[1] + size]
            out[0, block * rows : block * rows + rows, :] = values.astype(LOW)
        out[0, 4 * rows :, :] = ada_ref[number].astype(LOW)


def head_parts(line, core, qkv, out, ada):
    rows, width = qkv.shape[0] // 2, out.shape[1]
    size = width // 2
    shape = (1, 4 * rows + ada.shape[1], size)
    return line.call(
        head_kernel,
        (core[None], qkv, out, ada),
        [pl.BlockSpec((rows, 3 * width), lambda i, c: (c[0], 0)),
         pl.BlockSpec((rows, width), lambda i, c: (c[0], 0)),
         pl.BlockSpec((2, ada.shape[1], size), lambda i, c: (0, 0, c[0]))],
        prefetch=1,
        grid=(1,),
        out_specs=[whole(shape)] * 2,
        out_shape=[jax.ShapeDtypeStruct(shape, LOW)] * 2,
        compiler_params=params(1),
        cost_estimate=cost(0, 2 << 20),
        name="head_parts",
    )


def load_head(table_ref, pieces, blocks, full_ref, sems, ada_ref=None, ada_sems=None):
    core = table_ref[32]
    size = pieces[0].shape[2]
    ada_rows = 0 if ada_ref is None else ada_ref.shape[0] // 16
    copies = []
    for number, piece in enumerate(pieces):
        side = core if number < 4 else 1 - core
        for index in range(4):
            owner = table_ref[number * 4 + index]
            start = pl.multiple_of(owner * 64 + side * 32, 16)
            for place, block in enumerate(blocks):
                copies.append(
                    pltpu.make_async_copy(
                        piece.at[index, block * 32 : block * 32 + 32],
                        full_ref.at[pl.ds(start, 32), place * size : place * size + size],
                        sems.at[place, number, index],
                    )
                )
            if ada_ref is not None:
                start = pl.multiple_of(owner * ada_rows, 16)
                column = pl.multiple_of(side * size, 128)
                copies.append(
                    pltpu.make_async_copy(
                        piece.at[index, 128 : 128 + ada_rows],
                        ada_ref.at[pl.ds(start, ada_rows), pl.ds(column, size)],
                        ada_sems.at[number, index],
                    )
                )
    return copies


def cut_kernel(core_ref, up_ref, down_ref, *outs):
    width = down_ref.shape[2]
    low = lax.broadcasted_iota(jnp.int32, (up_ref.shape[0], 128), 1) < 64
    for start in range(0, 2 * width, 128):
        first, second, third = (up_ref[:, 3 * start + 128 * i : 3 * start + 128 * i + 128] for i in range(3))
        lanes = slice(start, start + 128)
        outs[0][0, :, lanes] = jnp.where(low, first, second).astype(LOW)
        outs[1][0, :, lanes] = pltpu.roll(jnp.where(low, third, first), 64, 1).astype(LOW)
        outs[2][0, :, lanes] = jnp.where(low, second, third).astype(LOW)
    for part, out in enumerate(outs):
        out[0, :, 2 * width :] = down_ref[part].astype(LOW)


def cut_parts(line, core, up, down):
    rows, columns = up.shape[0] // 2, up.shape[1]
    width = down.shape[2]
    return line.call(
        cut_kernel,
        (core[None], up, down),
        [pl.BlockSpec((rows, columns), lambda i, c: (c[0], 0)),
         pl.BlockSpec((3, rows, width), lambda i, c: (0, c[0], 0))],
        prefetch=1,
        grid=(1,),
        out_specs=[whole((1, rows, 3 * width))] * 3,
        out_shape=[jax.ShapeDtypeStruct((1, rows, 3 * width), LOW)] * 3,
        compiler_params=params(1),
        cost_estimate=cost(0, 4 << 20),
        name="cut",
    )


def load_qkv(even_ref, odd_ref, pieces, w_ref, sems, ada_ref=None, ada_sems=None):
    width = w_ref.shape[0]
    adas = (None, None) if ada_ref is None else (ada_ref.at[0], ada_ref.at[1])
    semaphores = (None, None) if ada_ref is None else (ada_sems.at[0], ada_sems.at[1])
    return load_head(
        even_ref, pieces[:8], (0, 1, 2, 3), w_ref.at[:, : 2 * width], sems.at[0], adas[0], semaphores[0]
    ) + load_head(
        odd_ref, pieces[8:], (0, 1), w_ref.at[:, 2 * width :], sems.at[1], adas[1], semaphores[1]
    )


def front_kernel(group, even_ref, odd_ref, x_ref, cond_ref, *rest):
    pieces, rest = rest[:16], rest[16:]
    sums_ref, spread_ref, root_ref, cos_ref, up_ref, down_ref, *rest = rest
    act_ref, q_ref, k_ref, v_ref, pack_ref, one_ref, two_ref, w_ref, ada_ref, sems, ada_sems = rest

    @pl.when(pl.program_id(0) == 0)
    def _():
        fetch(load_qkv(even_ref, odd_ref, pieces, w_ref, sems, ada_ref, ada_sems))
        for number, out in enumerate((one_ref, two_ref)):
            scale = 1.0 + mul(cond_ref[...], ada_ref[number])
            for image in range(scale.shape[0]):
                out[image] = scale[image : image + 1]

    scale_ref = one_ref.at[pl.ds(pl.program_id(0) * group, group)]
    width = x_ref.shape[1]
    x = x_ref[...].astype(WIDE)
    inverse = lax.rsqrt(jnp.mean(x * x, axis=-1, keepdims=True) + NORM_EPS)
    act = scaled(x * inverse, scale_ref).astype(LOW)
    act_ref[...] = act.T
    v_ref[...] = mul(act, w_ref[:, 2 * width :]).astype(LOW)
    q = mul(act, w_ref[:, :width])
    k = mul(act, w_ref[:, width : 2 * width])
    sums = mul((q * q).astype(LOW), sums_ref[0]) + mul((k * k).astype(LOW), sums_ref[1])
    factor = lax.rsqrt(sums + COSINE_EPS)
    high = factor.astype(LOW)
    low = (factor - high.astype(WIDE)).astype(LOW)
    lane = lax.broadcasted_iota(jnp.int32, factor.shape, 1)
    pack = jnp.where(lane < 32, high.astype(WIDE), jnp.where(lane < 64, low.astype(WIDE), 0.0))
    pack = pack.astype(LOW)
    pack_ref[...] = pack
    q = q * mul(pack, spread_ref[0]) * root_ref[...]
    k = k * mul(pack, spread_ref[1]) * root_ref[...]
    cos_rep, up_rep, down_rep = cos_ref[...], up_ref[...], down_ref[...]
    for pair in range(width // 128):
        lanes = slice(pair * 128, pair * 128 + 128)
        q_ref[:, lanes] = rotate(q[:, lanes], cos_rep, up_rep, down_rep, 1).astype(LOW)
        k_ref[:, lanes] = rotate(k[:, lanes], cos_rep, up_rep, down_rep, 1).astype(LOW)


def front(line, tables, x, cond, pieces, sums, spread, root, turns, images):
    tokens, width = x.shape
    group = grouped(images)
    seq = tokens // images * group
    row = pl.BlockSpec((seq, width), lambda i: (i, 0))
    narrow = pl.BlockSpec((seq, 128), lambda i: (i, 0))
    full = jax.ShapeDtypeStruct((tokens, width), LOW)
    return line.call(
        functools.partial(front_kernel, group),
        (*tables, x, cond, *pieces, sums, spread, root, *turns),
        [SMEM, SMEM, row, whole(cond.shape), *[ANY] * 16,
                  whole(sums.shape), whole(spread.shape), whole(root.shape), narrow, narrow, narrow],
        grid=(images // group,),
        out_specs=[turned_block(width, seq), row, row, row, narrow, whole((images, 1, width)), whole((images, 1, width))],
        out_shape=[turned_shape(width, tokens), full, full, full, jax.ShapeDtypeStruct((tokens, 128), LOW),
                   jax.ShapeDtypeStruct((images, 1, width), WIDE), jax.ShapeDtypeStruct((images, 1, width), WIDE)],
        scratch_shapes=[pltpu.VMEM((width, 3 * width), LOW), pltpu.VMEM((2, cond.shape[1], width), LOW),
                        pltpu.SemaphoreType.DMA((2, 4, 8, 4)), pltpu.SemaphoreType.DMA((2, 8, 4))],
        compiler_params=params(1),
        cost_estimate=cost(6 * tokens * width * width, 20 << 20),
        name="front",
    )


def attend_kernel(q_ref, k_ref, v_ref, valid_ref, o_ref, turned_ref, lse_ref):
    seq, width = q_ref.shape
    valid = valid_ref[...]
    lane = lax.broadcasted_iota(jnp.int32, (seq, 128), 1)
    first = lane < 64
    totals = jnp.zeros((seq, 128), WIDE)
    zero = jnp.zeros((seq, 128), LOW)
    for pair in range(width // 128):
        lanes = slice(pair * 128, pair * 128 + 128)
        q, k = q_ref[:, lanes], k_ref[:, lanes]
        v = v_ref[:, lanes] * valid
        mixed = None
        for half in range(2):
            pick = first if half == 0 else jnp.logical_not(first)
            scores = mul_nt(jnp.where(pick, q, zero), k)
            weights = jnp.exp(scores).astype(LOW)
            right = jnp.concatenate([jnp.where(pick, v, zero), valid], axis=1)
            both = mul(weights, right)
            total = both[:, 128:]
            part = both[:, :128] / total
            mixed = part if mixed is None else mixed + part
            totals = jnp.where(lane == 2 * pair + half, total, totals)
        mixed = mixed.astype(LOW)
        o_ref[:, lanes] = mixed
        turned_ref[lanes, :] = mixed.T
    lane_ok = lane < width // 64
    lse = jnp.log(jnp.where(lane_ok, totals, 1.0))
    lse_ref[0] = lse.T[: width // 64]


def attend(line, q, k, v, valid, images):
    tokens, width = q.shape
    seq = tokens // images
    row = pl.BlockSpec((seq, width), lambda i: (i, 0))
    heads = width // 64
    return line.call(
        attend_kernel,
        (q, k, v, valid),
        [row, row, row, pl.BlockSpec((seq, 128), lambda i: (i, 0))],
        grid=(images,),
        out_specs=[row, turned_block(width, seq), pl.BlockSpec((1, heads, seq), lambda i: (i, 0, 0))],
        out_shape=[jax.ShapeDtypeStruct((tokens, width), LOW), turned_shape(width, tokens),
                   jax.ShapeDtypeStruct((images, heads, seq), WIDE)],
        compiler_params=params(1),
        cost_estimate=cost(16 * tokens * seq * width, 8 << 20),
        name="attend",
    )


def middle_kernel(table_ref, o_ref, x_ref, scale_ref, *rest):
    pieces = rest[:8]
    mid_ref, act_ref, turned_ref, w_ref, sems = rest[8:]

    @pl.when(pl.program_id(0) == 0)
    def _():
        fetch(load_head(table_ref, pieces, (2, 3), w_ref, sems))

    mid = x_ref[...].astype(WIDE) + mul(o_ref[...], w_ref[...])
    mid_ref[...] = mid
    inverse = lax.rsqrt(jnp.mean(mid * mid, axis=-1, keepdims=True) + NORM_EPS)
    act = scaled(mid * inverse, scale_ref).astype(LOW)
    act_ref[...] = act
    turned_ref[...] = act.T


def middle_block(line, table, o, x, scale, pieces, images):
    tokens, width = x.shape
    group = grouped(images)
    seq = tokens // images * group
    row = pl.BlockSpec((seq, width), lambda i: (i, 0))
    return line.call(
        middle_kernel,
        (table, o, x, scale, *pieces),
        [SMEM, row, row, pl.BlockSpec((group, 1, width), lambda i: (i, 0, 0))] + [ANY] * 8,
        grid=(images // group,),
        out_specs=[row, row, turned_block(width, seq)],
        out_shape=[jax.ShapeDtypeStruct((tokens, width), WIDE), jax.ShapeDtypeStruct((tokens, width), LOW),
                   turned_shape(width, tokens)],
        scratch_shapes=[pltpu.VMEM((width, width), LOW), pltpu.SemaphoreType.DMA((2, 8, 4))],
        compiler_params=params(1),
        cost_estimate=cost(2 * tokens * width * width, 12 << 20),
        name="middle",
    )


def part_kernel(first, last, table_ref, act_ref, dy_ref, *rest):
    rest = list(rest)
    pieces = tuple(rest.pop(0) for _ in range(8))
    if last:
        mid_ref, scale_ref = rest.pop(0), rest.pop(0)
        out_pieces = tuple(rest.pop(0) for _ in range(8))
    acc_ref = None if first else rest.pop(0)
    hid_ref, dgu_ref, turned_ref = rest.pop(0), rest.pop(0), rest.pop(0)
    if last:
        dmid_ref, db_ref, do_ref, dscale_ref = (rest.pop(0) for _ in range(4))
    else:
        da_ref = rest.pop(0)
    w_ref, sems = rest.pop(0), rest.pop(0)
    if last:
        out_ref, sems_out = rest.pop(0), rest.pop(0)

    @pl.when(pl.program_id(0) == 0)
    def _():
        copies = load_weight(table_ref, pieces, w_ref, sems)
        if last:
            copies = copies + load_head(table_ref, out_pieces, (2, 3), out_ref, sems_out)
        fetch(copies)

    width = act_ref.shape[1]
    act, dy = act_ref[...], dy_ref[...]
    size = 512
    for start in range(0, width, size):
        cols = slice(start, start + size)
        above = slice(width + start, width + start + size)
        gate = mul(act, w_ref[:, cols])
        upper = mul(act, w_ref[:, above])
        grad = mul_nt(dy, w_ref[start : start + size, 2 * width :]).astype(LOW).astype(WIDE)
        cdf = 0.5 * (1.0 + lax.erf(gate * math.sqrt(0.5)))
        bell = jnp.exp(-0.5 * gate * gate) * (1.0 / math.sqrt(2.0 * math.pi))
        gelu = gate * cdf
        hid = (gelu * upper).astype(LOW)
        hid_ref[:, cols] = hid
        turned_ref[cols, :] = hid.T
        dgu_ref[:, cols] = (grad * upper * (cdf + gate * bell)).astype(LOW)
        dgu_ref[:, above] = (grad * gelu).astype(LOW)
    total = mul_nt(dgu_ref[:, :width], w_ref[:, :width])
    total += mul_nt(dgu_ref[:, width:], w_ref[:, width : 2 * width])
    if not first:
        total += acc_ref[...]
    if not last:
        da_ref[...] = total
        return
    dmid = dy.astype(WIDE) + norm_back(total, mid_ref[...], scale_ref, dscale_ref)
    dmid_ref[...] = dmid
    low = dmid.astype(LOW)
    db_ref[...] = low
    do_ref[...] = mul_nt(low, out_ref[...]).astype(LOW)


def geglu_part(line, table, act, dy, pieces, images, acc=None, final=None):
    tokens, width = act.shape
    group = grouped(images)
    seq = tokens // images * group
    first, last = acc is None, final is not None
    row = pl.BlockSpec((seq, width), lambda i: (i, 0))
    one = pl.BlockSpec((group, 1, width), lambda i: (i, 0, 0))
    args = [table, act, dy, *pieces]
    in_specs = [SMEM, row, row] + [ANY] * 8
    if last:
        mid, scale, out_pieces = final
        args += [mid, scale, *out_pieces]
        in_specs += [row, one] + [ANY] * 8
    if not first:
        args.append(acc)
        in_specs.append(row)
    low = jax.ShapeDtypeStruct((tokens, width), LOW)
    wide = jax.ShapeDtypeStruct((tokens, width), WIDE)
    out_specs = [row, pl.BlockSpec((seq, 2 * width), lambda i: (i, 0)), turned_block(width, seq)]
    out_shape = [low, jax.ShapeDtypeStruct((tokens, 2 * width), LOW), turned_shape(width, tokens)]
    scratch = [pltpu.VMEM((width, 3 * width), LOW), SEMS]
    if last:
        out_specs += [row, row, row, one]
        out_shape += [wide, low, low, jax.ShapeDtypeStruct((images, 1, width), WIDE)]
        scratch += [pltpu.VMEM((width, width), LOW), pltpu.SemaphoreType.DMA((2, 8, 4))]
    else:
        out_specs.append(row)
        out_shape.append(wide)
    return line.call(
        functools.partial(part_kernel, first, last),
        args,
        in_specs,
        grid=(images // group,),
        out_specs=out_specs,
        out_shape=out_shape,
        scratch_shapes=scratch,
        compiler_params=params(1),
        cost_estimate=cost((12 if last else 10) * tokens * width * width, 30 << 20),
        name="geglu_part",
    )


def attend_back_kernel(q_ref, k_ref, v_ref, o_ref, do_ref, lse_ref, valid_ref, pack_ref, spread_ref,
                       root_ref, pick_ref, block_ref, cos_ref, up_ref, down_ref, dproj_ref, dhead_ref):
    seq, width = q_ref.shape
    valid = valid_ref[...]
    valid_wide = valid.astype(WIDE)
    first = lax.broadcasted_iota(jnp.int32, (seq, 128), 1) < 64
    zero = jnp.zeros((seq, 128), LOW)
    cos_rep, up_rep, down_rep = cos_ref[...], up_ref[...], down_ref[...]
    product = (do_ref[...].astype(WIDE) * o_ref[...].astype(WIDE)).astype(LOW)
    delta = mul_nt(pick_ref[...], product)
    pack = pack_ref[...]
    block = block_ref[...]
    for pair in range(width // 128):
        lanes = slice(pair * 128, pair * 128 + 128)
        q, k, v, do = q_ref[:, lanes], k_ref[:, lanes], v_ref[:, lanes], do_ref[:, lanes]
        k_turned = (k * valid).T
        dv = dk = None
        dq_parts = []
        for half in range(2):
            head = 2 * pair + half
            pick = first if half == 0 else jnp.logical_not(first)
            q_one = jnp.where(pick, q, zero)
            do_one = jnp.where(pick, do, zero)
            weights = jnp.exp(mul_nt(k, q_one) - lse_ref[0, head : head + 1, :])
            grads = mul_nt(v, do_one)
            dscore = (weights * (grads - delta[head : head + 1, :])).astype(LOW)
            part_v = mul(weights.astype(LOW), do_one)
            part_k = mul(dscore, q_one)
            dv = part_v if dv is None else dv + part_v
            dk = part_k if dk is None else dk + part_k
            dq_parts.append(mul(k_turned[half * 64 : half * 64 + 64], dscore))
        dq = jnp.concatenate(dq_parts, axis=0).T
        dk = dk * valid_wide
        root = root_ref[:, lanes]
        for side, (grad, value) in enumerate(((dq, q), (dk, k))):
            value = value.astype(WIDE)
            inner = mul((grad * value).astype(LOW), block)
            total = jnp.sum(inner, axis=0, keepdims=True)
            if side == 0:
                head_total = total
            else:
                dhead_ref[0, :, lanes] = head_total + total
            factor = mul(pack, spread_ref[side, :, lanes])
            back = factor * (root * grad - value * (inner / root))
            back = rotate(back, cos_rep, up_rep, down_rep, -1)
            dproj_ref[:, side * width + pair * 128 : side * width + pair * 128 + 128] = back.astype(LOW)
        dproj_ref[:, 2 * width + pair * 128 : 2 * width + pair * 128 + 128] = (dv * valid_wide).astype(LOW)


def attend_back(line, q, k, v, o, do, lse, valid, pack, spread, root, pick, block, turns, images):
    tokens, width = q.shape
    seq = tokens // images
    heads = width // 64
    row = pl.BlockSpec((seq, width), lambda i: (i, 0))
    narrow = pl.BlockSpec((seq, 128), lambda i: (i, 0))
    return line.call(
        attend_back_kernel,
        (q, k, v, o, do, lse, valid, pack, spread, root, pick, block, *turns),
        [row, row, row, row, row, pl.BlockSpec((1, heads, seq), lambda i: (i, 0, 0)), narrow, narrow,
                  whole(spread.shape), whole(root.shape), whole(pick.shape), whole(block.shape),
                  narrow, narrow, narrow],
        grid=(images,),
        out_specs=[pl.BlockSpec((seq, 3 * width), lambda i: (i, 0)),
                   pl.BlockSpec((1, 1, width), lambda i: (i, 0, 0))],
        out_shape=[jax.ShapeDtypeStruct((tokens, 3 * width), LOW),
                   jax.ShapeDtypeStruct((images, 1, width), WIDE)],
        compiler_params=params(1),
        cost_estimate=cost(40 * tokens * seq * width, 20 << 20),
        name="attend_back",
    )


def input_kernel(even_ref, odd_ref, dproj_ref, x_ref, dmid_ref, scale_ref, *rest):
    pieces = rest[:16]
    out_ref, dscale_ref, w_ref, sems = rest[16:]

    @pl.when(pl.program_id(0) == 0)
    def _():
        fetch(load_qkv(even_ref, odd_ref, pieces, w_ref, sems))

    width = x_ref.shape[1]
    grad = mul_nt(dproj_ref[:, :width], w_ref[:, :width])
    grad += mul_nt(dproj_ref[:, width : 2 * width], w_ref[:, width : 2 * width])
    grad += mul_nt(dproj_ref[:, 2 * width :], w_ref[:, 2 * width :])
    x = x_ref[...].astype(WIDE)
    out_ref[...] = (dmid_ref[...] + norm_back(grad, x, scale_ref, dscale_ref)).astype(LOW)


def input_block(line, tables, dproj, x, dmid, scale, pieces, images):
    tokens, width = x.shape
    group = grouped(images)
    seq = tokens // images * group
    row = pl.BlockSpec((seq, width), lambda i: (i, 0))
    one = pl.BlockSpec((group, 1, width), lambda i: (i, 0, 0))
    return line.call(
        input_kernel,
        (*tables, dproj, x, dmid, scale, *pieces),
        [SMEM, SMEM, pl.BlockSpec((seq, 3 * width), lambda i: (i, 0)), row, row, one] + [ANY] * 16,
        grid=(images // group,),
        out_specs=[row, one],
        out_shape=[jax.ShapeDtypeStruct((tokens, width), LOW), jax.ShapeDtypeStruct((images, 1, width), WIDE)],
        scratch_shapes=[pltpu.VMEM((width, 3 * width), LOW), pltpu.SemaphoreType.DMA((2, 4, 8, 4))],
        compiler_params=params(1),
        cost_estimate=cost(6 * tokens * width * width, 24 << 20),
        name="input_grad",
    )


def result_kernel(even_ref, odd_ref, h0, h1, h2, mid_ref, *rest):
    pieces, out_ref, w_ref, sems = rest[:24], rest[24], rest[25], rest[26]
    width = mid_ref.shape[1]

    @pl.when(pl.program_id(0) == 0)
    def _():
        copies = []
        for part in range(3):
            ref = pieces[8 * part : 8 * part + 8]
            down = tuple(piece.at[:, :, 2 * width : 3 * width] for piece in ref)
            table_ref = odd_ref if part % 2 == 0 else even_ref
            copies += load_weight(table_ref, down, w_ref.at[part], sems.at[part])
        fetch(copies)

    total = mid_ref[...]
    for part, hid_ref in enumerate((h0, h1, h2)):
        total += mul(hid_ref[...], w_ref[part])
    out_ref[...] = total.astype(LOW)


def result_block(line, tables, hids, mid, pieces, images, place, places):
    tokens, width = mid.shape
    group = grouped(images)
    seq = tokens // images * group
    steps = images // group // places
    row = pl.BlockSpec((seq, width), lambda i: (place * steps + i, 0))
    return line.call(
        result_kernel,
        (*tables, *hids, mid, *[piece for part in pieces for piece in part]),
        [SMEM, SMEM, row, row, row, row] + [ANY] * 24,
        grid=(steps,),
        out_specs=pl.BlockSpec((seq, width), lambda i: (i, 0)),
        out_shape=jax.ShapeDtypeStruct((tokens // places, width), LOW),
        scratch_shapes=[pltpu.VMEM((3, width, width), LOW), pltpu.SemaphoreType.DMA((3, 8, 4))],
        compiler_params=params(1),
        cost_estimate=cost(6 * tokens * width * width, 20 << 20),
        name="result",
    )


def weight_kernel(lefts, table_ref, *refs):
    refs = list(refs)
    acts = [refs.pop(0) for _ in range(max(lefts) + 1)]
    grads = [refs.pop(0) for _ in lefts]
    outs = [refs.pop(0) for _ in range(8)]
    turned_ref, sems = refs
    rows = outs[0].shape[1]
    half = outs[0].shape[2]
    depth = turned_ref.shape[1]
    core = table_ref[32]
    step = pl.program_id(0)

    def copy(number, index):
        start = pl.multiple_of(index * 4 * rows, 16)
        return pltpu.make_async_copy(
            acts[number].at[pl.ds(start, 4 * rows)],
            turned_ref.at[number, index * 4 * rows : index * 4 * rows + 4 * rows],
            sems.at[number, index],
        )

    @pl.when(step == 0)
    def _():
        for number in range(len(acts)):
            for index in range(4):
                copy(number, index).start()

    for span, (left, grad_ref) in enumerate(zip(lefts, grads)):
        @pl.when(step == span)
        def _(span=span, left=left, grad_ref=grad_ref):
            if left not in lefts[:span]:
                for index in range(4):
                    copy(left, index).wait()
            for side in range(2):
                place = pl.multiple_of((core if side == 0 else 1 - core) * half, half)
                grad = grad_ref[:, pl.ds(place, half)]
                for piece in range(4):
                    parts = []
                    for index in range(4):
                        start = table_ref[side * 16 + piece * 4 + index] * rows
                        parts.append(turned_ref[left, pl.ds(pl.multiple_of(start, 16), rows), :])
                    total = mul(jnp.concatenate(parts, axis=0), grad)
                    out = outs[4 * side + piece]
                    out[...] = total.reshape(out.shape).astype(LOW)


def weight_halves(line, table, acts, spans):
    depth, tokens = acts[0].shape
    rows = depth // 16
    wide = spans[0][1].shape[1] // spans[0][3]
    half = wide // 2
    count = len(spans)

    def grad_spec(number, span):
        return pl.BlockSpec((tokens, wide), lambda m, t: (0, span))

    tile = pl.BlockSpec((4, rows, half), lambda m, t: (0, 0, m))
    shape = jax.ShapeDtypeStruct((4, rows, count * half), LOW)
    size = 2 * (tokens * (len(acts) * depth + count * wide) + depth * count * wide)
    outs = line.call(
        functools.partial(weight_kernel, [span[0] for span in spans]),
        (table, *acts, *[span[1] for span in spans]),
        [ANY for _ in acts] + [grad_spec(number, span[2]) for number, span in enumerate(spans)],
        prefetch=1,
        grid=(count,),
        out_specs=[tile] * 8,
        out_shape=[shape] * 8,
        scratch_shapes=[
            pltpu.VMEM((len(acts), depth, tokens), LOW), pltpu.SemaphoreType.DMA((len(acts), 4))
        ],
        compiler_params=params(1),
        cost_estimate=cost(2 * tokens * depth * count * wide, size),
        name="weight_grad",
    )
    return outs[:4], outs[4:]


def adam(weight, first, second, gradient, factor, rate, decay):
    clipped = gradient * factor
    new_first = BETA_ONE * first + (1.0 - BETA_ONE) * clipped
    new_second = BETA_TWO * second + (1.0 - BETA_TWO) * clipped * clipped
    denominator = jnp.sqrt(new_second / (1.0 - BETA_TWO**STEP)) + ADAM_EPS
    new_weight = (
        weight * (1.0 - rate * decay) - rate * (new_first / (1.0 - BETA_ONE**STEP)) / denominator
    )
    return (new_weight, new_first, new_second)


def adam_kernel(core_ref, total_ref, *refs):
    refs = list(refs)
    ada, qkv, out, up, down, scale = ([refs.pop(0) for _ in range(3)] for _ in range(6))
    ada_grad, head_grad = refs.pop(0), refs.pop(0)
    mines = [refs.pop(0) for _ in range(4)]
    others = [refs.pop(0) for _ in range(4)]
    norm_ref = refs.pop(0)
    new_ada, new_qkv, new_out, new_up, new_down, new_scale = ([refs.pop(0) for _ in range(3)] for _ in range(6))
    own_first = core_ref[0] == 0
    head = head_grad[...]
    total = total_ref[0:1, 0:1] + jnp.sum(head * head, axis=1, keepdims=True)
    norm = jnp.sqrt(total)
    factor = jnp.minimum(1.0, CLIP / (norm + 1e-06))

    def update(news, olds, at, gradient, rate, decay):
        weight, first, second = (ref[at] for ref in olds)
        for ref, value in zip(news, adam(weight, first, second, gradient, factor, rate, decay)):
            ref[at] = value

    @pl.when(pl.program_id(0) == 0)
    def _():
        norm_ref[...] = jnp.broadcast_to(norm, norm_ref.shape)
        update(new_scale, scale, (slice(None),) * 2, head, SCALE_RATE, 0.0)
        for index in range(ada_grad.shape[0]):
            update(new_ada, ada, (index,), ada_grad[index], RATE, DECAY)

    def columns(number, span):
        size = mines[0].shape[1] // 3
        mine = mines[number][:, span * size : span * size + size].astype(WIDE)
        other = others[number][:, span * size : span * size + size].astype(WIDE)
        return jnp.where(own_first, mine, other), jnp.where(own_first, other, mine)

    def by_halves(news, olds, number, spans, rate):
        for place, span in enumerate(spans):
            for half, gradient in enumerate(columns(number, span)):
                size = gradient.shape[1]
                start = (2 * place + half) * size
                update(news, olds, (slice(None), slice(start, start + size)), gradient, rate, DECAY)

    by_halves(new_qkv, qkv, 3, (0, 1, 2), RATE)
    by_halves(new_out, out, 2, (3,), OUTPUT_RATE)
    for part in range(3):
        for half, gradient in enumerate(columns(part, 2)):
            size = gradient.shape[1]
            update(new_down, down, (part, slice(None), slice(half * size, half * size + size)), gradient, RATE, DECAY)
    low = lax.broadcasted_iota(jnp.int32, (up[0].shape[0], 128), 1) < 64
    for span in range(2):
        parts = [columns(part, span) for part in range(3)]
        size = parts[0][0].shape[1]
        for half in range(2):
            for lane in range(0, size, 128):
                one, two, three = (parts[part][half][:, lane : lane + 128] for part in range(3))
                turned = pltpu.roll(two, 64, 1)
                start = 3 * ((2 * span + half) * size + lane)
                pieces = (jnp.where(low, one, turned), jnp.where(low, three, one), jnp.where(low, turned, three))
                for number, gradient in enumerate(pieces):
                    at = (slice(None), slice(start + 128 * number, start + 128 * number + 128))
                    update(new_up, up, at, gradient, RATE, DECAY)


def adam_all(line, core, total, ada, qkv, out, up, down, scale, ada_grad, head_grad, mines, others):
    steps = 4
    args = [core[None], total]
    in_specs = [SMEM, whole(total.shape)]
    out_specs = [whole(total.shape)]
    out_shape = [jax.ShapeDtypeStruct(total.shape, WIDE)]

    def by_rows(array):
        shape = array.shape[:-2] + (array.shape[-2] // steps, array.shape[-1])
        lead = (0,) * (array.ndim - 2)
        return pl.BlockSpec(shape, lambda i: lead + (i, 0))

    for group, cut in ((ada, False), (qkv, True), (out, True), (up, True), (down, True), (scale, False)):
        for array in group:
            spec = by_rows(array) if cut else whole(array.shape)
            args.append(array)
            in_specs.append(spec)
            out_specs.append(spec)
            out_shape.append(jax.ShapeDtypeStruct(array.shape, WIDE))
    args += [ada_grad, head_grad, *mines, *others]
    in_specs += [whole(ada_grad.shape), whole(head_grad.shape)] + [by_rows(m) for m in (*mines, *others)]
    return line.call(
        adam_kernel,
        args,
        in_specs,
        grid=(steps,),
        out_specs=out_specs,
        out_shape=out_shape,
        compiler_params=params(1),
        cost_estimate=cost(0, 30 << 20),
        name="adamw",
    )


def turn_kernel(shapes_ref, rates_ref, cos_ref, up_ref, down_ref, valid_ref):
    image = pl.program_id(0)
    height, width = shapes_ref[image, 0], shapes_ref[image, 1]
    shape = cos_ref.shape
    slot = lax.broadcasted_iota(jnp.int32, shape, 0)
    place = slot.astype(WIDE)
    wide = width.astype(WIDE)
    row = jnp.floor((place + 0.5) / wide)
    angle = row * rates_ref[0:1, :] + (place - row * wide) * rates_ref[1:2, :]
    lane = lax.broadcasted_iota(jnp.int32, shape, 1) % 64
    cosine, sine = jnp.cos(angle), jnp.sin(angle)
    cos_ref[...] = jnp.where(lane < 32, cosine, 1.0)
    up_ref[...] = jnp.where(lane < 16, -sine, 0.0)
    down_ref[...] = jnp.where((lane >= 16) & (lane < 32), sine, 0.0)
    valid_ref[...] = jnp.where(slot < height * width, 1.0, 0.0).astype(LOW)


def turn_tables(line, shapes, seq_len, head_dim):
    images = shapes.shape[0]
    count = head_dim // 8
    frequency = ROPE_BASE ** (-jnp.arange(count, dtype=WIDE) / count)
    none = jnp.zeros((count,), WIDE)
    blank = jnp.zeros((head_dim // 2,), WIDE)
    rates = jnp.stack(
        [
            jnp.concatenate([frequency, none, frequency, none, blank] * 2),
            jnp.concatenate([none, frequency, none, frequency, blank] * 2),
        ]
    )
    block = pl.BlockSpec((seq_len, 128), lambda i: (i, 0))
    wide = jax.ShapeDtypeStruct((images * seq_len, 128), WIDE)
    *turns, valid = line.call(
        turn_kernel,
        (shapes, rates),
        [SMEM, whole(rates.shape)],
        grid=(images,),
        out_specs=[block] * 4,
        out_shape=[wide, wide, wide, jax.ShapeDtypeStruct(wide.shape, LOW)],
        compiler_params=params(1),
        cost_estimate=cost(0, 2 << 20),
        name="turns",
    )
    return tuple(turns), valid


def head_matrices(width, head_dim):
    heads = width // head_dim
    owner = np.arange(width) // head_dim
    sums = np.zeros((2, width, 128), np.float32)
    spread = np.zeros((2, 128, width), np.float32)
    for side in range(2):
        for copy in range(2):
            sums[side, np.arange(width), side * heads + copy * 2 * heads + owner] = 1.0
            spread[side, side * heads + copy * 2 * heads + owner, np.arange(width)] = 1.0
    pick = np.zeros((heads, width), np.float32)
    pick[owner, np.arange(width)] = 1.0
    block = np.kron(np.eye(128 // head_dim), np.ones((head_dim, head_dim)))
    return tuple(jnp.asarray(m, LOW) for m in (sums, spread, pick, block))


def finish_wide(net, ada, qkv, out, up, down, scale, grad_ada, head_grad, mines, others):
    def columns(number, span):
        size = mines[0].shape[1] // 3
        mine = mines[number][:, span * size : span * size + size]
        other = others[number][:, span * size : span * size + size]
        pair = [jnp.where(net.core == 0, mine, other), jnp.where(net.core == 0, other, mine)]
        return jnp.concatenate(pair, axis=1).astype(WIDE)

    grad_up = [
        jnp.concatenate([columns(part, span) for span in range(2)], axis=1).reshape(-1, 2, 16, 64)
        for part in range(3)
    ]
    gradients = [
        jnp.concatenate([columns(3, span) for span in range(3)], axis=1),
        columns(2, 3),
        jnp.stack(grad_up, axis=3).reshape(-1, up[0].shape[1]),
        jnp.concatenate([columns(part, 2) for part in range(3)], axis=0),
    ]
    gradients = [grad_ada] + [net.split_sub(gradient) for gradient in gradients]
    total = lax.psum(sum(jnp.sum(gradient * gradient) for gradient in gradients), "fsdp")
    head_grad = head_grad[0]
    norm = jnp.sqrt(total + jnp.sum(head_grad * head_grad))
    factor = jnp.minimum(1.0, CLIP / (norm + 1e-06))
    rates = (RATE, RATE, OUTPUT_RATE, RATE, RATE)
    news = [norm]
    for group, gradient, rate in zip((ada, qkv, out, up, down), gradients, rates):
        news += adam(*group, gradient, factor, rate, DECAY)
    news += adam(*scale, head_grad, factor, SCALE_RATE, 0.0)
    return tuple(news)


def local(
    tokens,
    condition,
    shapes,
    cotangent,
    ada_weight,
    ada_first,
    ada_second,
    qkv_weight,
    qkv_first,
    qkv_second,
    out_weight,
    out_first,
    out_second,
    up_weight,
    up_first,
    up_second,
    down_weight,
    down_first,
    down_second,
    head_scale,
    scale_first,
    scale_second,
    *,
    dp_size,
    fsdp_size,
):
    net = Net(fsdp_size, dp_size)
    line = Line()
    core = net.core
    images = shapes.shape[0]
    width = tokens.shape[1]
    seq_len = tokens.shape[0] // images
    head_count = head_scale.shape[0]
    head_dim = width // head_count
    small = net.sub == 1
    even, odd = net.tables

    ada_joined = net.join_sub(ada_weight.transpose(1, 0, 2)).transpose(1, 0, 2) if net.sub > 1 else ada_weight
    half_qk, half_vo = head_parts(
        line, core, net.join_sub(qkv_weight), net.join_sub(out_weight), ada_joined
    )
    get_qk = Gather(net, line, 0, half_qk)
    get_vo = Gather(net, line, 1, half_vo)
    down_joined = net.join_sub(down_weight).reshape(3, -1, width)
    halves = cut_parts(line, core, net.join_sub(up_weight), down_joined)
    turns, valid = turn_tables(line, shapes, seq_len, head_dim)
    sums, spread, pick, block = head_matrices(width, head_dim)
    root = jnp.repeat(jnp.sqrt(head_scale), head_dim)[None]

    get_qk.second()
    get_vo.second()
    get_qk.third()
    get_vo.third()
    get_mlp = [Gather(net, line, 1, halves[0])]
    get_qk.fourth()
    get_qk.fifth()
    get_mlp[0].second()
    get_vo.fourth()
    get_vo.fifth()
    get_qk.finish()
    get_mlp[0].third()
    get_vo.finish()
    get_mlp.append(Gather(net, line, 0, halves[1]))

    qkv_pieces = get_qk.pieces + get_vo.pieces
    act_one, q, k, v, pack, scale_one, scale_two = front(
        line, net.tables, tokens, condition, qkv_pieces, sums, spread, root, turns, images
    )
    get_mlp[0].fourth()
    get_mlp[0].fifth()
    get_mlp[1].second()
    o, o_turned, lse = attend(line, q, k, v, valid, images)
    get_mlp[0].finish()
    get_mlp[1].third()
    get_mlp.append(Gather(net, line, 1, halves[2]))
    mid, act_two, act_two_turned = middle_block(
        line, odd, o, tokens, scale_two, get_vo.pieces, images
    )
    get_mlp[1].fourth()
    get_mlp[1].fifth()
    get_mlp[2].second()

    def put(parity, acts, spans):
        return Scatter(net, line, parity, *weight_halves(line, net.tables[parity], acts, spans))

    def mlp_spans(hid_turned, dgu):
        return ((act_two_turned, hid_turned), ((0, dgu, 0, 2), (0, dgu, 1, 2), (1, cotangent, 0, 1)))

    hid0, dgu0, turned0, acc = geglu_part(line, odd, act_two, cotangent, get_mlp[0].pieces, images)
    get_mlp[1].finish()
    get_mlp[2].third()
    put0 = put(0, *mlp_spans(turned0, dgu0))
    hid1, dgu1, turned1, acc = geglu_part(
        line, even, act_two, cotangent, get_mlp[1].pieces, images, acc
    )
    get_mlp[2].fourth()
    get_mlp[2].fifth()
    put0.first()
    put1 = put(1, *mlp_spans(turned1, dgu1))
    get_mlp[2].finish()
    put0.second()
    hid2, dgu2, turned2, dmid, db, do, dscale_two = geglu_part(
        line, odd, act_two, cotangent, get_mlp[2].pieces, images, acc,
        (mid, scale_two, get_vo.pieces),
    )
    put0.third()
    put1.first()
    acts2, spans2 = mlp_spans(turned2, dgu2)
    put2 = put(0, acts2 + (o_turned,), spans2 + ((2, db, 0, 1),))
    put0.fourth()
    put1.second()
    dproj, dhead = attend_back(
        line, q, k, v, o, do, lse, valid, pack, spread, root, pick, block, turns, images
    )
    put0.finish()
    put1.third()
    put2.first()
    put_qkv = put(1, (act_one,), tuple((0, dproj, span, 3) for span in range(3)))
    put1.fourth()
    put2.second()

    def result(place):
        return result_block(
            line, net.tables, (hid0, hid1, hid2), mid, [get.pieces for get in get_mlp], images,
            place, places,
        )

    places = 2 if images % (2 * grouped(images)) == 0 else 1
    outputs = [result(0)]
    put1.finish()
    put_qkv.first()
    put2.third()
    input_grad, dscale_one = input_block(
        line, net.tables, dproj, tokens, dmid, scale_one, qkv_pieces, images
    )
    put_qkv.second()
    put2.fourth()

    dhead = jnp.sum(dhead.reshape(images, head_count, head_dim)[:, :, 0], axis=0) / (2.0 * head_scale)
    rows = jnp.concatenate([dscale_one[:, 0], dscale_two[:, 0], condition.astype(WIDE)], axis=1)
    if small:
        dhead = jnp.pad(dhead[None], ((0, 7), (0, 128 - head_count)))
        rows = jnp.concatenate([rows.reshape(1, -1, 128), dhead[None]], axis=1)
        late = SmallGather(net, line, rows)
    if places > 1:
        outputs.append(result(1))
    block_output = jnp.concatenate(outputs, axis=0)
    if small:
        late.second()
        put_qkv.third()
        put2.finish()
        late.step()
        rows = late.held[:, :-8].reshape(16 * images, -1)
        head_grad = jnp.sum(late.held[:, -8, :head_count], axis=0)
    else:
        put_qkv.third()
        put2.finish()
        rows = lax.all_gather(rows, "fsdp", axis=0, tiled=True)
        head_grad = lax.psum(dhead, "fsdp")
    own_rows = ada_weight.shape[1]
    own_start = 2 * width + lax.axis_index("fsdp") * own_rows
    cond_own = lax.dynamic_slice_in_dim(rows, own_start, own_rows, axis=1)
    grad_ada = jnp.dot(cond_own.T, rows[:, : 2 * width], precision=PRECISE)
    head_grad = jnp.pad(head_grad, (0, width - head_count))[None]
    grad_small = jnp.concatenate([grad_ada.reshape(-1, width), head_grad])
    grad_small = grad_small + net.swap(grad_small)
    grad_ada = grad_small[:-1].reshape(own_rows, 2, width).transpose(1, 0, 2)
    head_grad = grad_small[-1:, :head_count]

    put_qkv.fourth()
    put_qkv.finish()
    puts = (put0, put1, put2, put_qkv)
    mines = tuple(each.mine for each in puts)
    others = tuple(each.other for each in puts)
    ada = (ada_weight, ada_first, ada_second)
    qkv = (qkv_weight, qkv_first, qkv_second)
    out = (out_weight, out_first, out_second)
    up = (up_weight, up_first, up_second)
    down = (down_weight, down_first, down_second)
    scale = (head_scale, scale_first, scale_second)
    if not small:
        return (block_output, input_grad) + finish_wide(
            net, ada, qkv, out, up, down, scale, grad_ada, head_grad, mines, others
        )
    local_squares = sum(each.square for each in puts) + 0.5 * jnp.sum(grad_ada * grad_ada)
    total = net.total(local_squares)
    rows = down_weight.shape[0] // 3
    news = adam_all(
        line, core, total, ada, qkv, out, up,
        tuple(array.reshape(3, rows, width) for array in down),
        tuple(array[None] for array in scale), grad_ada, head_grad, mines, others,
    )
    return (
        block_output,
        input_grad,
        news[0][0, 0],
        *news[1:13],
        *[array.reshape(down_weight.shape) for array in news[13:16]],
        *[array[0] for array in news[16:19]],
    )


def solution(mesh):
    tokens = P(("dp", "fsdp"), None)
    ada = P(None, "fsdp", None)
    rows = P("fsdp", None)
    return jax.shard_map(
        functools.partial(local, dp_size=mesh.shape["dp"], fsdp_size=mesh.shape["fsdp"]),
        mesh=mesh,
        in_specs=(tokens,) * 4 + (ada,) * 3 + (rows,) * 12 + (P(),) * 3,
        out_specs=(tokens, tokens, P()) + (ada,) * 3 + (rows,) * 12 + (P(),) * 3,
        check_vma=False,
    )
```

```python
import functools
import math

import jax
import jax.numpy as jnp
import numpy as np
from jax import lax
from jax.experimental import pallas as pl
from jax.experimental.pallas import tpu as pltpu
from jax.sharding import PartitionSpec as P

FF = 3072
STEP = 10


NORM_EPS = 1e-06
COSINE_EPS = 1e-06
ROPE_BASE = 100.0
CLIP = 1.0
RATE = 0.02
OUTPUT_RATE = 0.2
SCALE_RATE = 8.0
BETA_ONE = 0.9
BETA_TWO = 0.95
ADAM_EPS = 1e-08
DECAY = 0.01
PRECISE = lax.Precision.HIGHEST
AXES = ("dp", "fsdp")
LOW = jnp.bfloat16
WIDE = jnp.float32


ORDERS = (
    ((8, 4, 1, 2), (2, 8, 4, 1)),
    ((8, 4, 2, 1), (1, 8, 4, 2)),
)


class Net:
    def __init__(self, size, dp_size):
        self.size = size
        self.dp_size = dp_size
        self.sub = size // 16
        self.core = lax.axis_index("dp")
        self.me = lax.axis_index("fsdp") // self.sub
        self.tables = tuple(self.table(order) for order in ORDERS)

    def exchange(self, array, bits):
        pairs = []
        for core in range(self.dp_size):
            for place in range(self.size):
                target = place ^ (bits[core % 2] * self.sub)
                pairs.append((core * self.size + place, core * self.size + target))
        return lax.ppermute(array, AXES, pairs)

    def cross(self, array, parity, stage):
        order = ORDERS[parity]
        return self.exchange(array, (order[0][stage], order[1][stage]))

    def swap(self, array):
        pairs = []
        for core in range(self.dp_size):
            for place in range(self.size):
                pairs.append((core * self.size + place, (core ^ 1) * self.size + place))
        return lax.ppermute(array, AXES, pairs)

    def table(self, order):
        index = lax.iota(jnp.int32, 32)
        side = self.core ^ (index >> 4)
        value = jnp.full((32,), self.me, jnp.int32)
        for stage in range(4):
            bit = jnp.where(side == 0, order[0][stage], order[1][stage])
            value = value ^ ((index >> stage & 1) * bit)
        return jnp.concatenate([value, self.core[None]]).astype(jnp.int32)

    def groups(self):
        return [list(range(g * self.sub, (g + 1) * self.sub)) for g in range(16)]

    def join_sub(self, shard):
        if self.sub == 1:
            return shard
        return lax.all_gather(shard, "fsdp", axis=0, tiled=True, axis_index_groups=self.groups())

    def split_sub(self, gradient):
        gathered = lax.all_gather(gradient, "fsdp", axis=0, axis_index_groups=self.groups())
        rows = gradient.shape[0] // self.sub
        place = lax.axis_index("fsdp") % self.sub
        return lax.dynamic_slice_in_dim(jnp.sum(gathered, axis=0), place * rows, rows, axis=0)

    def total(self, value):
        for bits in ((1, 2, 3), (4, 8, 12)):
            value = value + sum(self.exchange(value, (bit, bit)) for bit in bits)
        return value + self.swap(value)


TIMES = {
    "front": 18,
    "attend": 13,
    "middle": 10,
    "geglu_part": 20,
    "weight_grad": 14,
    "attend_back": 30,
    "input_grad": 12,
    "result": 11,
}
WORK = 1150000000


class Line:
    def __init__(self):
        self.last = None
        self.waits = []

    def call(self, kernel, args, in_specs, prefetch=0, into=None, **kwargs):
        deps = []
        if self.last is not None:
            token = self.last
            if self.waits:
                token = lax.optimization_barrier((token, *self.waits))[0]
            deps = [token]
        self.waits = []
        count = len(deps)
        if into is not None:
            args, in_specs = (*args, into), (*in_specs, ANY)
            kwargs["input_output_aliases"] = {count + len(args) - 1: 0}
            inner = kernel

            def kernel(*refs):
                inner(*refs[: len(args) - 1], *refs[len(args) :])

        one = not isinstance(kwargs["out_shape"], (list, tuple))
        shapes = [kwargs["out_shape"]] if one else list(kwargs["out_shape"])
        specs = kwargs["out_specs"]
        specs = [specs] if not isinstance(specs, (list, tuple)) else list(specs)
        place = prefetch + len(in_specs) + len(shapes)

        def body(*refs):
            refs = refs[:prefetch] + refs[prefetch + count :]
            refs[place][...] = jnp.zeros((8, 128), WIDE)
            kernel(*refs[:place], *refs[place + 1 :])

        in_specs = [ANY] * count + list(in_specs)
        out_specs = specs + [whole((8, 128)) if "grid" in kwargs else VMEM]
        del kwargs["out_specs"]
        kwargs["out_shape"] = shapes + [jax.ShapeDtypeStruct((8, 128), WIDE)]
        if prefetch:
            kwargs["grid_spec"] = pltpu.PrefetchScalarGridSpec(
                num_scalar_prefetch=prefetch,
                grid=kwargs.pop("grid"),
                in_specs=in_specs,
                out_specs=out_specs,
                scratch_shapes=kwargs.pop("scratch_shapes", []),
            )
        else:
            kwargs["in_specs"] = in_specs
            kwargs["out_specs"] = out_specs
        if kwargs["name"] in TIMES:
            kwargs["cost_estimate"] = cost(TIMES[kwargs["name"]] * WORK, 1 << 20)
        *outs, self.last = pl.pallas_call(body, **kwargs)(*args[:prefetch], *deps, *args[prefetch:])
        return outs[0] if one else outs

    def pin(self, array):
        if self.last is not None:
            array, _ = lax.optimization_barrier((array, self.last))
        self.waits.append(array)
        return array


class Gather:
    def __init__(self, net, line, parity, half):
        self.net, self.line, self.parity = net, line, parity
        self.held = line.pin(half)
        self.got = net.cross(self.held, parity, 0)

    def wait(self):
        self.got = self.line.pin(self.got)

    def second(self):
        self.wait()
        self.held = join(self.line, self.held, self.got)
        self.got = self.net.cross(self.held, self.parity, 1)

    def third(self):
        self.wait()
        self.held = join(self.line, self.held, self.got)
        self.near = self.net.cross(self.held, self.parity, 2)
        self.far = self.net.cross(self.held, self.parity, 3)
        self.swapped = [self.net.swap(self.held)]

    def wait_near(self):
        self.near, self.far = self.line.pin(self.near), self.line.pin(self.far)

    def wait_last(self):
        self.last = self.line.pin(self.last)

    def fourth(self):
        self.wait_near()
        self.swapped = [self.line.pin(array) for array in self.swapped]
        self.last = self.net.cross(self.near, self.parity, 3)
        self.swapped += [self.net.swap(self.near), self.net.swap(self.far)]

    def finish(self):
        self.last = self.line.pin(self.last)
        self.swapped = [self.line.pin(array) for array in self.swapped]
        self.swapped.append(self.net.swap(self.last))
        self.pieces = (self.held, self.near, self.far, self.last, *self.swapped)


class Scatter:
    def __init__(self, net, line, parity, keep, send):
        self.net, self.line, self.parity = net, line, parity
        self.keep, self.send = keep, send
        self.part = [None] * 4

    def swap(self, number):
        self.part[number] = self.net.swap(self.line.pin(self.send[number]))

    def start(self):
        self.swap(3)
        self.swap(2)

    def wait(self):
        self.got = self.line.pin(self.got)

    def first(self):
        two, three = fold_pair(self.line, self.keep[2:], self.part[2:])
        self.got = self.net.cross(three, self.parity, 3)
        self.late = self.net.cross(two, self.parity, 3)
        self.swap(1)

    def second(self):
        self.wait()
        (held,) = fold(self.line, self.keep[1], (self.part[1], self.got), 1)
        self.got = self.net.cross(held, self.parity, 2)
        self.swap(0)

    def third(self):
        self.wait()
        self.late = self.line.pin(self.late)
        self.held, send = fold(self.line, self.keep[0], (self.part[0], self.late, self.got), 2)
        self.got = self.net.cross(send, self.parity, 1)

    def fourth(self):
        self.wait()
        self.held, send = fold(self.line, self.held, (self.got,), 2)
        self.got = self.net.cross(send, self.parity, 0)

    def finish(self):
        self.wait()
        self.mine, self.square = fold_last(self.line, self.held[0], self.got[0])
        self.other = self.net.swap(self.mine)


class SmallGather:
    def __init__(self, net, line, rows):
        self.net, self.line = net, line
        self.held = line.pin(rows)
        self.got = [net.swap(self.held)]

    def step(self, bits=()):
        got = [self.line.pin(array) for array in self.got]
        self.held = jnp.concatenate([self.held, *got], axis=0)
        self.got = [self.net.exchange(self.held, (bit, bit)) for bit in bits]


ANY = pl.BlockSpec(memory_space=pl.ANY)
SMEM = pl.BlockSpec(memory_space=pltpu.SMEM)
VMEM = pl.BlockSpec(memory_space=pltpu.VMEM)
NT = (((1,), (1,)), ((), ()))
TN = (((0,), (0,)), ((), ()))
VMEM_LIMIT = 56 * 1024 * 1024
SMALL_LIMIT = 16 * 1024 * 1024


def load_weight(table_ref, pieces, full_ref, sems):
    core = table_ref[32]
    rows = pieces[0].shape[1]
    copies = []
    for number, piece in enumerate(pieces):
        side = core if number < 4 else 1 - core
        for index in range(4):
            start = pl.multiple_of(table_ref[number * 4 + index] * (2 * rows) + side * rows, 16)
            copies.append(
                pltpu.make_async_copy(
                    piece.at[index], full_ref.at[pl.ds(start, rows)], sems.at[number, index]
                )
            )
    return copies


def part_of(pieces, first, size):
    return tuple(piece.at[:, :, first : first + size] for piece in pieces)


def fetch(copies):
    for copy in copies:
        copy.start()
    for copy in copies:
        copy.wait()


SEMS = pltpu.SemaphoreType.DMA((8, 4))


def params(dims):
    return pltpu.CompilerParams(
        dimension_semantics=("arbitrary",) * dims, vmem_limit_bytes=VMEM_LIMIT
    )


def cost(flops, size):
    return pl.CostEstimate(flops=flops, bytes_accessed=size, transcendentals=0)


def mul(a, b):
    return jnp.dot(a, b, preferred_element_type=WIDE)


def mul_nt(a, b):
    return lax.dot_general(a, b, NT, preferred_element_type=WIDE)


def mul_tn(a, b):
    return lax.dot_general(a, b, TN, preferred_element_type=WIDE)


def whole(shape):
    return pl.BlockSpec(shape, lambda *_: (0,) * len(shape))


def turned_block(width, seq):
    return pl.BlockSpec((width, seq), lambda i: (0, i))


def turned_shape(width, tokens):
    return jax.ShapeDtypeStruct((width, tokens), LOW)


def grouped(images):
    return 2 if images % 2 == 0 else 1


def scaled(values, scale_ref):
    count = scale_ref.shape[0]
    rows = values.shape[0] // count
    parts = [values[i * rows : i * rows + rows] * scale_ref[i] for i in range(count)]
    return parts[0] if count == 1 else jnp.concatenate(parts, axis=0)


def norm_back(grad, values, scale_ref, dscale_ref):
    inverse = lax.rsqrt(jnp.mean(values * values, axis=-1, keepdims=True) + NORM_EPS)
    normed = values * inverse
    product = grad * normed
    count = scale_ref.shape[0]
    rows = values.shape[0] // count
    for i in range(count):
        dscale_ref[i] = jnp.sum(product[i * rows : i * rows + rows], axis=0, keepdims=True)
    grad = scaled(grad, scale_ref)
    inner = jnp.mean(grad * normed, axis=-1, keepdims=True)
    return inverse * (grad - normed * inner)


def rotate(values, cos_rep, up_rep, down_rep, sign):
    ahead = pltpu.roll(values, values.shape[-1] - 16, 1)
    behind = pltpu.roll(values, 16, 1)
    turned = ahead * up_rep + behind * down_rep
    return values * cos_rep + (turned if sign > 0 else -turned)


def join_kernel(a_ref, b_ref, out_ref, sems):
    count = a_ref.shape[0]
    fetch(
        [
            pltpu.make_async_copy(a_ref, out_ref.at[:count], sems.at[0]),
            pltpu.make_async_copy(b_ref, out_ref.at[count:], sems.at[1]),
        ]
    )


def join(line, a, b):
    shape = (2 * a.shape[0],) + a.shape[1:]
    return line.call(
        join_kernel,
        (a, b),
        [ANY, ANY],
        out_specs=VMEM,
        out_shape=jax.ShapeDtypeStruct(shape, a.dtype),
        scratch_shapes=[pltpu.SemaphoreType.DMA((2,))],
        compiler_params=pltpu.CompilerParams(vmem_limit_bytes=SMALL_LIMIT),
        cost_estimate=cost(0, 4 * math.prod(shape)),
        name="join",
    )


def fold_kernel(count, held_ref, *refs):
    outs = refs[count:]
    total = held_ref[...].astype(WIDE)
    for ref in refs[:count]:
        total += ref[...].astype(WIDE)
    size = outs[0].shape[0]
    for number, out in enumerate(outs):
        out[...] = total[number * size : number * size + size].astype(out.dtype)


def fold(line, held, others, parts):
    shape = (held.shape[0] // parts,) + held.shape[1:]
    return line.call(
        functools.partial(fold_kernel, len(others)),
        (held, *others),
        [VMEM] * (1 + len(others)),
        out_specs=[VMEM] * parts,
        out_shape=[jax.ShapeDtypeStruct(shape, held.dtype)] * parts,
        compiler_params=pltpu.CompilerParams(vmem_limit_bytes=SMALL_LIMIT),
        cost_estimate=cost(0, 2 * math.prod(held.shape) * (2 + len(others))),
        name="fold",
    )


def fold_pair_kernel(a_ref, b_ref, c_ref, d_ref, first_ref, second_ref):
    first_ref[...] = (a_ref[...].astype(WIDE) + c_ref[...].astype(WIDE)).astype(LOW)
    second_ref[...] = (b_ref[...].astype(WIDE) + d_ref[...].astype(WIDE)).astype(LOW)


def fold_pair(line, held, others):
    shape = jax.ShapeDtypeStruct(held[0].shape, LOW)
    return line.call(
        fold_pair_kernel,
        (*held, *others),
        [VMEM] * 4,
        out_specs=[VMEM] * 2,
        out_shape=[shape] * 2,
        compiler_params=pltpu.CompilerParams(vmem_limit_bytes=SMALL_LIMIT),
        cost_estimate=cost(0, 12 * math.prod(shape.shape)),
        name="fold_pair",
    )


def fold_last_kernel(held_ref, other_ref, out_ref, square_ref):
    total = (held_ref[...].astype(WIDE) + other_ref[...].astype(WIDE)).astype(LOW)
    out_ref[...] = total
    total = total.astype(WIDE)
    sums = jnp.sum(jnp.sum(total * total, axis=0, keepdims=True), axis=1, keepdims=True)
    square_ref[...] = jnp.broadcast_to(sums, square_ref.shape)


def fold_last(line, held, other):
    return line.call(
        fold_last_kernel,
        (held, other),
        [VMEM, VMEM],
        out_specs=[VMEM, VMEM],
        out_shape=[jax.ShapeDtypeStruct(held.shape, LOW), jax.ShapeDtypeStruct((1, 128), WIDE)],
        compiler_params=pltpu.CompilerParams(vmem_limit_bytes=SMALL_LIMIT),
        cost_estimate=cost(0, 6 * math.prod(held.shape)),
        name="fold_last",
    )


def head_kernel(core_ref, qkv_ref, out_ref, ada_ref, *outs):
    rows, size = qkv_ref.shape[0], ada_ref.shape[2]
    for number, out in enumerate(outs):
        for block in range(4):
            at = (4 * number + block) * size
            past = at - qkv_ref.shape[1]
            values = qkv_ref[:, at : at + size] if past < 0 else out_ref[:, past : past + size]
            out[0, block * rows : block * rows + rows, :] = values.astype(LOW)
        out[0, 4 * rows :, :] = ada_ref[number].astype(LOW)


def head_parts(line, core, qkv, out, ada):
    rows, width = qkv.shape[0] // 2, out.shape[1]
    size = width // 2
    shape = (1, 4 * rows + ada.shape[1], size)
    return line.call(
        head_kernel,
        (core[None], qkv, out, ada),
        [pl.BlockSpec((rows, 3 * width), lambda i, c: (c[0], 0)),
         pl.BlockSpec((rows, width), lambda i, c: (c[0], 0)),
         pl.BlockSpec((2, ada.shape[1], size), lambda i, c: (0, 0, c[0]))],
        prefetch=1,
        grid=(1,),
        out_specs=[whole(shape)] * 2,
        out_shape=[jax.ShapeDtypeStruct(shape, LOW)] * 2,
        compiler_params=params(1),
        cost_estimate=cost(0, 2 << 20),
        name="head_parts",
    )


def load_head(table_ref, pieces, first, full_ref, sems, ada_ref=None, ada_sems=None):
    core = table_ref[32]
    size = pieces[0].shape[2]
    ada_rows = 0 if ada_ref is None else ada_ref.shape[0] // 16
    copies = []
    for number, piece in enumerate(pieces):
        side = core if number < 4 else 1 - core
        for index in range(4):
            owner = table_ref[number * 4 + index]
            start = pl.multiple_of(owner * 64 + side * 32, 16)
            for block in range(full_ref.shape[1] // size):
                copies.append(
                    pltpu.make_async_copy(
                        piece.at[index, (first + block) * 32 : (first + block) * 32 + 32],
                        full_ref.at[pl.ds(start, 32), block * size : block * size + size],
                        sems.at[block, number, index],
                    )
                )
            if ada_ref is not None:
                start = pl.multiple_of(owner * ada_rows, 16)
                column = pl.multiple_of(side * size, 128)
                copies.append(
                    pltpu.make_async_copy(
                        piece.at[index, piece.shape[1] - ada_rows :],
                        ada_ref.at[pl.ds(start, ada_rows), pl.ds(column, size)],
                        ada_sems.at[number, index],
                    )
                )
    return copies


def cut_kernel(core_ref, up_ref, down_ref, *outs):
    width = down_ref.shape[2]
    low = lax.broadcasted_iota(jnp.int32, (up_ref.shape[0], 128), 1) < 64
    for start in range(0, 2 * width, 128):
        first, second, third = (up_ref[:, 3 * start + 128 * i : 3 * start + 128 * i + 128] for i in range(3))
        lanes = slice(start, start + 128)
        outs[0][0, :, lanes] = jnp.where(low, first, second).astype(LOW)
        outs[1][0, :, lanes] = pltpu.roll(jnp.where(low, third, first), 64, 1).astype(LOW)
        outs[2][0, :, lanes] = jnp.where(low, second, third).astype(LOW)
    for part, out in enumerate(outs):
        out[0, :, 2 * width :] = down_ref[part].astype(LOW)


def cut_parts(line, core, up, down):
    rows, columns = up.shape[0] // 2, up.shape[1]
    width = down.shape[2]
    return line.call(
        cut_kernel,
        (core[None], up, down),
        [pl.BlockSpec((rows, columns), lambda i, c: (c[0], 0)),
         pl.BlockSpec((3, rows, width), lambda i, c: (0, c[0], 0))],
        prefetch=1,
        grid=(1,),
        out_specs=[whole((1, rows, 3 * width))] * 3,
        out_shape=[jax.ShapeDtypeStruct((1, rows, 3 * width), LOW)] * 3,
        compiler_params=params(1),
        cost_estimate=cost(0, 4 << 20),
        name="cut",
    )


def conditioned(cond_ref, ada_ref, out_ref):
    scale = 1.0 + mul(cond_ref[...], ada_ref[...])
    for image in range(scale.shape[0]):
        out_ref[image] = scale[image : image + 1]


def front_kernel(group, table_ref, x_ref, cond_ref, *rest):
    pieces, rest = rest[:8], rest[8:]
    sums_ref, spread_ref, root_ref, cos_ref, up_ref, down_ref, *rest = rest
    act_ref, q_ref, k_ref, pack_ref, one_ref, w_ref, ada_ref, sems, ada_sems = rest

    @pl.when(pl.program_id(0) == 0)
    def _():
        fetch(load_head(table_ref, pieces, 0, w_ref, sems, ada_ref, ada_sems))
        conditioned(cond_ref, ada_ref, one_ref)

    scale_ref = one_ref.at[pl.ds(pl.program_id(0) * group, group)]
    width = x_ref.shape[1]
    x = x_ref[...].astype(WIDE)
    inverse = lax.rsqrt(jnp.mean(x * x, axis=-1, keepdims=True) + NORM_EPS)
    act = scaled(x * inverse, scale_ref).astype(LOW)
    act_ref[...] = act.T
    q = mul(act, w_ref[:, :width])
    k = mul(act, w_ref[:, width:])
    sums = mul((q * q).astype(LOW), sums_ref[0]) + mul((k * k).astype(LOW), sums_ref[1])
    factor = lax.rsqrt(sums + COSINE_EPS)
    high = factor.astype(LOW)
    low = (factor - high.astype(WIDE)).astype(LOW)
    lane = lax.broadcasted_iota(jnp.int32, factor.shape, 1)
    pack = jnp.where(lane < 32, high.astype(WIDE), jnp.where(lane < 64, low.astype(WIDE), 0.0))
    pack = pack.astype(LOW)
    pack_ref[...] = pack
    q = q * mul(pack, spread_ref[0]) * root_ref[...]
    k = k * mul(pack, spread_ref[1]) * root_ref[...]
    cos_rep, up_rep, down_rep = cos_ref[...], up_ref[...], down_ref[...]
    for pair in range(width // 128):
        lanes = slice(pair * 128, pair * 128 + 128)
        q_ref[:, lanes] = rotate(q[:, lanes], cos_rep, up_rep, down_rep, 1).astype(LOW)
        k_ref[:, lanes] = rotate(k[:, lanes], cos_rep, up_rep, down_rep, 1).astype(LOW)


def front(line, table, x, cond, pieces, sums, spread, root, turns, images):
    tokens, width = x.shape
    group = grouped(images)
    seq = tokens // images * group
    row = pl.BlockSpec((seq, width), lambda i: (i, 0))
    narrow = pl.BlockSpec((seq, 128), lambda i: (i, 0))
    full = jax.ShapeDtypeStruct((tokens, width), LOW)
    return line.call(
        functools.partial(front_kernel, group),
        (table, x, cond, *pieces, sums, spread, root, *turns),
        [SMEM, row, whole(cond.shape), *[ANY] * 8,
                  whole(sums.shape), whole(spread.shape), whole(root.shape), narrow, narrow, narrow],
        grid=(images // group,),
        out_specs=[turned_block(width, seq), row, row, narrow, whole((images, 1, width))],
        out_shape=[turned_shape(width, tokens), full, full, jax.ShapeDtypeStruct((tokens, 128), LOW),
                   jax.ShapeDtypeStruct((images, 1, width), WIDE)],
        scratch_shapes=[pltpu.VMEM((width, 2 * width), LOW), pltpu.VMEM((cond.shape[1], width), LOW),
                        pltpu.SemaphoreType.DMA((4, 8, 4)), SEMS],
        compiler_params=params(1),
        cost_estimate=cost(4 * tokens * width * width, 20 << 20),
        name="front",
    )


def attend_kernel(table_ref, q_ref, k_ref, valid_ref, x_ref, scale_ref, *rest):
    pieces = rest[:8]
    v_ref, o_ref, turned_ref, lse_ref, w_ref, sems = rest[8:]

    @pl.when(pl.program_id(0) == 0)
    def _():
        fetch(load_head(table_ref, pieces, 0, w_ref, sems))

    x = x_ref[...].astype(WIDE)
    inverse = lax.rsqrt(jnp.mean(x * x, axis=-1, keepdims=True) + NORM_EPS)
    act = scaled(x * inverse, scale_ref).astype(LOW)
    v_ref[...] = mul(act, w_ref[...]).astype(LOW)
    seq, width = q_ref.shape
    valid = valid_ref[...]
    lane = lax.broadcasted_iota(jnp.int32, (seq, 128), 1)
    first = lane < 64
    totals = jnp.zeros((seq, 128), WIDE)
    zero = jnp.zeros((seq, 128), LOW)
    for pair in range(width // 128):
        lanes = slice(pair * 128, pair * 128 + 128)
        q, k = q_ref[:, lanes], k_ref[:, lanes]
        v = v_ref[:, lanes] * valid
        mixed = None
        for half in range(2):
            pick = first if half == 0 else jnp.logical_not(first)
            scores = mul_nt(jnp.where(pick, q, zero), k)
            weights = jnp.exp(scores).astype(LOW)
            right = jnp.concatenate([jnp.where(pick, v, zero), valid], axis=1)
            both = mul(weights, right)
            total = both[:, 128:]
            part = both[:, :128] / total
            mixed = part if mixed is None else mixed + part
            totals = jnp.where(lane == 2 * pair + half, total, totals)
        mixed = mixed.astype(LOW)
        o_ref[:, lanes] = mixed
        turned_ref[lanes, :] = mixed.T
    lane_ok = lane < width // 64
    lse = jnp.log(jnp.where(lane_ok, totals, 1.0))
    lse_ref[0] = lse.T[: width // 64]


def attend(line, table, q, k, valid, x, scale, pieces, images):
    tokens, width = q.shape
    seq = tokens // images
    row = pl.BlockSpec((seq, width), lambda i: (i, 0))
    heads = width // 64
    low = jax.ShapeDtypeStruct((tokens, width), LOW)
    return line.call(
        attend_kernel,
        (table, q, k, valid, x, scale, *pieces),
        [SMEM, row, row, pl.BlockSpec((seq, 128), lambda i: (i, 0)), row,
         pl.BlockSpec((1, 1, width), lambda i: (i, 0, 0))] + [ANY] * 8,
        grid=(images,),
        out_specs=[row, row, turned_block(width, seq), pl.BlockSpec((1, heads, seq), lambda i: (i, 0, 0))],
        out_shape=[low, low, turned_shape(width, tokens),
                   jax.ShapeDtypeStruct((images, heads, seq), WIDE)],
        scratch_shapes=[pltpu.VMEM((width, width), LOW), pltpu.SemaphoreType.DMA((2, 8, 4))],
        compiler_params=params(1),
        cost_estimate=cost(16 * tokens * seq * width, 12 << 20),
        name="attend",
    )


def middle_kernel(group, table_ref, o_ref, x_ref, cond_ref, *rest):
    pieces = rest[:8]
    mid_ref, act_ref, turned_ref, two_ref, w_ref, ada_ref, sems, ada_sems = rest[8:]

    @pl.when(pl.program_id(0) == 0)
    def _():
        fetch(load_head(table_ref, pieces, 2, w_ref, sems, ada_ref, ada_sems))
        conditioned(cond_ref, ada_ref, two_ref)

    scale_ref = two_ref.at[pl.ds(pl.program_id(0) * group, group)]
    mid = x_ref[...].astype(WIDE) + mul(o_ref[...], w_ref[...])
    mid_ref[...] = mid
    inverse = lax.rsqrt(jnp.mean(mid * mid, axis=-1, keepdims=True) + NORM_EPS)
    act = scaled(mid * inverse, scale_ref).astype(LOW)
    act_ref[...] = act
    turned_ref[...] = act.T


def middle_block(line, table, o, x, cond, pieces, images):
    tokens, width = x.shape
    group = grouped(images)
    seq = tokens // images * group
    row = pl.BlockSpec((seq, width), lambda i: (i, 0))
    return line.call(
        functools.partial(middle_kernel, group),
        (table, o, x, cond, *pieces),
        [SMEM, row, row, whole(cond.shape)] + [ANY] * 8,
        grid=(images // group,),
        out_specs=[row, row, turned_block(width, seq), whole((images, 1, width))],
        out_shape=[jax.ShapeDtypeStruct((tokens, width), WIDE), jax.ShapeDtypeStruct((tokens, width), LOW),
                   turned_shape(width, tokens), jax.ShapeDtypeStruct((images, 1, width), WIDE)],
        scratch_shapes=[pltpu.VMEM((width, width), LOW), pltpu.VMEM((cond.shape[1], width), LOW),
                        pltpu.SemaphoreType.DMA((2, 8, 4)), SEMS],
        compiler_params=params(1),
        cost_estimate=cost(2 * tokens * width * width, 12 << 20),
        name="middle",
    )


def part_kernel(first, last, table_ref, act_ref, dy_ref, *rest):
    rest = list(rest)
    pieces = tuple(rest.pop(0) for _ in range(8))
    if last:
        mid_ref, scale_ref, out_table_ref = rest.pop(0), rest.pop(0), rest.pop(0)
        out_pieces = tuple(rest.pop(0) for _ in range(8))
    acc_ref = None if first else rest.pop(0)
    hid_ref, dgu_ref, turned_ref = rest.pop(0), rest.pop(0), rest.pop(0)
    if last:
        dmid_ref, db_ref, do_ref, dscale_ref = (rest.pop(0) for _ in range(4))
    else:
        da_ref = rest.pop(0)
    w_ref, sems = rest.pop(0), rest.pop(0)
    if last:
        out_ref, sems_out = rest.pop(0), rest.pop(0)

    @pl.when(pl.program_id(0) == 0)
    def _():
        copies = load_weight(table_ref, pieces, w_ref, sems)
        if last:
            copies = copies + load_head(out_table_ref, out_pieces, 2, out_ref, sems_out)
        fetch(copies)

    width = act_ref.shape[1]
    act, dy = act_ref[...], dy_ref[...]
    size = 512
    for start in range(0, width, size):
        cols = slice(start, start + size)
        above = slice(width + start, width + start + size)
        gate = mul(act, w_ref[:, cols])
        upper = mul(act, w_ref[:, above])
        grad = mul_nt(dy, w_ref[start : start + size, 2 * width :]).astype(LOW).astype(WIDE)
        cdf = 0.5 * (1.0 + lax.erf(gate * math.sqrt(0.5)))
        bell = jnp.exp(-0.5 * gate * gate) * (1.0 / math.sqrt(2.0 * math.pi))
        gelu = gate * cdf
        hid = (gelu * upper).astype(LOW)
        hid_ref[:, cols] = hid
        turned_ref[cols, :] = hid.T
        dgu_ref[:, cols] = (grad * upper * (cdf + gate * bell)).astype(LOW)
        dgu_ref[:, above] = (grad * gelu).astype(LOW)
    total = mul_nt(dgu_ref[:, :width], w_ref[:, :width])
    total += mul_nt(dgu_ref[:, width:], w_ref[:, width : 2 * width])
    if not first:
        total += acc_ref[...]
    if not last:
        da_ref[...] = total
        return
    dmid = dy.astype(WIDE) + norm_back(total, mid_ref[...], scale_ref, dscale_ref)
    dmid_ref[...] = dmid
    low = dmid.astype(LOW)
    db_ref[...] = low
    do_ref[...] = mul_nt(low, out_ref[...]).astype(LOW)


def geglu_part(line, table, act, dy, pieces, images, acc=None, final=None):
    tokens, width = act.shape
    group = grouped(images)
    seq = tokens // images * group
    first, last = acc is None, final is not None
    row = pl.BlockSpec((seq, width), lambda i: (i, 0))
    one = pl.BlockSpec((group, 1, width), lambda i: (i, 0, 0))
    args = [table, act, dy, *pieces]
    in_specs = [SMEM, row, row] + [ANY] * 8
    if last:
        mid, scale, out_table, out_pieces = final
        args += [mid, scale, out_table, *out_pieces]
        in_specs += [row, one, SMEM] + [ANY] * 8
    if not first:
        args.append(acc)
        in_specs.append(row)
    low = jax.ShapeDtypeStruct((tokens, width), LOW)
    wide = jax.ShapeDtypeStruct((tokens, width), WIDE)
    out_specs = [row, pl.BlockSpec((seq, 2 * width), lambda i: (i, 0)), turned_block(width, seq)]
    out_shape = [low, jax.ShapeDtypeStruct((tokens, 2 * width), LOW), turned_shape(width, tokens)]
    scratch = [pltpu.VMEM((width, 3 * width), LOW), SEMS]
    if last:
        out_specs += [row, row, row, one]
        out_shape += [wide, low, low, jax.ShapeDtypeStruct((images, 1, width), WIDE)]
        scratch += [pltpu.VMEM((width, width), LOW), pltpu.SemaphoreType.DMA((2, 8, 4))]
    else:
        out_specs.append(row)
        out_shape.append(wide)
    return line.call(
        functools.partial(part_kernel, first, last),
        args,
        in_specs,
        grid=(images // group,),
        out_specs=out_specs,
        out_shape=out_shape,
        scratch_shapes=scratch,
        compiler_params=params(1),
        cost_estimate=cost((12 if last else 10) * tokens * width * width, 30 << 20),
        name="geglu_part",
    )


def attend_back_kernel(q_ref, k_ref, v_ref, o_ref, do_ref, lse_ref, valid_ref, pack_ref, spread_ref,
                       root_ref, pick_ref, block_ref, cos_ref, up_ref, down_ref, dproj_ref, dhead_ref):
    seq, width = q_ref.shape
    valid = valid_ref[...]
    valid_wide = valid.astype(WIDE)
    first = lax.broadcasted_iota(jnp.int32, (seq, 128), 1) < 64
    zero = jnp.zeros((seq, 128), LOW)
    cos_rep, up_rep, down_rep = cos_ref[...], up_ref[...], down_ref[...]
    product = (do_ref[...].astype(WIDE) * o_ref[...].astype(WIDE)).astype(LOW)
    delta = mul_nt(pick_ref[...], product)
    pack = pack_ref[...]
    block = block_ref[...]
    head_lane = lax.broadcasted_iota(jnp.int32, (1, 128), 1)
    row = jnp.zeros((1, 128), WIDE)
    for pair in range(width // 128):
        lanes = slice(pair * 128, pair * 128 + 128)
        q, k, v, do = q_ref[:, lanes], k_ref[:, lanes], v_ref[:, lanes], do_ref[:, lanes]
        k_turned = (k * valid).T
        dv = dk = None
        dq_parts = []
        for half in range(2):
            head = 2 * pair + half
            pick = first if half == 0 else jnp.logical_not(first)
            q_one = jnp.where(pick, q, zero)
            do_one = jnp.where(pick, do, zero)
            weights = jnp.exp(mul_nt(k, q_one) - lse_ref[0, head : head + 1, :])
            grads = mul_nt(v, do_one)
            dscore = (weights * (grads - delta[head : head + 1, :])).astype(LOW)
            part_v = mul(weights.astype(LOW), do_one)
            part_k = mul(dscore, q_one)
            dv = part_v if dv is None else dv + part_v
            dk = part_k if dk is None else dk + part_k
            dq_parts.append(mul(k_turned[half * 64 : half * 64 + 64], dscore))
        dq = jnp.concatenate(dq_parts, axis=0).T
        dk = dk * valid_wide
        root = root_ref[:, lanes]
        for side, (grad, value) in enumerate(((dq, q), (dk, k))):
            value = value.astype(WIDE)
            inner = mul((grad * value).astype(LOW), block)
            total = jnp.sum(inner, axis=0, keepdims=True)
            if side == 0:
                head_total = total
            else:
                total = head_total + total
                row = jnp.where(head_lane == 2 * pair, total[:, :1], row)
                row = jnp.where(head_lane == 2 * pair + 1, total[:, 64:65], row)
            factor = mul(pack, spread_ref[side, :, lanes])
            back = factor * (root * grad - value * (inner / root))
            back = rotate(back, cos_rep, up_rep, down_rep, -1)
            dproj_ref[:, side * width + pair * 128 : side * width + pair * 128 + 128] = back.astype(LOW)
        dproj_ref[:, 2 * width + pair * 128 : 2 * width + pair * 128 + 128] = (dv * valid_wide).astype(LOW)
    dhead_ref[0] = row


def attend_back(line, q, k, v, o, do, lse, valid, pack, spread, root, pick, block, turns, images):
    tokens, width = q.shape
    seq = tokens // images
    heads = width // 64
    row = pl.BlockSpec((seq, width), lambda i: (i, 0))
    narrow = pl.BlockSpec((seq, 128), lambda i: (i, 0))
    return line.call(
        attend_back_kernel,
        (q, k, v, o, do, lse, valid, pack, spread, root, pick, block, *turns),
        [row, row, row, row, row, pl.BlockSpec((1, heads, seq), lambda i: (i, 0, 0)), narrow, narrow,
                  whole(spread.shape), whole(root.shape), whole(pick.shape), whole(block.shape),
                  narrow, narrow, narrow],
        grid=(images,),
        out_specs=[pl.BlockSpec((seq, 3 * width), lambda i: (i, 0)),
                   pl.BlockSpec((1, 1, 128), lambda i: (i, 0, 0))],
        out_shape=[jax.ShapeDtypeStruct((tokens, 3 * width), LOW),
                   jax.ShapeDtypeStruct((images, 1, 128), WIDE)],
        compiler_params=params(1),
        cost_estimate=cost(40 * tokens * seq * width, 20 << 20),
        name="attend_back",
    )


def input_kernel(even_ref, odd_ref, dproj_ref, x_ref, dmid_ref, scale_ref, *rest):
    pieces = rest[:16]
    out_ref, dscale_ref, w_ref, sems = rest[16:]

    @pl.when(pl.program_id(0) == 0)
    def _():
        width = x_ref.shape[1]
        fetch(
            load_head(even_ref, pieces[:8], 0, w_ref.at[:, : 2 * width], sems.at[:4])
            + load_head(odd_ref, pieces[8:], 0, w_ref.at[:, 2 * width :], sems.at[4:])
        )

    width = x_ref.shape[1]
    grad = mul_nt(dproj_ref[:, :width], w_ref[:, :width])
    grad += mul_nt(dproj_ref[:, width : 2 * width], w_ref[:, width : 2 * width])
    grad += mul_nt(dproj_ref[:, 2 * width :], w_ref[:, 2 * width :])
    x = x_ref[...].astype(WIDE)
    out_ref[...] = (dmid_ref[...] + norm_back(grad, x, scale_ref, dscale_ref)).astype(LOW)


def input_block(line, tables, dproj, x, dmid, scale, pieces, images, place, places, into):
    tokens, width = x.shape
    group = grouped(images)
    seq = tokens // images * group
    steps = images // group // places
    row = pl.BlockSpec((seq, width), lambda i: (place * steps + i, 0))
    one = pl.BlockSpec((group, 1, width), lambda i: (place * steps + i, 0, 0))
    return line.call(
        input_kernel,
        (*tables, dproj, x, dmid, scale, *pieces),
        [SMEM, SMEM, pl.BlockSpec((seq, 3 * width), lambda i: (place * steps + i, 0)), row, row, one] + [ANY] * 16,
        into=into,
        grid=(steps,),
        out_specs=[row,
                   pl.BlockSpec((group, 1, width), lambda i: (i, 0, 0))],
        out_shape=[jax.ShapeDtypeStruct((tokens, width), LOW),
                   jax.ShapeDtypeStruct((images // places, 1, width), WIDE)],
        scratch_shapes=[pltpu.VMEM((width, 3 * width), LOW), pltpu.SemaphoreType.DMA((6, 8, 4))],
        compiler_params=params(1),
        cost_estimate=cost(6 * tokens * width * width // places, 24 << 20),
        name="input_grad",
    )


def result_kernel(even_ref, odd_ref, h0, h1, h2, mid_ref, *rest):
    pieces, out_ref, w_ref, sems = rest[:24], rest[24], rest[25], rest[26]
    width = mid_ref.shape[1]

    @pl.when(pl.program_id(0) == 0)
    def _():
        copies = []
        for part in range(3):
            ref = pieces[8 * part : 8 * part + 8]
            down = tuple(piece.at[:, :, 2 * width : 3 * width] for piece in ref)
            table_ref = odd_ref if part % 2 == 0 else even_ref
            copies += load_weight(table_ref, down, w_ref.at[part], sems.at[part])
        fetch(copies)

    total = mid_ref[...]
    for part, hid_ref in enumerate((h0, h1, h2)):
        total += mul(hid_ref[...], w_ref[part])
    out_ref[...] = total.astype(LOW)


def result_block(line, tables, hids, mid, pieces, images, place, places, into):
    tokens, width = mid.shape
    group = grouped(images)
    seq = tokens // images * group
    steps = images // group // places
    row = pl.BlockSpec((seq, width), lambda i: (place * steps + i, 0))
    return line.call(
        result_kernel,
        (*tables, *hids, mid, *[piece for part in pieces for piece in part]),
        [SMEM, SMEM, row, row, row, row] + [ANY] * 24,
        grid=(steps,),
        into=into,
        out_specs=row,
        out_shape=jax.ShapeDtypeStruct((tokens, width), LOW),
        scratch_shapes=[pltpu.VMEM((3, width, width), LOW), pltpu.SemaphoreType.DMA((3, 8, 4))],
        compiler_params=params(1),
        cost_estimate=cost(6 * tokens * width * width, 20 << 20),
        name="result",
    )


def weight_kernel(lefts, table_ref, *refs):
    refs = list(refs)
    acts = [refs.pop(0) for _ in range(max(lefts) + 1)]
    grads = [refs.pop(0) for _ in lefts]
    outs = [refs.pop(0) for _ in range(8)]
    turned_ref, sems = refs
    rows = outs[0].shape[1]
    half = outs[0].shape[2]
    depth = turned_ref.shape[1]
    core = table_ref[32]
    step = pl.program_id(0)

    def copy(number, index):
        start = pl.multiple_of(index * 4 * rows, 16)
        return pltpu.make_async_copy(
            acts[number].at[pl.ds(start, 4 * rows)],
            turned_ref.at[number, index * 4 * rows : index * 4 * rows + 4 * rows],
            sems.at[number, index],
        )

    @pl.when(step == 0)
    def _():
        for number in range(len(acts)):
            for index in range(4):
                copy(number, index).start()

    for span, (left, grad_ref) in enumerate(zip(lefts, grads)):
        @pl.when(step == span)
        def _(span=span, left=left, grad_ref=grad_ref):
            if left not in lefts[:span]:
                for index in range(4):
                    copy(left, index).wait()
            for side in range(2):
                place = pl.multiple_of((core if side == 0 else 1 - core) * half, half)
                grad = grad_ref[:, pl.ds(place, half)]
                for piece in range(4):
                    parts = []
                    for index in range(4):
                        start = table_ref[side * 16 + piece * 4 + index] * rows
                        parts.append(turned_ref[left, pl.ds(pl.multiple_of(start, 16), rows), :])
                    total = mul(jnp.concatenate(parts, axis=0), grad)
                    out = outs[4 * side + piece]
                    out[...] = total.reshape(out.shape).astype(LOW)


def weight_halves(line, table, acts, spans):
    depth, tokens = acts[0].shape
    rows = depth // 16
    wide = spans[0][1].shape[1] // spans[0][3]
    half = wide // 2
    count = len(spans)

    def grad_spec(number, span):
        return pl.BlockSpec((tokens, wide), lambda m, t: (0, span))

    tile = pl.BlockSpec((4, rows, half), lambda m, t: (0, 0, m))
    shape = jax.ShapeDtypeStruct((4, rows, count * half), LOW)
    size = 2 * (tokens * (len(acts) * depth + count * wide) + depth * count * wide)
    outs = line.call(
        functools.partial(weight_kernel, [span[0] for span in spans]),
        (table, *acts, *[span[1] for span in spans]),
        [ANY for _ in acts] + [grad_spec(number, span[2]) for number, span in enumerate(spans)],
        prefetch=1,
        grid=(count,),
        out_specs=[tile] * 8,
        out_shape=[shape] * 8,
        scratch_shapes=[
            pltpu.VMEM((len(acts), depth, tokens), LOW), pltpu.SemaphoreType.DMA((len(acts), 4))
        ],
        compiler_params=params(1),
        cost_estimate=cost(2 * tokens * depth * count * wide, size),
        name="weight_grad",
    )
    return outs[:4], outs[4:]


def adam(weight, first, second, gradient, factor, rate, decay):
    clipped = gradient * factor
    new_first = BETA_ONE * first + (1.0 - BETA_ONE) * clipped
    new_second = BETA_TWO * second + (1.0 - BETA_TWO) * clipped * clipped
    denominator = jnp.sqrt(new_second / (1.0 - BETA_TWO**STEP)) + ADAM_EPS
    new_weight = (
        weight * (1.0 - rate * decay) - rate * (new_first / (1.0 - BETA_ONE**STEP)) / denominator
    )
    return (new_weight, new_first, new_second)


def adam_kernel(core_ref, total_ref, *refs):
    refs = list(refs)
    ada, qkv, out, up, down, scale = ([refs.pop(0) for _ in range(3)] for _ in range(6))
    ada_grad, head_grad = refs.pop(0), refs.pop(0)
    mines = [refs.pop(0) for _ in range(4)]
    others = [refs.pop(0) for _ in range(4)]
    norm_ref = refs.pop(0)
    new_ada, new_qkv, new_out, new_up, new_down, new_scale = ([refs.pop(0) for _ in range(3)] for _ in range(6))
    own_first = core_ref[0] == 0
    head = head_grad[...]
    total = total_ref[0:1, 0:1] + jnp.sum(head * head, axis=1, keepdims=True)
    norm = jnp.sqrt(total)
    factor = jnp.minimum(1.0, CLIP / (norm + 1e-06))

    def update(news, olds, at, gradient, rate, decay):
        weight, first, second = (ref[at] for ref in olds)
        for ref, value in zip(news, adam(weight, first, second, gradient, factor, rate, decay)):
            ref[at] = value

    @pl.when(pl.program_id(0) == 0)
    def _():
        norm_ref[...] = jnp.broadcast_to(norm, norm_ref.shape)
        update(new_scale, scale, (slice(None),) * 2, head, SCALE_RATE, 0.0)
        for index in range(ada_grad.shape[0]):
            update(new_ada, ada, (index,), ada_grad[index], RATE, DECAY)

    def columns(number, span):
        size = mines[0].shape[1] // 3
        mine = mines[number][:, span * size : span * size + size].astype(WIDE)
        other = others[number][:, span * size : span * size + size].astype(WIDE)
        return jnp.where(own_first, mine, other), jnp.where(own_first, other, mine)

    def by_halves(news, olds, number, spans, rate):
        for place, span in enumerate(spans):
            for half, gradient in enumerate(columns(number, span)):
                size = gradient.shape[1]
                start = (2 * place + half) * size
                update(news, olds, (slice(None), slice(start, start + size)), gradient, rate, DECAY)

    by_halves(new_qkv, qkv, 3, (0, 1, 2), RATE)
    by_halves(new_out, out, 2, (3,), OUTPUT_RATE)
    for part in range(3):
        for half, gradient in enumerate(columns(part, 2)):
            size = gradient.shape[1]
            update(new_down, down, (part, slice(None), slice(half * size, half * size + size)), gradient, RATE, DECAY)
    low = lax.broadcasted_iota(jnp.int32, (up[0].shape[0], 128), 1) < 64
    for span in range(2):
        parts = [columns(part, span) for part in range(3)]
        size = parts[0][0].shape[1]
        for half in range(2):
            for lane in range(0, size, 128):
                one, two, three = (parts[part][half][:, lane : lane + 128] for part in range(3))
                turned = pltpu.roll(two, 64, 1)
                start = 3 * ((2 * span + half) * size + lane)
                pieces = (jnp.where(low, one, turned), jnp.where(low, three, one), jnp.where(low, turned, three))
                for number, gradient in enumerate(pieces):
                    at = (slice(None), slice(start + 128 * number, start + 128 * number + 128))
                    update(new_up, up, at, gradient, RATE, DECAY)


def adam_all(line, core, total, ada, qkv, out, up, down, scale, ada_grad, head_grad, mines, others):
    steps = 4
    args = [core[None], total]
    in_specs = [SMEM, whole(total.shape)]
    out_specs = [whole(total.shape)]
    out_shape = [jax.ShapeDtypeStruct(total.shape, WIDE)]

    def by_rows(array):
        shape = array.shape[:-2] + (array.shape[-2] // steps, array.shape[-1])
        lead = (0,) * (array.ndim - 2)
        return pl.BlockSpec(shape, lambda i: lead + (i, 0))

    for group, cut in ((ada, False), (qkv, True), (out, True), (up, True), (down, True), (scale, False)):
        for array in group:
            spec = by_rows(array) if cut else whole(array.shape)
            args.append(array)
            in_specs.append(spec)
            out_specs.append(spec)
            out_shape.append(jax.ShapeDtypeStruct(array.shape, WIDE))
    args += [ada_grad, head_grad, *mines, *others]
    in_specs += [whole(ada_grad.shape), whole(head_grad.shape)] + [by_rows(m) for m in (*mines, *others)]
    return line.call(
        adam_kernel,
        args,
        in_specs,
        grid=(steps,),
        out_specs=out_specs,
        out_shape=out_shape,
        compiler_params=params(1),
        cost_estimate=cost(0, 30 << 20),
        name="adamw",
    )


def turn_kernel(shapes_ref, rates_ref, cos_ref, up_ref, down_ref, valid_ref):
    image = pl.program_id(0)
    height, width = shapes_ref[image, 0], shapes_ref[image, 1]
    shape = cos_ref.shape
    slot = lax.broadcasted_iota(jnp.int32, shape, 0)
    place = slot.astype(WIDE)
    wide = width.astype(WIDE)
    row = jnp.floor((place + 0.5) / wide)
    angle = row * rates_ref[0:1, :] + (place - row * wide) * rates_ref[1:2, :]
    lane = lax.broadcasted_iota(jnp.int32, shape, 1) % 64
    cosine, sine = jnp.cos(angle), jnp.sin(angle)
    cos_ref[...] = jnp.where(lane < 32, cosine, 1.0)
    up_ref[...] = jnp.where(lane < 16, -sine, 0.0)
    down_ref[...] = jnp.where((lane >= 16) & (lane < 32), sine, 0.0)
    valid_ref[...] = jnp.where(slot < height * width, 1.0, 0.0).astype(LOW)


def turn_tables(line, shapes, seq_len, head_dim):
    images = shapes.shape[0]
    count = head_dim // 8
    frequency = ROPE_BASE ** (-jnp.arange(count, dtype=WIDE) / count)
    none = jnp.zeros((count,), WIDE)
    blank = jnp.zeros((head_dim // 2,), WIDE)
    rates = jnp.stack(
        [
            jnp.concatenate([frequency, none, frequency, none, blank] * 2),
            jnp.concatenate([none, frequency, none, frequency, blank] * 2),
        ]
    )
    block = pl.BlockSpec((seq_len, 128), lambda i: (i, 0))
    wide = jax.ShapeDtypeStruct((images * seq_len, 128), WIDE)
    *turns, valid = line.call(
        turn_kernel,
        (shapes, rates),
        [SMEM, whole(rates.shape)],
        grid=(images,),
        out_specs=[block] * 4,
        out_shape=[wide, wide, wide, jax.ShapeDtypeStruct(wide.shape, LOW)],
        compiler_params=params(1),
        cost_estimate=cost(0, 2 << 20),
        name="turns",
    )
    return tuple(turns), valid


def head_matrices(width, head_dim):
    heads = width // head_dim
    owner = np.arange(width) // head_dim
    sums = np.zeros((2, width, 128), np.float32)
    spread = np.zeros((2, 128, width), np.float32)
    for side in range(2):
        for copy in range(2):
            sums[side, np.arange(width), side * heads + copy * 2 * heads + owner] = 1.0
            spread[side, side * heads + copy * 2 * heads + owner, np.arange(width)] = 1.0
    pick = np.zeros((heads, width), np.float32)
    pick[owner, np.arange(width)] = 1.0
    block = np.kron(np.eye(128 // head_dim), np.ones((head_dim, head_dim)))
    return tuple(jnp.asarray(m, LOW) for m in (sums, spread, pick, block))


def finish_wide(net, ada, qkv, out, up, down, scale, grad_ada, head_grad, mines, others):
    def columns(number, span):
        size = mines[0].shape[1] // 3
        mine = mines[number][:, span * size : span * size + size]
        other = others[number][:, span * size : span * size + size]
        pair = [jnp.where(net.core == 0, mine, other), jnp.where(net.core == 0, other, mine)]
        return jnp.concatenate(pair, axis=1).astype(WIDE)

    grad_up = [
        jnp.concatenate([columns(part, span) for span in range(2)], axis=1).reshape(-1, 2, 16, 64)
        for part in range(3)
    ]
    gradients = [
        jnp.concatenate([columns(3, span) for span in range(3)], axis=1),
        columns(2, 3),
        jnp.stack(grad_up, axis=3).reshape(-1, up[0].shape[1]),
        jnp.concatenate([columns(part, 2) for part in range(3)], axis=0),
    ]
    gradients = [grad_ada] + [net.split_sub(gradient) for gradient in gradients]
    total = lax.psum(sum(jnp.sum(gradient * gradient) for gradient in gradients), "fsdp")
    head_grad = head_grad[0]
    norm = jnp.sqrt(total + jnp.sum(head_grad * head_grad))
    factor = jnp.minimum(1.0, CLIP / (norm + 1e-06))
    rates = (RATE, RATE, OUTPUT_RATE, RATE, RATE)
    news = [norm]
    for group, gradient, rate in zip((ada, qkv, out, up, down), gradients, rates):
        news += adam(*group, gradient, factor, rate, DECAY)
    news += adam(*scale, head_grad, factor, SCALE_RATE, 0.0)
    return tuple(news)


def local(
    tokens,
    condition,
    shapes,
    cotangent,
    ada_weight,
    ada_first,
    ada_second,
    qkv_weight,
    qkv_first,
    qkv_second,
    out_weight,
    out_first,
    out_second,
    up_weight,
    up_first,
    up_second,
    down_weight,
    down_first,
    down_second,
    head_scale,
    scale_first,
    scale_second,
    *,
    dp_size,
    fsdp_size,
):
    net = Net(fsdp_size, dp_size)
    line = Line()
    core = net.core
    images = shapes.shape[0]
    width = tokens.shape[1]
    seq_len = tokens.shape[0] // images
    head_count = head_scale.shape[0]
    head_dim = width // head_count
    small = net.sub == 1
    even, odd = net.tables

    ada_joined = net.join_sub(ada_weight.transpose(1, 0, 2)).transpose(1, 0, 2) if net.sub > 1 else ada_weight
    half_qk, half_vo = head_parts(
        line, core, net.join_sub(qkv_weight), net.join_sub(out_weight), ada_joined
    )
    get_qk = Gather(net, line, 0, half_qk)
    down_joined = net.join_sub(down_weight).reshape(3, -1, width)
    halves = cut_parts(line, core, net.join_sub(up_weight), down_joined)
    get_qk.second()
    get_vo = Gather(net, line, 1, half_vo)
    turns, valid = turn_tables(line, shapes, seq_len, head_dim)
    sums, spread, pick, block = head_matrices(width, head_dim)
    root = jnp.repeat(jnp.sqrt(head_scale), head_dim)[None]
    get_vo.wait()
    get_qk.third()
    get_vo.second()
    get_vo.wait()
    get_qk.wait_near()
    get_vo.third()
    get_qk.fourth()
    get_mlp = [Gather(net, line, 1, halves[0])]
    get_qk.wait_last()
    get_mlp[0].second()
    get_mlp.append(Gather(net, line, 0, halves[1]))
    get_qk.finish()

    act_one, q, k, pack, scale_one = front(
        line, even, tokens, condition, get_qk.pieces, sums, spread, root, turns, images
    )
    get_mlp[0].third()
    get_vo.fourth()
    get_vo.finish()
    v, o, o_turned, lse = attend(
        line, odd, q, k, valid, tokens, scale_one, get_vo.pieces, images
    )
    get_mlp[1].second()
    get_mlp[0].fourth()
    mid, act_two, act_two_turned, scale_two = middle_block(
        line, odd, o, tokens, condition, get_vo.pieces, images
    )
    get_mlp[1].third()
    get_mlp[0].finish()
    get_mlp.append(Gather(net, line, 1, halves[2]))

    def put(parity, acts, spans):
        return Scatter(net, line, parity, *weight_halves(line, net.tables[parity], acts, spans))

    def mlp_spans(hid_turned, dgu):
        return ((act_two_turned, hid_turned), ((0, dgu, 0, 2), (0, dgu, 1, 2), (1, cotangent, 0, 1)))

    hid0, dgu0, turned0, acc = geglu_part(line, odd, act_two, cotangent, get_mlp[0].pieces, images)
    get_mlp[2].second()
    get_mlp[1].fourth()
    put0 = put(0, *mlp_spans(turned0, dgu0))
    get_mlp[2].third()
    get_mlp[1].finish()
    hid1, dgu1, turned1, acc = geglu_part(
        line, even, act_two, cotangent, get_mlp[1].pieces, images, acc
    )
    get_mlp[2].fourth()
    put0.start()
    put1 = put(1, *mlp_spans(turned1, dgu1))
    put0.first()
    get_mlp[2].finish()
    hid2, dgu2, turned2, dmid, db, do, dscale_two = geglu_part(
        line, odd, act_two, cotangent, get_mlp[2].pieces, images, acc,
        (mid, scale_two, odd, get_vo.pieces),
    )
    put0.second()
    put1.start()
    acts2, spans2 = mlp_spans(turned2, dgu2)
    put2 = put(0, acts2 + (o_turned,), spans2 + ((2, db, 0, 1),))
    put0.third()
    put1.first()
    dproj, dhead = attend_back(
        line, q, k, v, o, do, lse, valid, pack, spread, root, pick, block, turns, images
    )
    put0.fourth()
    put1.second()
    put2.start()
    put_qkv = put(1, (act_one,), tuple((0, dproj, span, 3) for span in range(3)))
    put0.finish()
    put1.third()
    put2.first()
    put_qkv.start()

    places = 2 if images % (2 * grouped(images)) == 0 else 1

    def result(place, into=None):
        return result_block(
            line, net.tables, (hid0, hid1, hid2), mid, [get.pieces for get in get_mlp], images,
            place, places, into,
        )

    qkv_pieces = get_qk.pieces + get_vo.pieces

    def to_input(place, into=None):
        return input_block(
            line, net.tables, dproj, tokens, dmid, scale_one, qkv_pieces, images, place, places, into
        )

    input_grad, dscale_one = to_input(0)
    put1.fourth()
    put2.second()
    put_qkv.first()
    if places > 1:
        input_grad, rest = to_input(1, input_grad)
        dscale_one = jnp.concatenate([dscale_one, rest], axis=0)
    put1.finish()
    put2.third()
    put_qkv.second()

    dhead = jnp.sum(dhead, axis=0)
    rows = jnp.concatenate([dscale_one[:, 0], dscale_two[:, 0], condition.astype(WIDE)], axis=1)
    if small:
        high = dhead.astype(LOW)
        rest = (dhead - high.astype(WIDE)).astype(LOW)
        heads = jnp.concatenate([high, rest, jnp.zeros((6, 128), LOW)], axis=0)
        rows = jnp.concatenate([rows.astype(LOW).reshape(1, -1, 128), heads[None]], axis=1)
        late = SmallGather(net, line, rows)
        late.step((4, 8, 12))
    block_output = result(0)
    put_qkv.third()
    put2.fourth()
    if small:
        late.step((1, 2, 3))
    if places > 1:
        block_output = result(1, block_output)
    put_qkv.fourth()
    put2.finish()
    if small:
        late.step()
        rows = late.held[:, :-8].reshape(32 * images, -1).astype(WIDE)
        dhead = jnp.sum(late.held[:, -8:-6].astype(WIDE), axis=(0, 1))[None]
    else:
        rows = lax.all_gather(rows, AXES, axis=0, tiled=True)
        dhead = lax.psum(dhead, AXES)
    own_rows = ada_weight.shape[1]
    own_start = 2 * width + lax.axis_index("fsdp") * own_rows
    cond_own = lax.dynamic_slice_in_dim(rows, own_start, own_rows, axis=1)
    grad_ada = jnp.stack(
        [jnp.dot(cond_own.T, rows[:, :width], precision=PRECISE),
         jnp.dot(cond_own.T, rows[:, width : 2 * width], precision=PRECISE)]
    )
    head_grad = dhead[:, :head_count] / (2.0 * head_scale)
    ada_square = line.pin(0.5 * jnp.sum(grad_ada * grad_ada))
    grad_ada, head_grad = line.pin(grad_ada), line.pin(head_grad)
    put_qkv.finish()
    puts = (put0, put1, put2, put_qkv)
    mines = tuple(each.mine for each in puts)
    others = tuple(each.other for each in puts)
    ada = (ada_weight, ada_first, ada_second)
    qkv = (qkv_weight, qkv_first, qkv_second)
    out = (out_weight, out_first, out_second)
    up = (up_weight, up_first, up_second)
    down = (down_weight, down_first, down_second)
    scale = (head_scale, scale_first, scale_second)
    if not small:
        return (block_output, input_grad) + finish_wide(
            net, ada, qkv, out, up, down, scale, grad_ada, head_grad, mines, others
        )
    local_squares = sum(each.square for each in puts) + ada_square
    total = net.total(local_squares)
    rows = down_weight.shape[0] // 3
    news = adam_all(
        line, core, total, ada, qkv, out, up,
        tuple(array.reshape(3, rows, width) for array in down),
        tuple(array[None] for array in scale), grad_ada, head_grad, mines, others,
    )
    return (
        block_output,
        input_grad,
        news[0][0, 0],
        *news[1:13],
        *[array.reshape(down_weight.shape) for array in news[13:16]],
        *[array[0] for array in news[16:19]],
    )


def solution(mesh):
    tokens = P(("dp", "fsdp"), None)
    ada = P(None, "fsdp", None)
    rows = P("fsdp", None)
    return jax.shard_map(
        functools.partial(local, dp_size=mesh.shape["dp"], fsdp_size=mesh.shape["fsdp"]),
        mesh=mesh,
        in_specs=(tokens,) * 4 + (ada,) * 3 + (rows,) * 12 + (P(),) * 3,
        out_specs=(tokens, tokens, P()) + (ada,) * 3 + (rows,) * 12 + (P(),) * 3,
        check_vma=False,
    )
```

```python
import functools
import math

import jax
import jax.numpy as jnp
import numpy as np
from jax import lax
from jax.experimental import pallas as pl
from jax.experimental.pallas import tpu as pltpu
from jax.sharding import PartitionSpec as P

FF = 3072
STEP = 10


NORM_EPS = 1e-06
COSINE_EPS = 1e-06
ROPE_BASE = 100.0
CLIP = 1.0
RATE = 0.02
OUTPUT_RATE = 0.2
SCALE_RATE = 8.0
BETA_ONE = 0.9
BETA_TWO = 0.95
ADAM_EPS = 1e-08
DECAY = 0.01
PRECISE = lax.Precision.HIGHEST
AXES = ("dp", "fsdp")
LOW = jnp.bfloat16
WIDE = jnp.float32


ORDERS = (
    ((8, 4, 1, 2), (2, 8, 4, 1)),
    ((8, 4, 2, 1), (1, 8, 4, 2)),
)


class Net:
    def __init__(self, size, dp_size):
        self.size = size
        self.dp_size = dp_size
        self.sub = size // 16
        self.core = lax.axis_index("dp")
        self.me = lax.axis_index("fsdp") // self.sub
        self.tables = tuple(self.table(order) for order in ORDERS)

    def exchange(self, array, bits):
        pairs = []
        for core in range(self.dp_size):
            for place in range(self.size):
                target = place ^ (bits[core % 2] * self.sub)
                pairs.append((core * self.size + place, core * self.size + target))
        return lax.ppermute(array, AXES, pairs)

    def cross(self, array, parity, stage):
        order = ORDERS[parity]
        return self.exchange(array, (order[0][stage], order[1][stage]))

    def swap(self, array):
        pairs = []
        for core in range(self.dp_size):
            for place in range(self.size):
                pairs.append((core * self.size + place, (core ^ 1) * self.size + place))
        return lax.ppermute(array, AXES, pairs)

    def table(self, order):
        index = lax.iota(jnp.int32, 32)
        side = self.core ^ (index >> 4)
        value = jnp.full((32,), self.me, jnp.int32)
        for stage in range(4):
            bit = jnp.where(side == 0, order[0][stage], order[1][stage])
            value = value ^ ((index >> stage & 1) * bit)
        return jnp.concatenate([value, self.core[None]]).astype(jnp.int32)

    def groups(self):
        return [list(range(g * self.sub, (g + 1) * self.sub)) for g in range(16)]

    def join_sub(self, shard):
        if self.sub == 1:
            return shard
        return lax.all_gather(shard, "fsdp", axis=0, tiled=True, axis_index_groups=self.groups())

    def split_sub(self, gradient):
        gathered = lax.all_gather(gradient, "fsdp", axis=0, axis_index_groups=self.groups())
        rows = gradient.shape[0] // self.sub
        place = lax.axis_index("fsdp") % self.sub
        return lax.dynamic_slice_in_dim(jnp.sum(gathered, axis=0), place * rows, rows, axis=0)

    def total(self, value):
        for bits in ((1, 2, 3), (4, 8, 12)):
            value = value + sum(self.exchange(value, (bit, bit)) for bit in bits)
        return value + self.swap(value)


TIMES = {
    "front": 18,
    "attend": 13,
    "middle": 10,
    "geglu_part": 20,
    "weight_grad": 14,
    "attend_back": 30,
    "input_grad": 12,
    "result": 11,
}
WORK = 1150000000


class Line:
    def __init__(self):
        self.last = None
        self.waits = []

    def call(self, kernel, args, in_specs, prefetch=0, into=None, **kwargs):
        deps = []
        if self.last is not None:
            token = self.last
            if self.waits:
                token = lax.optimization_barrier((token, *self.waits))[0]
            deps = [token]
        self.waits = []
        count = len(deps)
        if into is not None:
            args, in_specs = (*args, into), (*in_specs, ANY)
            kwargs["input_output_aliases"] = {count + len(args) - 1: 0}
            inner = kernel

            def kernel(*refs):
                inner(*refs[: len(args) - 1], *refs[len(args) :])

        one = not isinstance(kwargs["out_shape"], (list, tuple))
        shapes = [kwargs["out_shape"]] if one else list(kwargs["out_shape"])
        specs = kwargs["out_specs"]
        specs = [specs] if not isinstance(specs, (list, tuple)) else list(specs)
        place = prefetch + len(in_specs) + len(shapes)

        def body(*refs):
            refs = refs[:prefetch] + refs[prefetch + count :]
            refs[place][...] = jnp.zeros((8, 128), WIDE)
            kernel(*refs[:place], *refs[place + 1 :])

        in_specs = [ANY] * count + list(in_specs)
        out_specs = specs + [whole((8, 128)) if "grid" in kwargs else VMEM]
        del kwargs["out_specs"]
        kwargs["out_shape"] = shapes + [jax.ShapeDtypeStruct((8, 128), WIDE)]
        if prefetch:
            kwargs["grid_spec"] = pltpu.PrefetchScalarGridSpec(
                num_scalar_prefetch=prefetch,
                grid=kwargs.pop("grid"),
                in_specs=in_specs,
                out_specs=out_specs,
                scratch_shapes=kwargs.pop("scratch_shapes", []),
            )
        else:
            kwargs["in_specs"] = in_specs
            kwargs["out_specs"] = out_specs
        if kwargs["name"] in TIMES:
            kwargs["cost_estimate"] = cost(TIMES[kwargs["name"]] * WORK, 1 << 20)
        *outs, self.last = pl.pallas_call(body, **kwargs)(*args[:prefetch], *deps, *args[prefetch:])
        return outs[0] if one else outs

    def pin(self, array):
        if self.last is not None:
            array, _ = lax.optimization_barrier((array, self.last))
        self.waits.append(array)
        return array


class Gather:
    def __init__(self, net, line, parity, half):
        self.net, self.line, self.parity = net, line, parity
        self.held = line.pin(half)
        self.got = net.cross(self.held, parity, 0)

    def wait(self):
        self.got = self.line.pin(self.got)

    def second(self):
        self.wait()
        self.held = join(self.line, self.held, self.got)
        self.got = self.net.cross(self.held, self.parity, 1)

    def third(self):
        self.wait()
        self.held = join(self.line, self.held, self.got)
        self.near = self.net.cross(self.held, self.parity, 2)
        self.far = self.net.cross(self.held, self.parity, 3)
        self.swapped = [self.net.swap(self.held)]

    def wait_near(self):
        self.near, self.far = self.line.pin(self.near), self.line.pin(self.far)

    def wait_last(self):
        self.last = self.line.pin(self.last)

    def fourth(self):
        self.wait_near()
        self.swapped = [self.line.pin(array) for array in self.swapped]
        self.last = self.net.cross(self.near, self.parity, 3)
        self.swapped += [self.net.swap(self.near), self.net.swap(self.far)]

    def finish(self):
        self.last = self.line.pin(self.last)
        self.swapped = [self.line.pin(array) for array in self.swapped]
        self.swapped.append(self.net.swap(self.last))
        self.pieces = (self.held, self.near, self.far, self.last, *self.swapped)


class Scatter:
    def __init__(self, net, line, parity, keep, send):
        self.net, self.line, self.parity = net, line, parity
        self.keep, self.send = keep, send
        self.part = [None] * 4

    def swap(self, number):
        self.part[number] = self.net.swap(self.line.pin(self.send[number]))

    def start(self):
        self.swap(3)
        self.swap(2)

    def wait(self):
        self.got = self.line.pin(self.got)

    def first(self):
        two, three = fold_pair(self.line, self.keep[2:], self.part[2:])
        self.got = self.net.cross(three, self.parity, 3)
        self.late = self.net.cross(two, self.parity, 3)
        self.swap(1)

    def second(self):
        self.wait()
        (held,) = fold(self.line, self.keep[1], (self.part[1], self.got), 1)
        self.got = self.net.cross(held, self.parity, 2)
        self.swap(0)

    def third(self):
        self.wait()
        self.late = self.line.pin(self.late)
        self.held, send = fold(self.line, self.keep[0], (self.part[0], self.late, self.got), 2)
        self.got = self.net.cross(send, self.parity, 1)

    def fourth(self):
        self.wait()
        self.held, send = fold(self.line, self.held, (self.got,), 2)
        self.got = self.net.cross(send, self.parity, 0)

    def finish(self):
        self.wait()
        self.mine, self.square = fold_last(self.line, self.held[0], self.got[0])
        self.other = self.net.swap(self.mine)


class SmallGather:
    def __init__(self, net, line, rows):
        self.net, self.line = net, line
        self.held = line.pin(rows)
        self.got = [net.swap(self.held)]

    def step(self, bits=()):
        got = [self.line.pin(array) for array in self.got]
        self.held = jnp.concatenate([self.held, *got], axis=0)
        self.got = [self.net.exchange(self.held, (bit, bit)) for bit in bits]


ANY = pl.BlockSpec(memory_space=pl.ANY)
SMEM = pl.BlockSpec(memory_space=pltpu.SMEM)
VMEM = pl.BlockSpec(memory_space=pltpu.VMEM)
NT = (((1,), (1,)), ((), ()))
TN = (((0,), (0,)), ((), ()))
VMEM_LIMIT = 56 * 1024 * 1024
SMALL_LIMIT = 16 * 1024 * 1024


def load_weight(table_ref, pieces, full_ref, sems):
    core = table_ref[32]
    rows = pieces[0].shape[1]
    copies = []
    for number, piece in enumerate(pieces):
        side = core if number < 4 else 1 - core
        for index in range(4):
            start = pl.multiple_of(table_ref[number * 4 + index] * (2 * rows) + side * rows, 16)
            copies.append(
                pltpu.make_async_copy(
                    piece.at[index], full_ref.at[pl.ds(start, rows)], sems.at[number, index]
                )
            )
    return copies


def part_of(pieces, first, size):
    return tuple(piece.at[:, :, first : first + size] for piece in pieces)


def fetch(copies):
    for copy in copies:
        copy.start()
    for copy in copies:
        copy.wait()


SEMS = pltpu.SemaphoreType.DMA((8, 4))


def params(dims):
    return pltpu.CompilerParams(
        dimension_semantics=("arbitrary",) * dims, vmem_limit_bytes=VMEM_LIMIT
    )


def cost(flops, size):
    return pl.CostEstimate(flops=flops, bytes_accessed=size, transcendentals=0)


def mul(a, b):
    return jnp.dot(a, b, preferred_element_type=WIDE)


def mul_nt(a, b):
    return lax.dot_general(a, b, NT, preferred_element_type=WIDE)


def mul_tn(a, b):
    return lax.dot_general(a, b, TN, preferred_element_type=WIDE)


def whole(shape):
    return pl.BlockSpec(shape, lambda *_: (0,) * len(shape))


def turned_block(width, seq):
    return pl.BlockSpec((width, seq), lambda i: (0, i))


def turned_shape(width, tokens):
    return jax.ShapeDtypeStruct((width, tokens), LOW)


def grouped(images):
    return 2 if images % 2 == 0 else 1


def scaled(values, scale_ref):
    count = scale_ref.shape[0]
    rows = values.shape[0] // count
    parts = [values[i * rows : i * rows + rows] * scale_ref[i] for i in range(count)]
    return parts[0] if count == 1 else jnp.concatenate(parts, axis=0)


def norm_back(grad, values, scale_ref, dscale_ref):
    inverse = lax.rsqrt(jnp.mean(values * values, axis=-1, keepdims=True) + NORM_EPS)
    normed = values * inverse
    product = grad * normed
    count = scale_ref.shape[0]
    rows = values.shape[0] // count
    for i in range(count):
        dscale_ref[i] = jnp.sum(product[i * rows : i * rows + rows], axis=0, keepdims=True)
    grad = scaled(grad, scale_ref)
    inner = jnp.mean(grad * normed, axis=-1, keepdims=True)
    return inverse * (grad - normed * inner)


def rotate(values, cos_rep, up_rep, down_rep, sign):
    ahead = pltpu.roll(values, values.shape[-1] - 16, 1)
    behind = pltpu.roll(values, 16, 1)
    turned = ahead * up_rep + behind * down_rep
    return values * cos_rep + (turned if sign > 0 else -turned)


def join_kernel(a_ref, b_ref, out_ref, sems):
    count = a_ref.shape[0]
    fetch(
        [
            pltpu.make_async_copy(a_ref, out_ref.at[:count], sems.at[0]),
            pltpu.make_async_copy(b_ref, out_ref.at[count:], sems.at[1]),
        ]
    )


def join(line, a, b):
    shape = (2 * a.shape[0],) + a.shape[1:]
    return line.call(
        join_kernel,
        (a, b),
        [ANY, ANY],
        out_specs=VMEM,
        out_shape=jax.ShapeDtypeStruct(shape, a.dtype),
        scratch_shapes=[pltpu.SemaphoreType.DMA((2,))],
        compiler_params=pltpu.CompilerParams(vmem_limit_bytes=SMALL_LIMIT),
        cost_estimate=cost(0, 4 * math.prod(shape)),
        name="join",
    )


def fold_kernel(count, held_ref, *refs):
    outs = refs[count:]
    total = held_ref[...].astype(WIDE)
    for ref in refs[:count]:
        total += ref[...].astype(WIDE)
    size = outs[0].shape[0]
    for number, out in enumerate(outs):
        out[...] = total[number * size : number * size + size].astype(out.dtype)


def fold(line, held, others, parts):
    shape = (held.shape[0] // parts,) + held.shape[1:]
    return line.call(
        functools.partial(fold_kernel, len(others)),
        (held, *others),
        [VMEM] * (1 + len(others)),
        out_specs=[VMEM] * parts,
        out_shape=[jax.ShapeDtypeStruct(shape, held.dtype)] * parts,
        compiler_params=pltpu.CompilerParams(vmem_limit_bytes=SMALL_LIMIT),
        cost_estimate=cost(0, 2 * math.prod(held.shape) * (2 + len(others))),
        name="fold",
    )


def fold_pair_kernel(a_ref, b_ref, c_ref, d_ref, first_ref, second_ref):
    first_ref[...] = (a_ref[...].astype(WIDE) + c_ref[...].astype(WIDE)).astype(LOW)
    second_ref[...] = (b_ref[...].astype(WIDE) + d_ref[...].astype(WIDE)).astype(LOW)


def fold_pair(line, held, others):
    shape = jax.ShapeDtypeStruct(held[0].shape, LOW)
    return line.call(
        fold_pair_kernel,
        (*held, *others),
        [VMEM] * 4,
        out_specs=[VMEM] * 2,
        out_shape=[shape] * 2,
        compiler_params=pltpu.CompilerParams(vmem_limit_bytes=SMALL_LIMIT),
        cost_estimate=cost(0, 12 * math.prod(shape.shape)),
        name="fold_pair",
    )


def fold_last_kernel(held_ref, other_ref, out_ref, square_ref):
    total = (held_ref[...].astype(WIDE) + other_ref[...].astype(WIDE)).astype(LOW)
    out_ref[...] = total
    total = total.astype(WIDE)
    sums = jnp.sum(jnp.sum(total * total, axis=0, keepdims=True), axis=1, keepdims=True)
    square_ref[...] = jnp.broadcast_to(sums, square_ref.shape)


def fold_last(line, held, other):
    return line.call(
        fold_last_kernel,
        (held, other),
        [VMEM, VMEM],
        out_specs=[VMEM, VMEM],
        out_shape=[jax.ShapeDtypeStruct(held.shape, LOW), jax.ShapeDtypeStruct((1, 128), WIDE)],
        compiler_params=pltpu.CompilerParams(vmem_limit_bytes=SMALL_LIMIT),
        cost_estimate=cost(0, 6 * math.prod(held.shape)),
        name="fold_last",
    )


def head_kernel(core_ref, qkv_ref, out_ref, ada_ref, *outs):
    rows, size = qkv_ref.shape[0], ada_ref.shape[2]
    for number, out in enumerate(outs):
        for block in range(4):
            at = (4 * number + block) * size
            past = at - qkv_ref.shape[1]
            values = qkv_ref[:, at : at + size] if past < 0 else out_ref[:, past : past + size]
            out[0, block * rows : block * rows + rows, :] = values.astype(LOW)
        out[0, 4 * rows :, :] = ada_ref[number].astype(LOW)


def head_parts(line, core, qkv, out, ada):
    rows, width = qkv.shape[0] // 2, out.shape[1]
    size = width // 2
    shape = (1, 4 * rows + ada.shape[1], size)
    return line.call(
        head_kernel,
        (core[None], qkv, out, ada),
        [pl.BlockSpec((rows, 3 * width), lambda i, c: (c[0], 0)),
         pl.BlockSpec((rows, width), lambda i, c: (c[0], 0)),
         pl.BlockSpec((2, ada.shape[1], size), lambda i, c: (0, 0, c[0]))],
        prefetch=1,
        grid=(1,),
        out_specs=[whole(shape)] * 2,
        out_shape=[jax.ShapeDtypeStruct(shape, LOW)] * 2,
        compiler_params=params(1),
        cost_estimate=cost(0, 2 << 20),
        name="head_parts",
    )


def load_head(table_ref, pieces, first, full_ref, sems, ada_ref=None, ada_sems=None):
    core = table_ref[32]
    size = pieces[0].shape[2]
    ada_rows = 0 if ada_ref is None else ada_ref.shape[0] // 16
    copies = []
    for number, piece in enumerate(pieces):
        side = core if number < 4 else 1 - core
        for index in range(4):
            owner = table_ref[number * 4 + index]
            start = pl.multiple_of(owner * 64 + side * 32, 16)
            for block in range(full_ref.shape[1] // size):
                copies.append(
                    pltpu.make_async_copy(
                        piece.at[index, (first + block) * 32 : (first + block) * 32 + 32],
                        full_ref.at[pl.ds(start, 32), block * size : block * size + size],
                        sems.at[block, number, index],
                    )
                )
            if ada_ref is not None:
                start = pl.multiple_of(owner * ada_rows, 16)
                column = pl.multiple_of(side * size, 128)
                copies.append(
                    pltpu.make_async_copy(
                        piece.at[index, piece.shape[1] - ada_rows :],
                        ada_ref.at[pl.ds(start, ada_rows), pl.ds(column, size)],
                        ada_sems.at[number, index],
                    )
                )
    return copies


def cut_kernel(core_ref, up_ref, down_ref, *outs):
    width = down_ref.shape[2]
    low = lax.broadcasted_iota(jnp.int32, (up_ref.shape[0], 128), 1) < 64
    for start in range(0, 2 * width, 128):
        first, second, third = (up_ref[:, 3 * start + 128 * i : 3 * start + 128 * i + 128] for i in range(3))
        lanes = slice(start, start + 128)
        outs[0][0, :, lanes] = jnp.where(low, first, second).astype(LOW)
        outs[1][0, :, lanes] = pltpu.roll(jnp.where(low, third, first), 64, 1).astype(LOW)
        outs[2][0, :, lanes] = jnp.where(low, second, third).astype(LOW)
    for part, out in enumerate(outs):
        out[0, :, 2 * width :] = down_ref[part].astype(LOW)


def cut_parts(line, core, up, down):
    rows, columns = up.shape[0] // 2, up.shape[1]
    width = down.shape[2]
    return line.call(
        cut_kernel,
        (core[None], up, down),
        [pl.BlockSpec((rows, columns), lambda i, c: (c[0], 0)),
         pl.BlockSpec((3, rows, width), lambda i, c: (0, c[0], 0))],
        prefetch=1,
        grid=(1,),
        out_specs=[whole((1, rows, 3 * width))] * 3,
        out_shape=[jax.ShapeDtypeStruct((1, rows, 3 * width), LOW)] * 3,
        compiler_params=params(1),
        cost_estimate=cost(0, 4 << 20),
        name="cut",
    )


def conditioned(cond_ref, ada_ref, out_ref):
    scale = 1.0 + mul(cond_ref[...], ada_ref[...])
    for image in range(scale.shape[0]):
        out_ref[image] = scale[image : image + 1]


def front_kernel(group, table_ref, x_ref, cond_ref, *rest):
    pieces, rest = rest[:8], rest[8:]
    sums_ref, spread_ref, root_ref, cos_ref, up_ref, down_ref, *rest = rest
    act_ref, q_ref, k_ref, pack_ref, one_ref, w_ref, ada_ref, sems, ada_sems = rest

    @pl.when(pl.program_id(0) == 0)
    def _():
        fetch(load_head(table_ref, pieces, 0, w_ref, sems, ada_ref, ada_sems))
        conditioned(cond_ref, ada_ref, one_ref)

    scale_ref = one_ref.at[pl.ds(pl.program_id(0) * group, group)]
    width = x_ref.shape[1]
    x = x_ref[...].astype(WIDE)
    inverse = lax.rsqrt(jnp.mean(x * x, axis=-1, keepdims=True) + NORM_EPS)
    act = scaled(x * inverse, scale_ref).astype(LOW)
    act_ref[...] = act.T
    q = mul(act, w_ref[:, :width])
    k = mul(act, w_ref[:, width:])
    sums = mul((q * q).astype(LOW), sums_ref[0]) + mul((k * k).astype(LOW), sums_ref[1])
    factor = lax.rsqrt(sums + COSINE_EPS)
    high = factor.astype(LOW)
    low = (factor - high.astype(WIDE)).astype(LOW)
    lane = lax.broadcasted_iota(jnp.int32, factor.shape, 1)
    pack = jnp.where(lane < 32, high.astype(WIDE), jnp.where(lane < 64, low.astype(WIDE), 0.0))
    pack = pack.astype(LOW)
    pack_ref[...] = pack
    q = q * mul(pack, spread_ref[0]) * root_ref[...]
    k = k * mul(pack, spread_ref[1]) * root_ref[...]
    cos_rep, up_rep, down_rep = cos_ref[...], up_ref[...], down_ref[...]
    for pair in range(width // 128):
        lanes = slice(pair * 128, pair * 128 + 128)
        q_ref[:, lanes] = rotate(q[:, lanes], cos_rep, up_rep, down_rep, 1).astype(LOW)
        k_ref[:, lanes] = rotate(k[:, lanes], cos_rep, up_rep, down_rep, 1).astype(LOW)


def front(line, table, x, cond, pieces, sums, spread, root, turns, images):
    tokens, width = x.shape
    group = grouped(images)
    seq = tokens // images * group
    row = pl.BlockSpec((seq, width), lambda i: (i, 0))
    narrow = pl.BlockSpec((seq, 128), lambda i: (i, 0))
    full = jax.ShapeDtypeStruct((tokens, width), LOW)
    return line.call(
        functools.partial(front_kernel, group),
        (table, x, cond, *pieces, sums, spread, root, *turns),
        [SMEM, row, whole(cond.shape), *[ANY] * 8,
                  whole(sums.shape), whole(spread.shape), whole(root.shape), narrow, narrow, narrow],
        grid=(images // group,),
        out_specs=[turned_block(width, seq), row, row, narrow, whole((images, 1, width))],
        out_shape=[turned_shape(width, tokens), full, full, jax.ShapeDtypeStruct((tokens, 128), LOW),
                   jax.ShapeDtypeStruct((images, 1, width), WIDE)],
        scratch_shapes=[pltpu.VMEM((width, 2 * width), LOW), pltpu.VMEM((cond.shape[1], width), LOW),
                        pltpu.SemaphoreType.DMA((4, 8, 4)), SEMS],
        compiler_params=params(1),
        cost_estimate=cost(4 * tokens * width * width, 20 << 20),
        name="front",
    )


def attend_kernel(table_ref, q_ref, k_ref, valid_ref, x_ref, scale_ref, *rest):
    pieces = rest[:8]
    v_ref, o_ref, turned_ref, lse_ref, w_ref, sems = rest[8:]

    @pl.when(pl.program_id(0) == 0)
    def _():
        fetch(load_head(table_ref, pieces, 0, w_ref, sems))

    x = x_ref[...].astype(WIDE)
    inverse = lax.rsqrt(jnp.mean(x * x, axis=-1, keepdims=True) + NORM_EPS)
    act = scaled(x * inverse, scale_ref).astype(LOW)
    v_ref[...] = mul(act, w_ref[...]).astype(LOW)
    seq, width = q_ref.shape
    valid = valid_ref[...]
    lane = lax.broadcasted_iota(jnp.int32, (seq, 128), 1)
    first = lane < 64
    totals = jnp.zeros((seq, 128), WIDE)
    zero = jnp.zeros((seq, 128), LOW)
    for pair in range(width // 128):
        lanes = slice(pair * 128, pair * 128 + 128)
        q, k = q_ref[:, lanes], k_ref[:, lanes]
        v = v_ref[:, lanes] * valid
        mixed = None
        for half in range(2):
            pick = first if half == 0 else jnp.logical_not(first)
            scores = mul_nt(jnp.where(pick, q, zero), k)
            weights = jnp.exp(scores).astype(LOW)
            right = jnp.concatenate([jnp.where(pick, v, zero), valid], axis=1)
            both = mul(weights, right)
            total = both[:, 128:]
            part = both[:, :128] / total
            mixed = part if mixed is None else mixed + part
            totals = jnp.where(lane == 2 * pair + half, total, totals)
        mixed = mixed.astype(LOW)
        o_ref[:, lanes] = mixed
        turned_ref[lanes, :] = mixed.T
    lane_ok = lane < width // 64
    lse = jnp.log(jnp.where(lane_ok, totals, 1.0))
    lse_ref[0] = lse.T[: width // 64]


def attend(line, table, q, k, valid, x, scale, pieces, images):
    tokens, width = q.shape
    seq = tokens // images
    row = pl.BlockSpec((seq, width), lambda i: (i, 0))
    heads = width // 64
    low = jax.ShapeDtypeStruct((tokens, width), LOW)
    return line.call(
        attend_kernel,
        (table, q, k, valid, x, scale, *pieces),
        [SMEM, row, row, pl.BlockSpec((seq, 128), lambda i: (i, 0)), row,
         pl.BlockSpec((1, 1, width), lambda i: (i, 0, 0))] + [ANY] * 8,
        grid=(images,),
        out_specs=[row, row, turned_block(width, seq), pl.BlockSpec((1, heads, seq), lambda i: (i, 0, 0))],
        out_shape=[low, low, turned_shape(width, tokens),
                   jax.ShapeDtypeStruct((images, heads, seq), WIDE)],
        scratch_shapes=[pltpu.VMEM((width, width), LOW), pltpu.SemaphoreType.DMA((2, 8, 4))],
        compiler_params=params(1),
        cost_estimate=cost(16 * tokens * seq * width, 12 << 20),
        name="attend",
    )


def middle_kernel(group, table_ref, o_ref, x_ref, cond_ref, *rest):
    pieces = rest[:8]
    mid_ref, act_ref, turned_ref, two_ref, w_ref, ada_ref, sems, ada_sems = rest[8:]

    @pl.when(pl.program_id(0) == 0)
    def _():
        fetch(load_head(table_ref, pieces, 2, w_ref, sems, ada_ref, ada_sems))
        conditioned(cond_ref, ada_ref, two_ref)

    scale_ref = two_ref.at[pl.ds(pl.program_id(0) * group, group)]
    mid = x_ref[...].astype(WIDE) + mul(o_ref[...], w_ref[...])
    mid_ref[...] = mid
    inverse = lax.rsqrt(jnp.mean(mid * mid, axis=-1, keepdims=True) + NORM_EPS)
    act = scaled(mid * inverse, scale_ref).astype(LOW)
    act_ref[...] = act
    turned_ref[...] = act.T


def middle_block(line, table, o, x, cond, pieces, images):
    tokens, width = x.shape
    group = grouped(images)
    seq = tokens // images * group
    row = pl.BlockSpec((seq, width), lambda i: (i, 0))
    return line.call(
        functools.partial(middle_kernel, group),
        (table, o, x, cond, *pieces),
        [SMEM, row, row, whole(cond.shape)] + [ANY] * 8,
        grid=(images // group,),
        out_specs=[row, row, turned_block(width, seq), whole((images, 1, width))],
        out_shape=[jax.ShapeDtypeStruct((tokens, width), WIDE), jax.ShapeDtypeStruct((tokens, width), LOW),
                   turned_shape(width, tokens), jax.ShapeDtypeStruct((images, 1, width), WIDE)],
        scratch_shapes=[pltpu.VMEM((width, width), LOW), pltpu.VMEM((cond.shape[1], width), LOW),
                        pltpu.SemaphoreType.DMA((2, 8, 4)), SEMS],
        compiler_params=params(1),
        cost_estimate=cost(2 * tokens * width * width, 12 << 20),
        name="middle",
    )


def part_kernel(first, last, table_ref, act_ref, dy_ref, *rest):
    rest = list(rest)
    pieces = tuple(rest.pop(0) for _ in range(8))
    if last:
        mid_ref, scale_ref, out_table_ref = rest.pop(0), rest.pop(0), rest.pop(0)
        out_pieces = tuple(rest.pop(0) for _ in range(8))
    acc_ref = None if first else rest.pop(0)
    hid_ref, dgu_ref, turned_ref = rest.pop(0), rest.pop(0), rest.pop(0)
    if last:
        dmid_ref, db_ref, do_ref, dscale_ref = (rest.pop(0) for _ in range(4))
    else:
        da_ref = rest.pop(0)
    w_ref, sems = rest.pop(0), rest.pop(0)
    if last:
        out_ref, sems_out = rest.pop(0), rest.pop(0)

    @pl.when(pl.program_id(0) == 0)
    def _():
        copies = load_weight(table_ref, pieces, w_ref, sems)
        if last:
            copies = copies + load_head(out_table_ref, out_pieces, 2, out_ref, sems_out)
        fetch(copies)

    width = act_ref.shape[1]
    act, dy = act_ref[...], dy_ref[...]
    size = 512
    for start in range(0, width, size):
        cols = slice(start, start + size)
        above = slice(width + start, width + start + size)
        gate = mul(act, w_ref[:, cols])
        upper = mul(act, w_ref[:, above])
        grad = mul_nt(dy, w_ref[start : start + size, 2 * width :]).astype(LOW).astype(WIDE)
        cdf = 0.5 * (1.0 + lax.erf(gate * math.sqrt(0.5)))
        bell = jnp.exp(-0.5 * gate * gate) * (1.0 / math.sqrt(2.0 * math.pi))
        gelu = gate * cdf
        hid = (gelu * upper).astype(LOW)
        hid_ref[:, cols] = hid
        turned_ref[cols, :] = hid.T
        dgu_ref[:, cols] = (grad * upper * (cdf + gate * bell)).astype(LOW)
        dgu_ref[:, above] = (grad * gelu).astype(LOW)
    total = mul_nt(dgu_ref[:, :width], w_ref[:, :width])
    total += mul_nt(dgu_ref[:, width:], w_ref[:, width : 2 * width])
    if not first:
        total += acc_ref[...]
    if not last:
        da_ref[...] = total
        return
    dmid = dy.astype(WIDE) + norm_back(total, mid_ref[...], scale_ref, dscale_ref)
    dmid_ref[...] = dmid
    low = dmid.astype(LOW)
    db_ref[...] = low
    do_ref[...] = mul_nt(low, out_ref[...]).astype(LOW)


def geglu_part(line, table, act, dy, pieces, images, acc=None, final=None):
    tokens, width = act.shape
    group = grouped(images)
    seq = tokens // images * group
    first, last = acc is None, final is not None
    row = pl.BlockSpec((seq, width), lambda i: (i, 0))
    one = pl.BlockSpec((group, 1, width), lambda i: (i, 0, 0))
    args = [table, act, dy, *pieces]
    in_specs = [SMEM, row, row] + [ANY] * 8
    if last:
        mid, scale, out_table, out_pieces = final
        args += [mid, scale, out_table, *out_pieces]
        in_specs += [row, one, SMEM] + [ANY] * 8
    if not first:
        args.append(acc)
        in_specs.append(row)
    low = jax.ShapeDtypeStruct((tokens, width), LOW)
    wide = jax.ShapeDtypeStruct((tokens, width), WIDE)
    out_specs = [row, pl.BlockSpec((seq, 2 * width), lambda i: (i, 0)), turned_block(width, seq)]
    out_shape = [low, jax.ShapeDtypeStruct((tokens, 2 * width), LOW), turned_shape(width, tokens)]
    scratch = [pltpu.VMEM((width, 3 * width), LOW), SEMS]
    if last:
        out_specs += [row, row, row, one]
        out_shape += [wide, low, low, jax.ShapeDtypeStruct((images, 1, width), WIDE)]
        scratch += [pltpu.VMEM((width, width), LOW), pltpu.SemaphoreType.DMA((2, 8, 4))]
    else:
        out_specs.append(row)
        out_shape.append(wide)
    return line.call(
        functools.partial(part_kernel, first, last),
        args,
        in_specs,
        grid=(images // group,),
        out_specs=out_specs,
        out_shape=out_shape,
        scratch_shapes=scratch,
        compiler_params=params(1),
        cost_estimate=cost((12 if last else 10) * tokens * width * width, 30 << 20),
        name="geglu_part",
    )


def attend_back_kernel(q_ref, k_ref, v_ref, o_ref, do_ref, lse_ref, valid_ref, pack_ref, spread_ref,
                       root_ref, pick_ref, block_ref, cos_ref, up_ref, down_ref, dproj_ref, dhead_ref,
                       grad_ref, product_ref, inner_ref):
    seq, width = q_ref.shape
    valid = valid_ref[...]
    valid_wide = valid.astype(WIDE)
    first = lax.broadcasted_iota(jnp.int32, (seq, 128), 1) < 64
    zero = jnp.zeros((seq, 128), LOW)
    cos_rep, up_rep, down_rep = cos_ref[...], up_ref[...], down_ref[...]
    product = (do_ref[...].astype(WIDE) * o_ref[...].astype(WIDE)).astype(LOW)
    delta = mul_nt(pick_ref[...], product)
    pack = pack_ref[...]
    block = block_ref[...]
    head_lane = lax.broadcasted_iota(jnp.int32, (1, 128), 1)
    row = jnp.zeros((1, 128), WIDE)
    for pair in range(width // 128):
        lanes = slice(pair * 128, pair * 128 + 128)
        q, k, v, do = q_ref[:, lanes], k_ref[:, lanes], v_ref[:, lanes], do_ref[:, lanes]
        k_turned = (k * valid).T
        picks = (first, jnp.logical_not(first))
        q_ones = [jnp.where(pick, q, zero) for pick in picks]
        do_ones = [jnp.where(pick, do, zero) for pick in picks]
        scores = [mul_nt(k, one) for one in q_ones]
        grads = [mul_nt(v, one) for one in do_ones]
        lows, dscores = [], []
        for half in range(2):
            head = 2 * pair + half
            weights = jnp.exp(scores[half] - lse_ref[0, head : head + 1, :])
            lows.append(weights.astype(LOW))
            dscores.append((weights * (grads[half] - delta[head : head + 1, :])).astype(LOW))
        dv = mul(jnp.concatenate(lows, axis=1), jnp.concatenate(do_ones, axis=0))
        dk = mul(jnp.concatenate(dscores, axis=1), jnp.concatenate(q_ones, axis=0))
        dq_parts = [mul(k_turned[half * 64 : half * 64 + 64], dscores[half]) for half in range(2)]
        dq = jnp.concatenate(dq_parts, axis=0).T
        dk = dk * valid_wide
        dproj_ref[:, 2 * width + pair * 128 : 2 * width + pair * 128 + 128] = (dv * valid_wide).astype(LOW)
        for side, (grad, value) in enumerate(((dq, q), (dk, k))):
            at = (side * (width // 128) + pair) * seq
            grad_ref[side, :, lanes] = grad
            product_ref[at : at + seq, :] = (grad * value.astype(WIDE)).astype(LOW)
    inner_ref[...] = mul(product_ref[...], block)
    factors = [mul(pack, spread_ref[side]) for side in range(2)]
    for pair in range(width // 128):
        lanes = slice(pair * 128, pair * 128 + 128)
        root = root_ref[:, lanes]
        total = 0.0
        for side, value_ref in enumerate((q_ref, k_ref)):
            at = (side * (width // 128) + pair) * seq
            inner = inner_ref[at : at + seq, :]
            total = total + jnp.sum(inner, axis=0, keepdims=True)
            back = root * grad_ref[side, :, lanes] - value_ref[:, lanes].astype(WIDE) * (inner / root)
            back = rotate(factors[side][:, lanes] * back, cos_rep, up_rep, down_rep, -1)
            dproj_ref[:, side * width + pair * 128 : side * width + pair * 128 + 128] = back.astype(LOW)
        row = jnp.where(head_lane == 2 * pair, total[:, :1], row)
        row = jnp.where(head_lane == 2 * pair + 1, total[:, 64:65], row)
    dhead_ref[0] = row


def attend_back(line, q, k, v, o, do, lse, valid, pack, spread, root, pick, block, turns, images):
    tokens, width = q.shape
    seq = tokens // images
    heads = width // 64
    row = pl.BlockSpec((seq, width), lambda i: (i, 0))
    narrow = pl.BlockSpec((seq, 128), lambda i: (i, 0))
    return line.call(
        attend_back_kernel,
        (q, k, v, o, do, lse, valid, pack, spread, root, pick, block, *turns),
        [row, row, row, row, row, pl.BlockSpec((1, heads, seq), lambda i: (i, 0, 0)), narrow, narrow,
                  whole(spread.shape), whole(root.shape), whole(pick.shape), whole(block.shape),
                  narrow, narrow, narrow],
        grid=(images,),
        out_specs=[pl.BlockSpec((seq, 3 * width), lambda i: (i, 0)),
                   pl.BlockSpec((1, 1, 128), lambda i: (i, 0, 0))],
        out_shape=[jax.ShapeDtypeStruct((tokens, 3 * width), LOW),
                   jax.ShapeDtypeStruct((images, 1, 128), WIDE)],
        scratch_shapes=[pltpu.VMEM((2, seq, width), WIDE), pltpu.VMEM((width // 64 * seq, 128), LOW),
                        pltpu.VMEM((width // 64 * seq, 128), WIDE)],
        compiler_params=params(1),
        cost_estimate=cost(40 * tokens * seq * width, 20 << 20),
        name="attend_back",
    )


def input_kernel(even_ref, odd_ref, dproj_ref, x_ref, dmid_ref, scale_ref, *rest):
    pieces = rest[:16]
    out_ref, dscale_ref, w_ref, sems = rest[16:]

    width = x_ref.shape[1]
    copies = [
        load_head(even_ref, pieces[:8], 0, w_ref.at[:, :width], sems.at[:2]),
        load_head(even_ref, pieces[:8], 2, w_ref.at[:, width : 2 * width], sems.at[2:4]),
        load_head(odd_ref, pieces[8:], 0, w_ref.at[:, 2 * width :], sems.at[4:]),
    ]
    for copy in sum(copies, []):
        copy.start()
    grad = None
    for part in range(3):
        for copy in copies[part]:
            copy.wait()
        cols = slice(part * width, part * width + width)
        add = mul_nt(dproj_ref[:, cols], w_ref[:, cols])
        grad = add if grad is None else grad + add
    x = x_ref[...].astype(WIDE)
    out_ref[...] = (dmid_ref[...] + norm_back(grad, x, scale_ref, dscale_ref)).astype(LOW)


def input_block(line, tables, dproj, x, dmid, scale, pieces, images, place, places, into):
    tokens, width = x.shape
    group = grouped(images)
    seq = tokens // images * group
    steps = images // group // places
    row = pl.BlockSpec((seq, width), lambda i: (place * steps + i, 0))
    one = pl.BlockSpec((group, 1, width), lambda i: (place * steps + i, 0, 0))
    return line.call(
        input_kernel,
        (*tables, dproj, x, dmid, scale, *pieces),
        [SMEM, SMEM, pl.BlockSpec((seq, 3 * width), lambda i: (place * steps + i, 0)), row, row, one] + [ANY] * 16,
        into=into,
        grid=(steps,),
        out_specs=[row,
                   pl.BlockSpec((group, 1, width), lambda i: (i, 0, 0))],
        out_shape=[jax.ShapeDtypeStruct((tokens, width), LOW),
                   jax.ShapeDtypeStruct((images // places, 1, width), WIDE)],
        scratch_shapes=[pltpu.VMEM((width, 3 * width), LOW), pltpu.SemaphoreType.DMA((6, 8, 4))],
        compiler_params=params(1),
        cost_estimate=cost(6 * tokens * width * width // places, 24 << 20),
        name="input_grad",
    )


def result_kernel(even_ref, odd_ref, h0, h1, h2, mid_ref, *rest):
    pieces, out_ref, w_ref, sems = rest[:24], rest[24], rest[25], rest[26]
    width = mid_ref.shape[1]
    copies = []
    for part in range(3):
        ref = pieces[8 * part : 8 * part + 8]
        down = tuple(piece.at[:, :, 2 * width : 3 * width] for piece in ref)
        table_ref = odd_ref if part % 2 == 0 else even_ref
        copies.append(load_weight(table_ref, down, w_ref.at[part], sems.at[part]))
    for copy in sum(copies, []):
        copy.start()
    total = mid_ref[...]
    for part, hid_ref in enumerate((h0, h1, h2)):
        for copy in copies[part]:
            copy.wait()
        total += mul(hid_ref[...], w_ref[part])
    out_ref[...] = total.astype(LOW)


def result_block(line, tables, hids, mid, pieces, images, place, places, into):
    tokens, width = mid.shape
    group = grouped(images)
    seq = tokens // images * group
    steps = images // group // places
    row = pl.BlockSpec((seq, width), lambda i: (place * steps + i, 0))
    return line.call(
        result_kernel,
        (*tables, *hids, mid, *[piece for part in pieces for piece in part]),
        [SMEM, SMEM, row, row, row, row] + [ANY] * 24,
        grid=(steps,),
        into=into,
        out_specs=row,
        out_shape=jax.ShapeDtypeStruct((tokens, width), LOW),
        scratch_shapes=[pltpu.VMEM((3, width, width), LOW), pltpu.SemaphoreType.DMA((3, 8, 4))],
        compiler_params=params(1),
        cost_estimate=cost(6 * tokens * width * width, 20 << 20),
        name="result",
    )


def weight_kernel(lefts, table_ref, *refs):
    refs = list(refs)
    acts = [refs.pop(0) for _ in range(max(lefts) + 1)]
    grads = [refs.pop(0) for _ in lefts]
    outs = [refs.pop(0) for _ in range(8)]
    turned_ref, sems = refs
    rows = outs[0].shape[1]
    half = outs[0].shape[2]
    depth = turned_ref.shape[1]
    core = table_ref[32]
    step = pl.program_id(0)

    def copy(number, index):
        start = pl.multiple_of(index * 4 * rows, 16)
        return pltpu.make_async_copy(
            acts[number].at[pl.ds(start, 4 * rows)],
            turned_ref.at[number, index * 4 * rows : index * 4 * rows + 4 * rows],
            sems.at[number, index],
        )

    @pl.when(step == 0)
    def _():
        for number in range(len(acts)):
            for index in range(4):
                copy(number, index).start()

    for span, (left, grad_ref) in enumerate(zip(lefts, grads)):
        @pl.when(step == span)
        def _(span=span, left=left, grad_ref=grad_ref):
            if left not in lefts[:span]:
                for index in range(4):
                    copy(left, index).wait()
            for side in range(2):
                start = pl.multiple_of((core if side == 0 else 1 - core) * half, half)
                grad = grad_ref[:, pl.ds(start, half)]
                for pair in range(2):
                    parts = []
                    for index in range(8):
                        start = table_ref[side * 16 + pair * 8 + index] * rows
                        parts.append(turned_ref[left, pl.ds(pl.multiple_of(start, 16), rows), :])
                    total = mul(jnp.concatenate(parts, axis=0), grad)
                    for place in range(2):
                        out = outs[4 * side + 2 * pair + place]
                        part = total[place * 4 * rows : (place + 1) * 4 * rows]
                        out[...] = part.reshape(out.shape).astype(LOW)


def weight_halves(line, table, acts, spans):
    depth, tokens = acts[0].shape
    rows = depth // 16
    wide = spans[0][1].shape[1] // spans[0][3]
    half = wide // 2
    count = len(spans)

    def grad_spec(number, span):
        return pl.BlockSpec((tokens, wide), lambda m, t: (0, span))

    tile = pl.BlockSpec((4, rows, half), lambda m, t: (0, 0, m))
    shape = jax.ShapeDtypeStruct((4, rows, count * half), LOW)
    size = 2 * (tokens * (len(acts) * depth + count * wide) + depth * count * wide)
    outs = line.call(
        functools.partial(weight_kernel, [span[0] for span in spans]),
        (table, *acts, *[span[1] for span in spans]),
        [ANY for _ in acts] + [grad_spec(number, span[2]) for number, span in enumerate(spans)],
        prefetch=1,
        grid=(count,),
        out_specs=[tile] * 8,
        out_shape=[shape] * 8,
        scratch_shapes=[
            pltpu.VMEM((len(acts), depth, tokens), LOW), pltpu.SemaphoreType.DMA((len(acts), 4))
        ],
        compiler_params=params(1),
        cost_estimate=cost(2 * tokens * depth * count * wide, size),
        name="weight_grad",
    )
    return outs[:4], outs[4:]


def adam(weight, first, second, gradient, factor, rate, decay):
    clipped = gradient * factor
    new_first = BETA_ONE * first + (1.0 - BETA_ONE) * clipped
    new_second = BETA_TWO * second + (1.0 - BETA_TWO) * clipped * clipped
    denominator = jnp.sqrt(new_second / (1.0 - BETA_TWO**STEP)) + ADAM_EPS
    new_weight = (
        weight * (1.0 - rate * decay) - rate * (new_first / (1.0 - BETA_ONE**STEP)) / denominator
    )
    return (new_weight, new_first, new_second)


def adam_kernel(core_ref, total_ref, *refs):
    refs = list(refs)
    ada, qkv, out, up, down, scale = ([refs.pop(0) for _ in range(3)] for _ in range(6))
    ada_grad, head_grad = refs.pop(0), refs.pop(0)
    mines = [refs.pop(0) for _ in range(4)]
    others = [refs.pop(0) for _ in range(4)]
    norm_ref = refs.pop(0)
    new_ada, new_qkv, new_out, new_up, new_down, new_scale = ([refs.pop(0) for _ in range(3)] for _ in range(6))
    own_first = core_ref[0] == 0
    head = head_grad[...]
    total = total_ref[0:1, 0:1] + jnp.sum(head * head, axis=1, keepdims=True)
    norm = jnp.sqrt(total)
    factor = jnp.minimum(1.0, CLIP / (norm + 1e-06))

    def update(news, olds, at, gradient, rate, decay):
        weight, first, second = (ref[at] for ref in olds)
        for ref, value in zip(news, adam(weight, first, second, gradient, factor, rate, decay)):
            ref[at] = value

    @pl.when(pl.program_id(0) == 0)
    def _():
        norm_ref[...] = jnp.broadcast_to(norm, norm_ref.shape)
        update(new_scale, scale, (slice(None),) * 2, head, SCALE_RATE, 0.0)
        for index in range(ada_grad.shape[0]):
            update(new_ada, ada, (index,), ada_grad[index], RATE, DECAY)

    def columns(number, span):
        size = mines[0].shape[1] // 3
        mine = mines[number][:, span * size : span * size + size].astype(WIDE)
        other = others[number][:, span * size : span * size + size].astype(WIDE)
        return jnp.where(own_first, mine, other), jnp.where(own_first, other, mine)

    def by_halves(news, olds, number, spans, rate):
        for place, span in enumerate(spans):
            for half, gradient in enumerate(columns(number, span)):
                size = gradient.shape[1]
                start = (2 * place + half) * size
                update(news, olds, (slice(None), slice(start, start + size)), gradient, rate, DECAY)

    by_halves(new_qkv, qkv, 3, (0, 1, 2), RATE)
    by_halves(new_out, out, 2, (3,), OUTPUT_RATE)
    for part in range(3):
        for half, gradient in enumerate(columns(part, 2)):
            size = gradient.shape[1]
            update(new_down, down, (part, slice(None), slice(half * size, half * size + size)), gradient, RATE, DECAY)
    low = lax.broadcasted_iota(jnp.int32, (up[0].shape[0], 128), 1) < 64
    for span in range(2):
        parts = [columns(part, span) for part in range(3)]
        size = parts[0][0].shape[1]
        for half in range(2):
            for lane in range(0, size, 128):
                one, two, three = (parts[part][half][:, lane : lane + 128] for part in range(3))
                turned = pltpu.roll(two, 64, 1)
                start = 3 * ((2 * span + half) * size + lane)
                pieces = (jnp.where(low, one, turned), jnp.where(low, three, one), jnp.where(low, turned, three))
                for number, gradient in enumerate(pieces):
                    at = (slice(None), slice(start + 128 * number, start + 128 * number + 128))
                    update(new_up, up, at, gradient, RATE, DECAY)


def adam_all(line, core, total, ada, qkv, out, up, down, scale, ada_grad, head_grad, mines, others):
    steps = 4
    args = [core[None], total]
    in_specs = [SMEM, whole(total.shape)]
    out_specs = [whole(total.shape)]
    out_shape = [jax.ShapeDtypeStruct(total.shape, WIDE)]

    def by_rows(array):
        shape = array.shape[:-2] + (array.shape[-2] // steps, array.shape[-1])
        lead = (0,) * (array.ndim - 2)
        return pl.BlockSpec(shape, lambda i: lead + (i, 0))

    for group, cut in ((ada, False), (qkv, True), (out, True), (up, True), (down, True), (scale, False)):
        for array in group:
            spec = by_rows(array) if cut else whole(array.shape)
            args.append(array)
            in_specs.append(spec)
            out_specs.append(spec)
            out_shape.append(jax.ShapeDtypeStruct(array.shape, WIDE))
    args += [ada_grad, head_grad, *mines, *others]
    in_specs += [whole(ada_grad.shape), whole(head_grad.shape)] + [by_rows(m) for m in (*mines, *others)]
    return line.call(
        adam_kernel,
        args,
        in_specs,
        grid=(steps,),
        out_specs=out_specs,
        out_shape=out_shape,
        compiler_params=params(1),
        cost_estimate=cost(0, 30 << 20),
        name="adamw",
    )


def turn_kernel(shapes_ref, rates_ref, cos_ref, up_ref, down_ref, valid_ref):
    image = pl.program_id(0)
    height, width = shapes_ref[image, 0], shapes_ref[image, 1]
    shape = cos_ref.shape
    slot = lax.broadcasted_iota(jnp.int32, shape, 0)
    place = slot.astype(WIDE)
    wide = width.astype(WIDE)
    row = jnp.floor((place + 0.5) / wide)
    angle = row * rates_ref[0:1, :] + (place - row * wide) * rates_ref[1:2, :]
    lane = lax.broadcasted_iota(jnp.int32, shape, 1) % 64
    cosine, sine = jnp.cos(angle), jnp.sin(angle)
    cos_ref[...] = jnp.where(lane < 32, cosine, 1.0)
    up_ref[...] = jnp.where(lane < 16, -sine, 0.0)
    down_ref[...] = jnp.where((lane >= 16) & (lane < 32), sine, 0.0)
    valid_ref[...] = jnp.where(slot < height * width, 1.0, 0.0).astype(LOW)


def turn_tables(line, shapes, seq_len, head_dim):
    images = shapes.shape[0]
    count = head_dim // 8
    frequency = ROPE_BASE ** (-jnp.arange(count, dtype=WIDE) / count)
    none = jnp.zeros((count,), WIDE)
    blank = jnp.zeros((head_dim // 2,), WIDE)
    rates = jnp.stack(
        [
            jnp.concatenate([frequency, none, frequency, none, blank] * 2),
            jnp.concatenate([none, frequency, none, frequency, blank] * 2),
        ]
    )
    block = pl.BlockSpec((seq_len, 128), lambda i: (i, 0))
    wide = jax.ShapeDtypeStruct((images * seq_len, 128), WIDE)
    *turns, valid = line.call(
        turn_kernel,
        (shapes, rates),
        [SMEM, whole(rates.shape)],
        grid=(images,),
        out_specs=[block] * 4,
        out_shape=[wide, wide, wide, jax.ShapeDtypeStruct(wide.shape, LOW)],
        compiler_params=params(1),
        cost_estimate=cost(0, 2 << 20),
        name="turns",
    )
    return tuple(turns), valid


def head_matrices(width, head_dim):
    heads = width // head_dim
    owner = np.arange(width) // head_dim
    sums = np.zeros((2, width, 128), np.float32)
    spread = np.zeros((2, 128, width), np.float32)
    for side in range(2):
        for copy in range(2):
            sums[side, np.arange(width), side * heads + copy * 2 * heads + owner] = 1.0
            spread[side, side * heads + copy * 2 * heads + owner, np.arange(width)] = 1.0
    pick = np.zeros((heads, width), np.float32)
    pick[owner, np.arange(width)] = 1.0
    block = np.kron(np.eye(128 // head_dim), np.ones((head_dim, head_dim)))
    return tuple(jnp.asarray(m, LOW) for m in (sums, spread, pick, block))


def finish_wide(net, ada, qkv, out, up, down, scale, grad_ada, head_grad, mines, others):
    def columns(number, span):
        size = mines[0].shape[1] // 3
        mine = mines[number][:, span * size : span * size + size]
        other = others[number][:, span * size : span * size + size]
        pair = [jnp.where(net.core == 0, mine, other), jnp.where(net.core == 0, other, mine)]
        return jnp.concatenate(pair, axis=1).astype(WIDE)

    grad_up = [
        jnp.concatenate([columns(part, span) for span in range(2)], axis=1).reshape(-1, 2, 16, 64)
        for part in range(3)
    ]
    gradients = [
        jnp.concatenate([columns(3, span) for span in range(3)], axis=1),
        columns(2, 3),
        jnp.stack(grad_up, axis=3).reshape(-1, up[0].shape[1]),
        jnp.concatenate([columns(part, 2) for part in range(3)], axis=0),
    ]
    gradients = [grad_ada] + [net.split_sub(gradient) for gradient in gradients]
    total = lax.psum(sum(jnp.sum(gradient * gradient) for gradient in gradients), "fsdp")
    head_grad = head_grad[0]
    norm = jnp.sqrt(total + jnp.sum(head_grad * head_grad))
    factor = jnp.minimum(1.0, CLIP / (norm + 1e-06))
    rates = (RATE, RATE, OUTPUT_RATE, RATE, RATE)
    news = [norm]
    for group, gradient, rate in zip((ada, qkv, out, up, down), gradients, rates):
        news += adam(*group, gradient, factor, rate, DECAY)
    news += adam(*scale, head_grad, factor, SCALE_RATE, 0.0)
    return tuple(news)


def local(
    tokens,
    condition,
    shapes,
    cotangent,
    ada_weight,
    ada_first,
    ada_second,
    qkv_weight,
    qkv_first,
    qkv_second,
    out_weight,
    out_first,
    out_second,
    up_weight,
    up_first,
    up_second,
    down_weight,
    down_first,
    down_second,
    head_scale,
    scale_first,
    scale_second,
    *,
    dp_size,
    fsdp_size,
):
    net = Net(fsdp_size, dp_size)
    line = Line()
    core = net.core
    images = shapes.shape[0]
    width = tokens.shape[1]
    seq_len = tokens.shape[0] // images
    head_count = head_scale.shape[0]
    head_dim = width // head_count
    small = net.sub == 1
    even, odd = net.tables

    ada_joined = net.join_sub(ada_weight.transpose(1, 0, 2)).transpose(1, 0, 2) if net.sub > 1 else ada_weight
    half_qk, half_vo = head_parts(
        line, core, net.join_sub(qkv_weight), net.join_sub(out_weight), ada_joined
    )
    get_qk = Gather(net, line, 0, half_qk)
    down_joined = net.join_sub(down_weight).reshape(3, -1, width)
    halves = cut_parts(line, core, net.join_sub(up_weight), down_joined)
    get_qk.second()
    get_vo = Gather(net, line, 1, half_vo)
    turns, valid = turn_tables(line, shapes, seq_len, head_dim)
    sums, spread, pick, block = head_matrices(width, head_dim)
    root = jnp.repeat(jnp.sqrt(head_scale), head_dim)[None]
    get_vo.wait()
    get_qk.third()
    get_vo.second()
    get_vo.wait()
    get_qk.wait_near()
    get_vo.third()
    get_qk.fourth()
    get_mlp = [Gather(net, line, 1, halves[0])]
    get_qk.wait_last()
    get_mlp[0].second()
    get_mlp.append(Gather(net, line, 0, halves[1]))
    get_qk.finish()

    act_one, q, k, pack, scale_one = front(
        line, even, tokens, condition, get_qk.pieces, sums, spread, root, turns, images
    )
    get_mlp[0].third()
    get_vo.fourth()
    get_vo.finish()
    v, o, o_turned, lse = attend(
        line, odd, q, k, valid, tokens, scale_one, get_vo.pieces, images
    )
    get_mlp[1].second()
    get_mlp[0].fourth()
    mid, act_two, act_two_turned, scale_two = middle_block(
        line, odd, o, tokens, condition, get_vo.pieces, images
    )
    get_mlp[1].third()
    get_mlp[0].finish()
    get_mlp.append(Gather(net, line, 1, halves[2]))

    def put(parity, acts, spans):
        return Scatter(net, line, parity, *weight_halves(line, net.tables[parity], acts, spans))

    def mlp_spans(hid_turned, dgu):
        return ((act_two_turned, hid_turned), ((0, dgu, 0, 2), (0, dgu, 1, 2), (1, cotangent, 0, 1)))

    hid0, dgu0, turned0, acc = geglu_part(line, odd, act_two, cotangent, get_mlp[0].pieces, images)
    get_mlp[2].second()
    get_mlp[1].fourth()
    put0 = put(0, *mlp_spans(turned0, dgu0))
    get_mlp[2].third()
    get_mlp[1].finish()
    hid1, dgu1, turned1, acc = geglu_part(
        line, even, act_two, cotangent, get_mlp[1].pieces, images, acc
    )
    get_mlp[2].fourth()
    put0.start()
    put1 = put(1, *mlp_spans(turned1, dgu1))
    put0.first()
    get_mlp[2].finish()
    hid2, dgu2, turned2, dmid, db, do, dscale_two = geglu_part(
        line, odd, act_two, cotangent, get_mlp[2].pieces, images, acc,
        (mid, scale_two, odd, get_vo.pieces),
    )
    put0.second()
    put1.start()
    acts2, spans2 = mlp_spans(turned2, dgu2)
    put2 = put(0, acts2 + (o_turned,), spans2 + ((2, db, 0, 1),))
    put0.third()
    put1.first()
    dproj, dhead = attend_back(
        line, q, k, v, o, do, lse, valid, pack, spread, root, pick, block, turns, images
    )
    put0.fourth()
    put1.second()
    put2.start()
    put_qkv = put(1, (act_one,), tuple((0, dproj, span, 3) for span in range(3)))
    put0.finish()
    put1.third()
    put2.first()
    put_qkv.start()

    places = 2 if images % (2 * grouped(images)) == 0 else 1

    def result(place, into=None):
        return result_block(
            line, net.tables, (hid0, hid1, hid2), mid, [get.pieces for get in get_mlp], images,
            place, places, into,
        )

    qkv_pieces = get_qk.pieces + get_vo.pieces

    def to_input(place, into=None):
        return input_block(
            line, net.tables, dproj, tokens, dmid, scale_one, qkv_pieces, images, place, places, into
        )

    input_grad, dscale_one = to_input(0)
    put1.fourth()
    put2.second()
    put_qkv.first()
    if places > 1:
        input_grad, rest = to_input(1, input_grad)
        dscale_one = jnp.concatenate([dscale_one, rest], axis=0)
    put1.finish()
    put2.third()
    put_qkv.second()

    dhead = jnp.sum(dhead, axis=0)
    rows = jnp.concatenate([dscale_one[:, 0], dscale_two[:, 0], condition.astype(WIDE)], axis=1)
    if small:
        high = dhead.astype(LOW)
        rest = (dhead - high.astype(WIDE)).astype(LOW)
        heads = jnp.concatenate([high, rest, jnp.zeros((6, 128), LOW)], axis=0)
        rows = jnp.concatenate([rows.astype(LOW).reshape(1, -1, 128), heads[None]], axis=1)
        late = SmallGather(net, line, rows)
        late.step((4, 8, 12))
    block_output = result(0)
    put_qkv.third()
    put2.fourth()
    if small:
        late.step((1, 2, 3))
    if places > 1:
        block_output = result(1, block_output)
    put_qkv.fourth()
    put2.finish()
    if small:
        late.step()
        rows = late.held[:, :-8].reshape(32 * images, -1).astype(WIDE)
        dhead = jnp.sum(late.held[:, -8:-6].astype(WIDE), axis=(0, 1))[None]
    else:
        rows = lax.all_gather(rows, AXES, axis=0, tiled=True)
        dhead = lax.psum(dhead, AXES)
    own_rows = ada_weight.shape[1]
    own_start = 2 * width + lax.axis_index("fsdp") * own_rows
    cond_own = lax.dynamic_slice_in_dim(rows, own_start, own_rows, axis=1)
    grad_ada = jnp.stack(
        [jnp.dot(cond_own.T, rows[:, :width], precision=PRECISE),
         jnp.dot(cond_own.T, rows[:, width : 2 * width], precision=PRECISE)]
    )
    head_grad = dhead[:, :head_count] / (2.0 * head_scale)
    ada_square = line.pin(0.5 * jnp.sum(grad_ada * grad_ada))
    grad_ada, head_grad = line.pin(grad_ada), line.pin(head_grad)
    put_qkv.finish()
    puts = (put0, put1, put2, put_qkv)
    mines = tuple(each.mine for each in puts)
    others = tuple(each.other for each in puts)
    ada = (ada_weight, ada_first, ada_second)
    qkv = (qkv_weight, qkv_first, qkv_second)
    out = (out_weight, out_first, out_second)
    up = (up_weight, up_first, up_second)
    down = (down_weight, down_first, down_second)
    scale = (head_scale, scale_first, scale_second)
    if not small:
        return (block_output, input_grad) + finish_wide(
            net, ada, qkv, out, up, down, scale, grad_ada, head_grad, mines, others
        )
    local_squares = sum(each.square for each in puts) + ada_square
    total = net.total(local_squares)
    rows = down_weight.shape[0] // 3
    news = adam_all(
        line, core, total, ada, qkv, out, up,
        tuple(array.reshape(3, rows, width) for array in down),
        tuple(array[None] for array in scale), grad_ada, head_grad, mines, others,
    )
    return (
        block_output,
        input_grad,
        news[0][0, 0],
        *news[1:13],
        *[array.reshape(down_weight.shape) for array in news[13:16]],
        *[array[0] for array in news[16:19]],
    )


def solution(mesh):
    tokens = P(("dp", "fsdp"), None)
    ada = P(None, "fsdp", None)
    rows = P("fsdp", None)
    return jax.shard_map(
        functools.partial(local, dp_size=mesh.shape["dp"], fsdp_size=mesh.shape["fsdp"]),
        mesh=mesh,
        in_specs=(tokens,) * 4 + (ada,) * 3 + (rows,) * 12 + (P(),) * 3,
        out_specs=(tokens, tokens, P()) + (ada,) * 3 + (rows,) * 12 + (P(),) * 3,
        check_vma=False,
    )
```

```python
import functools
import math

import jax
import jax.numpy as jnp
import numpy as np
from jax import lax
from jax.experimental import pallas as pl
from jax.experimental.pallas import tpu as pltpu
from jax.sharding import PartitionSpec as P

FF = 3072
STEP = 10


NORM_EPS = 1e-06
COSINE_EPS = 1e-06
ROPE_BASE = 100.0
CLIP = 1.0
RATE = 0.02
OUTPUT_RATE = 0.2
SCALE_RATE = 8.0
BETA_ONE = 0.9
BETA_TWO = 0.95
ADAM_EPS = 1e-08
DECAY = 0.01
PRECISE = lax.Precision.HIGHEST
AXES = ("dp", "fsdp")
LOW = jnp.bfloat16
WIDE = jnp.float32


ORDERS = (
    ((8, 4, 1, 2), (2, 8, 4, 1)),
    ((8, 4, 2, 1), (1, 8, 4, 2)),
)


class Net:
    def __init__(self, size, dp_size):
        self.size = size
        self.dp_size = dp_size
        self.sub = size // 16
        self.core = lax.axis_index("dp")
        self.me = lax.axis_index("fsdp") // self.sub
        self.tables = tuple(self.table(order) for order in ORDERS)

    def exchange(self, array, bits):
        pairs = []
        for core in range(self.dp_size):
            for place in range(self.size):
                target = place ^ (bits[core % 2] * self.sub)
                pairs.append((core * self.size + place, core * self.size + target))
        return lax.ppermute(array, AXES, pairs)

    def cross(self, array, parity, stage):
        order = ORDERS[parity]
        return self.exchange(array, (order[0][stage], order[1][stage]))

    def swap(self, array):
        pairs = []
        for core in range(self.dp_size):
            for place in range(self.size):
                pairs.append((core * self.size + place, (core ^ 1) * self.size + place))
        return lax.ppermute(array, AXES, pairs)

    def table(self, order):
        index = lax.iota(jnp.int32, 32)
        side = self.core ^ (index >> 4)
        value = jnp.full((32,), self.me, jnp.int32)
        for stage in range(4):
            bit = jnp.where(side == 0, order[0][stage], order[1][stage])
            value = value ^ ((index >> stage & 1) * bit)
        return jnp.concatenate([value, self.core[None]]).astype(jnp.int32)

    def groups(self):
        return [list(range(g * self.sub, (g + 1) * self.sub)) for g in range(16)]

    def join_sub(self, shard):
        if self.sub == 1:
            return shard
        return lax.all_gather(shard, "fsdp", axis=0, tiled=True, axis_index_groups=self.groups())

    def split_sub(self, gradient):
        gathered = lax.all_gather(gradient, "fsdp", axis=0, axis_index_groups=self.groups())
        rows = gradient.shape[0] // self.sub
        place = lax.axis_index("fsdp") % self.sub
        return lax.dynamic_slice_in_dim(jnp.sum(gathered, axis=0), place * rows, rows, axis=0)

    def total(self, value):
        for bits in ((1, 2, 3), (4, 8, 12)):
            value = value + sum(self.exchange(value, (bit, bit)) for bit in bits)
        return value + self.swap(value)


TIMES = {
    "front": 18,
    "attend": 13,
    "middle": 10,
    "geglu_part": 20,
    "weight_grad": 14,
    "attend_back": 30,
    "input_grad": 12,
    "result": 11,
}
WORK = 1150000000


class Line:
    def __init__(self):
        self.last = None
        self.waits = []

    def call(self, kernel, args, in_specs, prefetch=0, into=None, **kwargs):
        deps = []
        if self.last is not None:
            token = self.last
            if self.waits:
                token = lax.optimization_barrier((token, *self.waits))[0]
            deps = [token]
        self.waits = []
        count = len(deps)
        if into is not None:
            args, in_specs = (*args, into), (*in_specs, ANY)
            kwargs["input_output_aliases"] = {count + len(args) - 1: 0}
            inner = kernel

            def kernel(*refs):
                inner(*refs[: len(args) - 1], *refs[len(args) :])

        one = not isinstance(kwargs["out_shape"], (list, tuple))
        shapes = [kwargs["out_shape"]] if one else list(kwargs["out_shape"])
        specs = kwargs["out_specs"]
        specs = [specs] if not isinstance(specs, (list, tuple)) else list(specs)
        place = prefetch + len(in_specs) + len(shapes)

        def body(*refs):
            refs = refs[:prefetch] + refs[prefetch + count :]
            refs[place][...] = jnp.zeros((8, 128), WIDE)
            kernel(*refs[:place], *refs[place + 1 :])

        in_specs = [ANY] * count + list(in_specs)
        out_specs = specs + [whole((8, 128)) if "grid" in kwargs else VMEM]
        del kwargs["out_specs"]
        kwargs["out_shape"] = shapes + [jax.ShapeDtypeStruct((8, 128), WIDE)]
        if prefetch:
            kwargs["grid_spec"] = pltpu.PrefetchScalarGridSpec(
                num_scalar_prefetch=prefetch,
                grid=kwargs.pop("grid"),
                in_specs=in_specs,
                out_specs=out_specs,
                scratch_shapes=kwargs.pop("scratch_shapes", []),
            )
        else:
            kwargs["in_specs"] = in_specs
            kwargs["out_specs"] = out_specs
        if kwargs["name"] in TIMES:
            kwargs["cost_estimate"] = cost(TIMES[kwargs["name"]] * WORK, 1 << 20)
        *outs, self.last = pl.pallas_call(body, **kwargs)(*args[:prefetch], *deps, *args[prefetch:])
        return outs[0] if one else outs

    def pin(self, array):
        if self.last is not None:
            array, _ = lax.optimization_barrier((array, self.last))
        self.waits.append(array)
        return array


class Gather:
    def __init__(self, net, line, parity, half):
        self.net, self.line, self.parity = net, line, parity
        self.held = line.pin(half)
        self.got = net.cross(self.held, parity, 0)

    def wait(self):
        self.got = self.line.pin(self.got)

    def second(self):
        self.wait()
        self.held = join(self.line, self.held, self.got)
        self.got = self.net.cross(self.held, self.parity, 1)

    def third(self):
        self.wait()
        self.held = join(self.line, self.held, self.got)
        self.near = self.net.cross(self.held, self.parity, 2)
        self.far = self.net.cross(self.held, self.parity, 3)
        self.swapped = [self.net.swap(self.held)]

    def wait_near(self):
        self.near, self.far = self.line.pin(self.near), self.line.pin(self.far)

    def wait_last(self):
        self.last = self.line.pin(self.last)

    def fourth(self):
        self.wait_near()
        self.swapped = [self.line.pin(array) for array in self.swapped]
        self.last = self.net.cross(self.near, self.parity, 3)
        self.swapped += [self.net.swap(self.near), self.net.swap(self.far)]

    def finish(self):
        self.last = self.line.pin(self.last)
        self.swapped = [self.line.pin(array) for array in self.swapped]
        self.swapped.append(self.net.swap(self.last))
        self.pieces = (self.held, self.near, self.far, self.last, *self.swapped)


class Scatter:
    def __init__(self, net, line, parity, keep, send):
        self.net, self.line, self.parity = net, line, parity
        self.keep, self.send = keep, send
        self.part = [None] * 4

    def swap(self, number):
        self.part[number] = self.net.swap(self.line.pin(self.send[number]))

    def start(self):
        self.swap(3)
        self.swap(2)

    def wait(self):
        self.got = self.line.pin(self.got)

    def first(self):
        two, three = fold_pair(self.line, self.keep[2:], self.part[2:])
        self.got = self.net.cross(three, self.parity, 3)
        self.late = self.net.cross(two, self.parity, 3)
        self.swap(1)

    def second(self):
        self.wait()
        (held,) = fold(self.line, self.keep[1], (self.part[1], self.got), 1)
        self.got = self.net.cross(held, self.parity, 2)
        self.swap(0)

    def third(self):
        self.wait()
        self.late = self.line.pin(self.late)
        self.held, send = fold(self.line, self.keep[0], (self.part[0], self.late, self.got), 2)
        self.got = self.net.cross(send, self.parity, 1)

    def fourth(self):
        self.wait()
        self.held, send = fold(self.line, self.held, (self.got,), 2)
        self.got = self.net.cross(send, self.parity, 0)

    def finish(self):
        self.wait()
        self.mine, self.square = fold_last(self.line, self.held[0], self.got[0])
        self.other = self.net.swap(self.mine)


class SmallGather:
    def __init__(self, net, line, rows):
        self.net, self.line = net, line
        self.held = line.pin(rows)
        self.got = [net.swap(self.held)]

    def step(self, bits=()):
        got = [self.line.pin(array) for array in self.got]
        self.held = jnp.concatenate([self.held, *got], axis=0)
        self.got = [self.net.exchange(self.held, (bit, bit)) for bit in bits]


ANY = pl.BlockSpec(memory_space=pl.ANY)
SMEM = pl.BlockSpec(memory_space=pltpu.SMEM)
VMEM = pl.BlockSpec(memory_space=pltpu.VMEM)
NT = (((1,), (1,)), ((), ()))
TN = (((0,), (0,)), ((), ()))
VMEM_LIMIT = 56 * 1024 * 1024
SMALL_LIMIT = 16 * 1024 * 1024


def load_weight(table_ref, pieces, full_ref, sems):
    core = table_ref[32]
    rows = pieces[0].shape[1]
    copies = []
    for number, piece in enumerate(pieces):
        side = core if number < 4 else 1 - core
        for index in range(4):
            start = pl.multiple_of(table_ref[number * 4 + index] * (2 * rows) + side * rows, 16)
            copies.append(
                pltpu.make_async_copy(
                    piece.at[index], full_ref.at[pl.ds(start, rows)], sems.at[number, index]
                )
            )
    return copies


def part_of(pieces, first, size):
    return tuple(piece.at[:, :, first : first + size] for piece in pieces)


def fetch(copies):
    for copy in copies:
        copy.start()
    for copy in copies:
        copy.wait()


SEMS = pltpu.SemaphoreType.DMA((8, 4))


def params(dims):
    return pltpu.CompilerParams(
        dimension_semantics=("arbitrary",) * dims, vmem_limit_bytes=VMEM_LIMIT
    )


def cost(flops, size):
    return pl.CostEstimate(flops=flops, bytes_accessed=size, transcendentals=0)


def mul(a, b):
    return jnp.dot(a, b, preferred_element_type=WIDE)


def mul_nt(a, b):
    return lax.dot_general(a, b, NT, preferred_element_type=WIDE)


def mul_tn(a, b):
    return lax.dot_general(a, b, TN, preferred_element_type=WIDE)


def whole(shape):
    return pl.BlockSpec(shape, lambda *_: (0,) * len(shape))


def turned_block(width, seq):
    return pl.BlockSpec((width, seq), lambda i: (0, i))


def turned_shape(width, tokens):
    return jax.ShapeDtypeStruct((width, tokens), LOW)


def grouped(images):
    return 2 if images % 2 == 0 else 1


def scaled(values, scale_ref):
    count = scale_ref.shape[0]
    rows = values.shape[0] // count
    parts = [values[i * rows : i * rows + rows] * scale_ref[i] for i in range(count)]
    return parts[0] if count == 1 else jnp.concatenate(parts, axis=0)


def norm_back(grad, values, scale_ref, dscale_ref):
    inverse = lax.rsqrt(jnp.mean(values * values, axis=-1, keepdims=True) + NORM_EPS)
    normed = values * inverse
    product = grad * normed
    count = scale_ref.shape[0]
    rows = values.shape[0] // count
    for i in range(count):
        dscale_ref[i] = jnp.sum(product[i * rows : i * rows + rows], axis=0, keepdims=True)
    grad = scaled(grad, scale_ref)
    inner = jnp.mean(grad * normed, axis=-1, keepdims=True)
    return inverse * (grad - normed * inner)


def rotate(values, cos_rep, up_rep, down_rep, sign):
    ahead = pltpu.roll(values, values.shape[-1] - 16, 1)
    behind = pltpu.roll(values, 16, 1)
    turned = ahead * up_rep + behind * down_rep
    return values * cos_rep + (turned if sign > 0 else -turned)


def join_kernel(a_ref, b_ref, out_ref, sems):
    count = a_ref.shape[0]
    fetch(
        [
            pltpu.make_async_copy(a_ref, out_ref.at[:count], sems.at[0]),
            pltpu.make_async_copy(b_ref, out_ref.at[count:], sems.at[1]),
        ]
    )


def join(line, a, b):
    shape = (2 * a.shape[0],) + a.shape[1:]
    return line.call(
        join_kernel,
        (a, b),
        [ANY, ANY],
        out_specs=VMEM,
        out_shape=jax.ShapeDtypeStruct(shape, a.dtype),
        scratch_shapes=[pltpu.SemaphoreType.DMA((2,))],
        compiler_params=pltpu.CompilerParams(vmem_limit_bytes=SMALL_LIMIT),
        cost_estimate=cost(0, 4 * math.prod(shape)),
        name="join",
    )


def fold_kernel(count, held_ref, *refs):
    outs = refs[count:]
    total = held_ref[...].astype(WIDE)
    for ref in refs[:count]:
        total += ref[...].astype(WIDE)
    size = outs[0].shape[0]
    for number, out in enumerate(outs):
        out[...] = total[number * size : number * size + size].astype(out.dtype)


def fold(line, held, others, parts):
    shape = (held.shape[0] // parts,) + held.shape[1:]
    return line.call(
        functools.partial(fold_kernel, len(others)),
        (held, *others),
        [VMEM] * (1 + len(others)),
        out_specs=[VMEM] * parts,
        out_shape=[jax.ShapeDtypeStruct(shape, held.dtype)] * parts,
        compiler_params=pltpu.CompilerParams(vmem_limit_bytes=SMALL_LIMIT),
        cost_estimate=cost(0, 2 * math.prod(held.shape) * (2 + len(others))),
        name="fold",
    )


def fold_pair_kernel(a_ref, b_ref, c_ref, d_ref, first_ref, second_ref):
    first_ref[...] = (a_ref[...].astype(WIDE) + c_ref[...].astype(WIDE)).astype(LOW)
    second_ref[...] = (b_ref[...].astype(WIDE) + d_ref[...].astype(WIDE)).astype(LOW)


def fold_pair(line, held, others):
    shape = jax.ShapeDtypeStruct(held[0].shape, LOW)
    return line.call(
        fold_pair_kernel,
        (*held, *others),
        [VMEM] * 4,
        out_specs=[VMEM] * 2,
        out_shape=[shape] * 2,
        compiler_params=pltpu.CompilerParams(vmem_limit_bytes=SMALL_LIMIT),
        cost_estimate=cost(0, 12 * math.prod(shape.shape)),
        name="fold_pair",
    )


def fold_last_kernel(held_ref, other_ref, out_ref, square_ref):
    total = (held_ref[...].astype(WIDE) + other_ref[...].astype(WIDE)).astype(LOW)
    out_ref[...] = total
    total = total.astype(WIDE)
    sums = jnp.sum(jnp.sum(total * total, axis=0, keepdims=True), axis=1, keepdims=True)
    square_ref[...] = jnp.broadcast_to(sums, square_ref.shape)


def fold_last(line, held, other):
    return line.call(
        fold_last_kernel,
        (held, other),
        [VMEM, VMEM],
        out_specs=[VMEM, VMEM],
        out_shape=[jax.ShapeDtypeStruct(held.shape, LOW), jax.ShapeDtypeStruct((1, 128), WIDE)],
        compiler_params=pltpu.CompilerParams(vmem_limit_bytes=SMALL_LIMIT),
        cost_estimate=cost(0, 6 * math.prod(held.shape)),
        name="fold_last",
    )


def head_kernel(core_ref, qkv_ref, out_ref, ada_ref, *outs):
    rows, size = qkv_ref.shape[0], ada_ref.shape[2]
    for number, out in enumerate(outs):
        for block in range(4):
            at = (4 * number + block) * size
            past = at - qkv_ref.shape[1]
            values = qkv_ref[:, at : at + size] if past < 0 else out_ref[:, past : past + size]
            out[0, block * rows : block * rows + rows, :] = values.astype(LOW)
        out[0, 4 * rows :, :] = ada_ref[number].astype(LOW)


def head_parts(line, core, qkv, out, ada):
    rows, width = qkv.shape[0] // 2, out.shape[1]
    size = width // 2
    shape = (1, 4 * rows + ada.shape[1], size)
    return line.call(
        head_kernel,
        (core[None], qkv, out, ada),
        [pl.BlockSpec((rows, 3 * width), lambda i, c: (c[0], 0)),
         pl.BlockSpec((rows, width), lambda i, c: (c[0], 0)),
         pl.BlockSpec((2, ada.shape[1], size), lambda i, c: (0, 0, c[0]))],
        prefetch=1,
        grid=(1,),
        out_specs=[whole(shape)] * 2,
        out_shape=[jax.ShapeDtypeStruct(shape, LOW)] * 2,
        compiler_params=params(1),
        cost_estimate=cost(0, 2 << 20),
        name="head_parts",
    )


def load_head(table_ref, pieces, first, full_ref, sems, ada_ref=None, ada_sems=None):
    core = table_ref[32]
    size = pieces[0].shape[2]
    ada_rows = 0 if ada_ref is None else ada_ref.shape[0] // 16
    copies = []
    for number, piece in enumerate(pieces):
        side = core if number < 4 else 1 - core
        for index in range(4):
            owner = table_ref[number * 4 + index]
            start = pl.multiple_of(owner * 64 + side * 32, 16)
            for block in range(full_ref.shape[1] // size):
                copies.append(
                    pltpu.make_async_copy(
                        piece.at[index, (first + block) * 32 : (first + block) * 32 + 32],
                        full_ref.at[pl.ds(start, 32), block * size : block * size + size],
                        sems.at[block, number, index],
                    )
                )
            if ada_ref is not None:
                start = pl.multiple_of(owner * ada_rows, 16)
                column = pl.multiple_of(side * size, 128)
                copies.append(
                    pltpu.make_async_copy(
                        piece.at[index, piece.shape[1] - ada_rows :],
                        ada_ref.at[pl.ds(start, ada_rows), pl.ds(column, size)],
                        ada_sems.at[number, index],
                    )
                )
    return copies


def cut_kernel(core_ref, up_ref, down_ref, *outs):
    width = down_ref.shape[2]
    low = lax.broadcasted_iota(jnp.int32, (up_ref.shape[0], 128), 1) < 64
    for start in range(0, 2 * width, 128):
        first, second, third = (up_ref[:, 3 * start + 128 * i : 3 * start + 128 * i + 128] for i in range(3))
        lanes = slice(start, start + 128)
        outs[0][0, :, lanes] = jnp.where(low, first, second).astype(LOW)
        outs[1][0, :, lanes] = pltpu.roll(jnp.where(low, third, first), 64, 1).astype(LOW)
        outs[2][0, :, lanes] = jnp.where(low, second, third).astype(LOW)
    for part, out in enumerate(outs):
        out[0, :, 2 * width :] = down_ref[part].astype(LOW)


def cut_parts(line, core, up, down):
    rows, columns = up.shape[0] // 2, up.shape[1]
    width = down.shape[2]
    return line.call(
        cut_kernel,
        (core[None], up, down),
        [pl.BlockSpec((rows, columns), lambda i, c: (c[0], 0)),
         pl.BlockSpec((3, rows, width), lambda i, c: (0, c[0], 0))],
        prefetch=1,
        grid=(1,),
        out_specs=[whole((1, rows, 3 * width))] * 3,
        out_shape=[jax.ShapeDtypeStruct((1, rows, 3 * width), LOW)] * 3,
        compiler_params=params(1),
        cost_estimate=cost(0, 4 << 20),
        name="cut",
    )


def conditioned(cond_ref, ada_ref, out_ref):
    scale = 1.0 + mul(cond_ref[...], ada_ref[...])
    for image in range(scale.shape[0]):
        out_ref[image] = scale[image : image + 1]


def front_kernel(group, table_ref, x_ref, cond_ref, *rest):
    pieces, rest = rest[:8], rest[8:]
    sums_ref, spread_ref, root_ref, cos_ref, up_ref, down_ref, *rest = rest
    act_ref, q_ref, k_ref, pack_ref, one_ref, w_ref, ada_ref, sems, ada_sems = rest

    @pl.when(pl.program_id(0) == 0)
    def _():
        fetch(load_head(table_ref, pieces, 0, w_ref, sems, ada_ref, ada_sems))
        conditioned(cond_ref, ada_ref, one_ref)

    scale_ref = one_ref.at[pl.ds(pl.program_id(0) * group, group)]
    width = x_ref.shape[1]
    x = x_ref[...].astype(WIDE)
    inverse = lax.rsqrt(jnp.mean(x * x, axis=-1, keepdims=True) + NORM_EPS)
    act = scaled(x * inverse, scale_ref).astype(LOW)
    act_ref[...] = act.T
    q = mul(act, w_ref[:, :width])
    k = mul(act, w_ref[:, width:])
    sums = mul((q * q).astype(LOW), sums_ref[0]) + mul((k * k).astype(LOW), sums_ref[1])
    factor = lax.rsqrt(sums + COSINE_EPS)
    high = factor.astype(LOW)
    low = (factor - high.astype(WIDE)).astype(LOW)
    lane = lax.broadcasted_iota(jnp.int32, factor.shape, 1)
    pack = jnp.where(lane < 32, high.astype(WIDE), jnp.where(lane < 64, low.astype(WIDE), 0.0))
    pack = pack.astype(LOW)
    pack_ref[...] = pack
    q = q * mul(pack, spread_ref[0]) * root_ref[...]
    k = k * mul(pack, spread_ref[1]) * root_ref[...]
    cos_rep, up_rep, down_rep = cos_ref[...], up_ref[...], down_ref[...]
    for pair in range(width // 128):
        lanes = slice(pair * 128, pair * 128 + 128)
        q_ref[:, lanes] = rotate(q[:, lanes], cos_rep, up_rep, down_rep, 1).astype(LOW)
        k_ref[:, lanes] = rotate(k[:, lanes], cos_rep, up_rep, down_rep, 1).astype(LOW)


def front(line, table, x, cond, pieces, sums, spread, root, turns, images):
    tokens, width = x.shape
    group = grouped(images)
    seq = tokens // images * group
    row = pl.BlockSpec((seq, width), lambda i: (i, 0))
    narrow = pl.BlockSpec((seq, 128), lambda i: (i, 0))
    full = jax.ShapeDtypeStruct((tokens, width), LOW)
    return line.call(
        functools.partial(front_kernel, group),
        (table, x, cond, *pieces, sums, spread, root, *turns),
        [SMEM, row, whole(cond.shape), *[ANY] * 8,
                  whole(sums.shape), whole(spread.shape), whole(root.shape), narrow, narrow, narrow],
        grid=(images // group,),
        out_specs=[turned_block(width, seq), row, row, narrow, whole((images, 1, width))],
        out_shape=[turned_shape(width, tokens), full, full, jax.ShapeDtypeStruct((tokens, 128), LOW),
                   jax.ShapeDtypeStruct((images, 1, width), WIDE)],
        scratch_shapes=[pltpu.VMEM((width, 2 * width), LOW), pltpu.VMEM((cond.shape[1], width), LOW),
                        pltpu.SemaphoreType.DMA((4, 8, 4)), SEMS],
        compiler_params=params(1),
        cost_estimate=cost(4 * tokens * width * width, 20 << 20),
        name="front",
    )


def attend_kernel(table_ref, q_ref, k_ref, valid_ref, x_ref, scale_ref, *rest):
    pieces = rest[:8]
    v_ref, o_ref, turned_ref, lse_ref, w_ref, sems = rest[8:]

    @pl.when(pl.program_id(0) == 0)
    def _():
        fetch(load_head(table_ref, pieces, 0, w_ref, sems))

    x = x_ref[...].astype(WIDE)
    inverse = lax.rsqrt(jnp.mean(x * x, axis=-1, keepdims=True) + NORM_EPS)
    act = scaled(x * inverse, scale_ref).astype(LOW)
    v_ref[...] = mul(act, w_ref[...]).astype(LOW)
    seq, width = q_ref.shape
    valid = valid_ref[...]
    lane = lax.broadcasted_iota(jnp.int32, (seq, 128), 1)
    first = lane < 64
    totals = jnp.zeros((seq, 128), WIDE)
    zero = jnp.zeros((seq, 128), LOW)
    for pair in range(width // 128):
        lanes = slice(pair * 128, pair * 128 + 128)
        q, k = q_ref[:, lanes], k_ref[:, lanes]
        v = v_ref[:, lanes] * valid
        picks = (first, jnp.logical_not(first))
        scores = [mul_nt(jnp.where(pick, q, zero), k) for pick in picks]
        weights = jnp.concatenate([jnp.exp(score).astype(LOW) for score in scores], axis=1)
        right = [
            jnp.concatenate([jnp.where(pick, v, zero), jnp.where(pick, valid, zero)], axis=1)
            for pick in picks
        ]
        both = mul(weights, jnp.concatenate(right, axis=0))
        total = both[:, 128:]
        mixed = both[:, :128] / total
        totals = jnp.where(lane == 2 * pair, total[:, :1], totals)
        totals = jnp.where(lane == 2 * pair + 1, total[:, 64:65], totals)
        mixed = mixed.astype(LOW)
        o_ref[:, lanes] = mixed
        turned_ref[lanes, :] = mixed.T
    lane_ok = lane < width // 64
    lse = jnp.log(jnp.where(lane_ok, totals, 1.0))
    lse_ref[0] = lse.T[: width // 64]


def attend(line, table, q, k, valid, x, scale, pieces, images):
    tokens, width = q.shape
    seq = tokens // images
    row = pl.BlockSpec((seq, width), lambda i: (i, 0))
    heads = width // 64
    low = jax.ShapeDtypeStruct((tokens, width), LOW)
    return line.call(
        attend_kernel,
        (table, q, k, valid, x, scale, *pieces),
        [SMEM, row, row, pl.BlockSpec((seq, 128), lambda i: (i, 0)), row,
         pl.BlockSpec((1, 1, width), lambda i: (i, 0, 0))] + [ANY] * 8,
        grid=(images,),
        out_specs=[row, row, turned_block(width, seq), pl.BlockSpec((1, heads, seq), lambda i: (i, 0, 0))],
        out_shape=[low, low, turned_shape(width, tokens),
                   jax.ShapeDtypeStruct((images, heads, seq), WIDE)],
        scratch_shapes=[pltpu.VMEM((width, width), LOW), pltpu.SemaphoreType.DMA((2, 8, 4))],
        compiler_params=params(1),
        cost_estimate=cost(16 * tokens * seq * width, 12 << 20),
        name="attend",
    )


def middle_kernel(group, table_ref, o_ref, x_ref, cond_ref, *rest):
    pieces = rest[:8]
    mid_ref, act_ref, turned_ref, two_ref, w_ref, ada_ref, sems, ada_sems = rest[8:]

    @pl.when(pl.program_id(0) == 0)
    def _():
        fetch(load_head(table_ref, pieces, 2, w_ref, sems, ada_ref, ada_sems))
        conditioned(cond_ref, ada_ref, two_ref)

    scale_ref = two_ref.at[pl.ds(pl.program_id(0) * group, group)]
    mid = x_ref[...].astype(WIDE) + mul(o_ref[...], w_ref[...])
    mid_ref[...] = mid
    inverse = lax.rsqrt(jnp.mean(mid * mid, axis=-1, keepdims=True) + NORM_EPS)
    act = scaled(mid * inverse, scale_ref).astype(LOW)
    act_ref[...] = act
    turned_ref[...] = act.T


def middle_block(line, table, o, x, cond, pieces, images):
    tokens, width = x.shape
    group = grouped(images)
    seq = tokens // images * group
    row = pl.BlockSpec((seq, width), lambda i: (i, 0))
    return line.call(
        functools.partial(middle_kernel, group),
        (table, o, x, cond, *pieces),
        [SMEM, row, row, whole(cond.shape)] + [ANY] * 8,
        grid=(images // group,),
        out_specs=[row, row, turned_block(width, seq), whole((images, 1, width))],
        out_shape=[jax.ShapeDtypeStruct((tokens, width), WIDE), jax.ShapeDtypeStruct((tokens, width), LOW),
                   turned_shape(width, tokens), jax.ShapeDtypeStruct((images, 1, width), WIDE)],
        scratch_shapes=[pltpu.VMEM((width, width), LOW), pltpu.VMEM((cond.shape[1], width), LOW),
                        pltpu.SemaphoreType.DMA((2, 8, 4)), SEMS],
        compiler_params=params(1),
        cost_estimate=cost(2 * tokens * width * width, 12 << 20),
        name="middle",
    )


def part_kernel(first, last, table_ref, act_ref, dy_ref, *rest):
    rest = list(rest)
    pieces = tuple(rest.pop(0) for _ in range(8))
    if last:
        mid_ref, scale_ref, out_table_ref = rest.pop(0), rest.pop(0), rest.pop(0)
        out_pieces = tuple(rest.pop(0) for _ in range(8))
    acc_ref = None if first else rest.pop(0)
    hid_ref, dgu_ref, turned_ref = rest.pop(0), rest.pop(0), rest.pop(0)
    if last:
        dmid_ref, db_ref, do_ref, dscale_ref = (rest.pop(0) for _ in range(4))
    else:
        da_ref = rest.pop(0)
    w_ref, sems = rest.pop(0), rest.pop(0)
    if last:
        out_ref, sems_out = rest.pop(0), rest.pop(0)

    @pl.when(pl.program_id(0) == 0)
    def _():
        copies = load_weight(table_ref, pieces, w_ref, sems)
        if last:
            copies = copies + load_head(out_table_ref, out_pieces, 2, out_ref, sems_out)
        fetch(copies)

    width = act_ref.shape[1]
    act, dy = act_ref[...], dy_ref[...]
    size = 512
    for start in range(0, width, size):
        cols = slice(start, start + size)
        above = slice(width + start, width + start + size)
        gate = mul(act, w_ref[:, cols])
        upper = mul(act, w_ref[:, above])
        grad = mul_nt(dy, w_ref[start : start + size, 2 * width :]).astype(LOW).astype(WIDE)
        cdf = 0.5 * (1.0 + lax.erf(gate * math.sqrt(0.5)))
        bell = jnp.exp(-0.5 * gate * gate) * (1.0 / math.sqrt(2.0 * math.pi))
        gelu = gate * cdf
        hid = (gelu * upper).astype(LOW)
        hid_ref[:, cols] = hid
        turned_ref[cols, :] = hid.T
        dgu_ref[:, cols] = (grad * upper * (cdf + gate * bell)).astype(LOW)
        dgu_ref[:, above] = (grad * gelu).astype(LOW)
    total = mul_nt(dgu_ref[:, :width], w_ref[:, :width])
    total += mul_nt(dgu_ref[:, width:], w_ref[:, width : 2 * width])
    if not first:
        total += acc_ref[...]
    if not last:
        da_ref[...] = total
        return
    dmid = dy.astype(WIDE) + norm_back(total, mid_ref[...], scale_ref, dscale_ref)
    dmid_ref[...] = dmid
    low = dmid.astype(LOW)
    db_ref[...] = low
    do_ref[...] = mul_nt(low, out_ref[...]).astype(LOW)


def geglu_part(line, table, act, dy, pieces, images, acc=None, final=None):
    tokens, width = act.shape
    group = grouped(images)
    seq = tokens // images * group
    first, last = acc is None, final is not None
    row = pl.BlockSpec((seq, width), lambda i: (i, 0))
    one = pl.BlockSpec((group, 1, width), lambda i: (i, 0, 0))
    args = [table, act, dy, *pieces]
    in_specs = [SMEM, row, row] + [ANY] * 8
    if last:
        mid, scale, out_table, out_pieces = final
        args += [mid, scale, out_table, *out_pieces]
        in_specs += [row, one, SMEM] + [ANY] * 8
    if not first:
        args.append(acc)
        in_specs.append(row)
    low = jax.ShapeDtypeStruct((tokens, width), LOW)
    wide = jax.ShapeDtypeStruct((tokens, width), WIDE)
    out_specs = [row, pl.BlockSpec((seq, 2 * width), lambda i: (i, 0)), turned_block(width, seq)]
    out_shape = [low, jax.ShapeDtypeStruct((tokens, 2 * width), LOW), turned_shape(width, tokens)]
    scratch = [pltpu.VMEM((width, 3 * width), LOW), SEMS]
    if last:
        out_specs += [row, row, row, one]
        out_shape += [wide, low, low, jax.ShapeDtypeStruct((images, 1, width), WIDE)]
        scratch += [pltpu.VMEM((width, width), LOW), pltpu.SemaphoreType.DMA((2, 8, 4))]
    else:
        out_specs.append(row)
        out_shape.append(wide)
    return line.call(
        functools.partial(part_kernel, first, last),
        args,
        in_specs,
        grid=(images // group,),
        out_specs=out_specs,
        out_shape=out_shape,
        scratch_shapes=scratch,
        compiler_params=params(1),
        cost_estimate=cost((12 if last else 10) * tokens * width * width, 30 << 20),
        name="geglu_part",
    )


def attend_back_kernel(q_ref, k_ref, v_ref, o_ref, do_ref, lse_ref, valid_ref, pack_ref, spread_ref,
                       root_ref, pick_ref, block_ref, cos_ref, up_ref, down_ref, dproj_ref, dhead_ref,
                       grad_ref, product_ref, inner_ref):
    seq, width = q_ref.shape
    valid = valid_ref[...]
    valid_wide = valid.astype(WIDE)
    first = lax.broadcasted_iota(jnp.int32, (seq, 128), 1) < 64
    zero = jnp.zeros((seq, 128), LOW)
    cos_rep, up_rep, down_rep = cos_ref[...], up_ref[...], down_ref[...]
    product = (do_ref[...].astype(WIDE) * o_ref[...].astype(WIDE)).astype(LOW)
    delta = mul_nt(pick_ref[...], product)
    pack = pack_ref[...]
    block = block_ref[...]
    head_lane = lax.broadcasted_iota(jnp.int32, (1, 128), 1)
    row = jnp.zeros((1, 128), WIDE)
    for pair in range(width // 128):
        lanes = slice(pair * 128, pair * 128 + 128)
        q, k, v, do = q_ref[:, lanes], k_ref[:, lanes], v_ref[:, lanes], do_ref[:, lanes]
        k_turned = (k * valid).T
        picks = (first, jnp.logical_not(first))
        q_ones = [jnp.where(pick, q, zero) for pick in picks]
        do_ones = [jnp.where(pick, do, zero) for pick in picks]
        scores = [mul_nt(k, one) for one in q_ones]
        grads = [mul_nt(v, one) for one in do_ones]
        lows, dscores = [], []
        for half in range(2):
            head = 2 * pair + half
            weights = jnp.exp(scores[half] - lse_ref[0, head : head + 1, :])
            lows.append(weights.astype(LOW))
            dscores.append((weights * (grads[half] - delta[head : head + 1, :])).astype(LOW))
        dv = mul(jnp.concatenate(lows, axis=1), jnp.concatenate(do_ones, axis=0))
        dk = mul(jnp.concatenate(dscores, axis=1), jnp.concatenate(q_ones, axis=0))
        dq_parts = [mul(k_turned[half * 64 : half * 64 + 64], dscores[half]) for half in range(2)]
        dq = jnp.concatenate(dq_parts, axis=0).T
        dk = dk * valid_wide
        dproj_ref[:, 2 * width + pair * 128 : 2 * width + pair * 128 + 128] = (dv * valid_wide).astype(LOW)
        for side, (grad, value) in enumerate(((dq, q), (dk, k))):
            at = (side * (width // 128) + pair) * seq
            grad_ref[side, :, lanes] = grad
            product_ref[at : at + seq, :] = (grad * value.astype(WIDE)).astype(LOW)
    inner_ref[...] = mul(product_ref[...], block)
    factors = [mul(pack, spread_ref[side]) for side in range(2)]
    for pair in range(width // 128):
        lanes = slice(pair * 128, pair * 128 + 128)
        root = root_ref[:, lanes]
        total = 0.0
        for side, value_ref in enumerate((q_ref, k_ref)):
            at = (side * (width // 128) + pair) * seq
            inner = inner_ref[at : at + seq, :]
            total = total + jnp.sum(inner, axis=0, keepdims=True)
            back = root * grad_ref[side, :, lanes] - value_ref[:, lanes].astype(WIDE) * (inner / root)
            back = rotate(factors[side][:, lanes] * back, cos_rep, up_rep, down_rep, -1)
            dproj_ref[:, side * width + pair * 128 : side * width + pair * 128 + 128] = back.astype(LOW)
        row = jnp.where(head_lane == 2 * pair, total[:, :1], row)
        row = jnp.where(head_lane == 2 * pair + 1, total[:, 64:65], row)
    dhead_ref[0] = row


def attend_back(line, q, k, v, o, do, lse, valid, pack, spread, root, pick, block, turns, images):
    tokens, width = q.shape
    seq = tokens // images
    heads = width // 64
    row = pl.BlockSpec((seq, width), lambda i: (i, 0))
    narrow = pl.BlockSpec((seq, 128), lambda i: (i, 0))
    return line.call(
        attend_back_kernel,
        (q, k, v, o, do, lse, valid, pack, spread, root, pick, block, *turns),
        [row, row, row, row, row, pl.BlockSpec((1, heads, seq), lambda i: (i, 0, 0)), narrow, narrow,
                  whole(spread.shape), whole(root.shape), whole(pick.shape), whole(block.shape),
                  narrow, narrow, narrow],
        grid=(images,),
        out_specs=[pl.BlockSpec((seq, 3 * width), lambda i: (i, 0)),
                   pl.BlockSpec((1, 1, 128), lambda i: (i, 0, 0))],
        out_shape=[jax.ShapeDtypeStruct((tokens, 3 * width), LOW),
                   jax.ShapeDtypeStruct((images, 1, 128), WIDE)],
        scratch_shapes=[pltpu.VMEM((2, seq, width), WIDE), pltpu.VMEM((width // 64 * seq, 128), LOW),
                        pltpu.VMEM((width // 64 * seq, 128), WIDE)],
        compiler_params=params(1),
        cost_estimate=cost(40 * tokens * seq * width, 20 << 20),
        name="attend_back",
    )


def input_kernel(even_ref, odd_ref, dproj_ref, x_ref, dmid_ref, scale_ref, *rest):
    pieces = rest[:16]
    out_ref, dscale_ref, w_ref, sems = rest[16:]

    width = x_ref.shape[1]
    copies = [
        load_head(even_ref, pieces[:8], 0, w_ref.at[:, :width], sems.at[:2]),
        load_head(even_ref, pieces[:8], 2, w_ref.at[:, width : 2 * width], sems.at[2:4]),
        load_head(odd_ref, pieces[8:], 0, w_ref.at[:, 2 * width :], sems.at[4:]),
    ]
    for copy in sum(copies, []):
        copy.start()
    grad = None
    for part in range(3):
        for copy in copies[part]:
            copy.wait()
        cols = slice(part * width, part * width + width)
        add = mul_nt(dproj_ref[:, cols], w_ref[:, cols])
        grad = add if grad is None else grad + add
    x = x_ref[...].astype(WIDE)
    out_ref[...] = (dmid_ref[...] + norm_back(grad, x, scale_ref, dscale_ref)).astype(LOW)


def input_block(line, tables, dproj, x, dmid, scale, pieces, images, place, places, into):
    tokens, width = x.shape
    group = grouped(images)
    seq = tokens // images * group
    steps = images // group // places
    row = pl.BlockSpec((seq, width), lambda i: (place * steps + i, 0))
    one = pl.BlockSpec((group, 1, width), lambda i: (place * steps + i, 0, 0))
    return line.call(
        input_kernel,
        (*tables, dproj, x, dmid, scale, *pieces),
        [SMEM, SMEM, pl.BlockSpec((seq, 3 * width), lambda i: (place * steps + i, 0)), row, row, one] + [ANY] * 16,
        into=into,
        grid=(steps,),
        out_specs=[row,
                   pl.BlockSpec((group, 1, width), lambda i: (i, 0, 0))],
        out_shape=[jax.ShapeDtypeStruct((tokens, width), LOW),
                   jax.ShapeDtypeStruct((images // places, 1, width), WIDE)],
        scratch_shapes=[pltpu.VMEM((width, 3 * width), LOW), pltpu.SemaphoreType.DMA((6, 8, 4))],
        compiler_params=params(1),
        cost_estimate=cost(6 * tokens * width * width // places, 24 << 20),
        name="input_grad",
    )


def result_kernel(even_ref, odd_ref, h0, h1, h2, mid_ref, *rest):
    pieces, out_ref, w_ref, sems = rest[:24], rest[24], rest[25], rest[26]
    width = mid_ref.shape[1]
    copies = []
    for part in range(3):
        ref = pieces[8 * part : 8 * part + 8]
        down = tuple(piece.at[:, :, 2 * width : 3 * width] for piece in ref)
        table_ref = odd_ref if part % 2 == 0 else even_ref
        copies.append(load_weight(table_ref, down, w_ref.at[part], sems.at[part]))
    for copy in sum(copies, []):
        copy.start()
    total = mid_ref[...]
    for part, hid_ref in enumerate((h0, h1, h2)):
        for copy in copies[part]:
            copy.wait()
        total += mul(hid_ref[...], w_ref[part])
    out_ref[...] = total.astype(LOW)


def result_block(line, tables, hids, mid, pieces, images, place, places, into):
    tokens, width = mid.shape
    group = grouped(images)
    seq = tokens // images * group
    steps = images // group // places
    row = pl.BlockSpec((seq, width), lambda i: (place * steps + i, 0))
    return line.call(
        result_kernel,
        (*tables, *hids, mid, *[piece for part in pieces for piece in part]),
        [SMEM, SMEM, row, row, row, row] + [ANY] * 24,
        grid=(steps,),
        into=into,
        out_specs=row,
        out_shape=jax.ShapeDtypeStruct((tokens, width), LOW),
        scratch_shapes=[pltpu.VMEM((3, width, width), LOW), pltpu.SemaphoreType.DMA((3, 8, 4))],
        compiler_params=params(1),
        cost_estimate=cost(6 * tokens * width * width, 20 << 20),
        name="result",
    )


def weight_kernel(lefts, table_ref, *refs):
    refs = list(refs)
    acts = [refs.pop(0) for _ in range(max(lefts) + 1)]
    grads = [refs.pop(0) for _ in lefts]
    outs = [refs.pop(0) for _ in range(8)]
    turned_ref, sems = refs
    rows = outs[0].shape[1]
    half = outs[0].shape[2]
    depth = turned_ref.shape[1]
    core = table_ref[32]
    step = pl.program_id(0)

    def copy(number, index):
        start = pl.multiple_of(index * 4 * rows, 16)
        return pltpu.make_async_copy(
            acts[number].at[pl.ds(start, 4 * rows)],
            turned_ref.at[number, index * 4 * rows : index * 4 * rows + 4 * rows],
            sems.at[number, index],
        )

    @pl.when(step == 0)
    def _():
        for number in range(len(acts)):
            for index in range(4):
                copy(number, index).start()

    for span, (left, grad_ref) in enumerate(zip(lefts, grads)):
        @pl.when(step == span)
        def _(span=span, left=left, grad_ref=grad_ref):
            if left not in lefts[:span]:
                for index in range(4):
                    copy(left, index).wait()
            for side in range(2):
                start = pl.multiple_of((core if side == 0 else 1 - core) * half, half)
                grad = grad_ref[:, pl.ds(start, half)]
                for pair in range(2):
                    parts = []
                    for index in range(8):
                        start = table_ref[side * 16 + pair * 8 + index] * rows
                        parts.append(turned_ref[left, pl.ds(pl.multiple_of(start, 16), rows), :])
                    total = mul(jnp.concatenate(parts, axis=0), grad)
                    for place in range(2):
                        out = outs[4 * side + 2 * pair + place]
                        part = total[place * 4 * rows : (place + 1) * 4 * rows]
                        out[...] = part.reshape(out.shape).astype(LOW)


def weight_halves(line, table, acts, spans):
    depth, tokens = acts[0].shape
    rows = depth // 16
    wide = spans[0][1].shape[1] // spans[0][3]
    half = wide // 2
    count = len(spans)

    def grad_spec(number, span):
        return pl.BlockSpec((tokens, wide), lambda m, t: (0, span))

    tile = pl.BlockSpec((4, rows, half), lambda m, t: (0, 0, m))
    shape = jax.ShapeDtypeStruct((4, rows, count * half), LOW)
    size = 2 * (tokens * (len(acts) * depth + count * wide) + depth * count * wide)
    outs = line.call(
        functools.partial(weight_kernel, [span[0] for span in spans]),
        (table, *acts, *[span[1] for span in spans]),
        [ANY for _ in acts] + [grad_spec(number, span[2]) for number, span in enumerate(spans)],
        prefetch=1,
        grid=(count,),
        out_specs=[tile] * 8,
        out_shape=[shape] * 8,
        scratch_shapes=[
            pltpu.VMEM((len(acts), depth, tokens), LOW), pltpu.SemaphoreType.DMA((len(acts), 4))
        ],
        compiler_params=params(1),
        cost_estimate=cost(2 * tokens * depth * count * wide, size),
        name="weight_grad",
    )
    return outs[:4], outs[4:]


def adam(weight, first, second, gradient, factor, rate, decay):
    clipped = gradient * factor
    new_first = BETA_ONE * first + (1.0 - BETA_ONE) * clipped
    new_second = BETA_TWO * second + (1.0 - BETA_TWO) * clipped * clipped
    denominator = jnp.sqrt(new_second / (1.0 - BETA_TWO**STEP)) + ADAM_EPS
    new_weight = (
        weight * (1.0 - rate * decay) - rate * (new_first / (1.0 - BETA_ONE**STEP)) / denominator
    )
    return (new_weight, new_first, new_second)


def adam_kernel(core_ref, total_ref, *refs):
    refs = list(refs)
    ada, qkv, out, up, down, scale = ([refs.pop(0) for _ in range(3)] for _ in range(6))
    ada_grad, head_grad = refs.pop(0), refs.pop(0)
    mines = [refs.pop(0) for _ in range(4)]
    others = [refs.pop(0) for _ in range(4)]
    norm_ref = refs.pop(0)
    new_ada, new_qkv, new_out, new_up, new_down, new_scale = ([refs.pop(0) for _ in range(3)] for _ in range(6))
    own_first = core_ref[0] == 0
    head = head_grad[...]
    total = total_ref[0:1, 0:1] + jnp.sum(head * head, axis=1, keepdims=True)
    norm = jnp.sqrt(total)
    factor = jnp.minimum(1.0, CLIP / (norm + 1e-06))

    def update(news, olds, at, gradient, rate, decay):
        weight, first, second = (ref[at] for ref in olds)
        for ref, value in zip(news, adam(weight, first, second, gradient, factor, rate, decay)):
            ref[at] = value

    @pl.when(pl.program_id(0) == 0)
    def _():
        norm_ref[...] = jnp.broadcast_to(norm, norm_ref.shape)
        update(new_scale, scale, (slice(None),) * 2, head, SCALE_RATE, 0.0)
        for index in range(ada_grad.shape[0]):
            update(new_ada, ada, (index,), ada_grad[index], RATE, DECAY)

    def columns(number, span):
        size = mines[0].shape[1] // 3
        mine = mines[number][:, span * size : span * size + size].astype(WIDE)
        other = others[number][:, span * size : span * size + size].astype(WIDE)
        return jnp.where(own_first, mine, other), jnp.where(own_first, other, mine)

    def by_halves(news, olds, number, spans, rate):
        for place, span in enumerate(spans):
            for half, gradient in enumerate(columns(number, span)):
                size = gradient.shape[1]
                start = (2 * place + half) * size
                update(news, olds, (slice(None), slice(start, start + size)), gradient, rate, DECAY)

    by_halves(new_qkv, qkv, 3, (0, 1, 2), RATE)
    by_halves(new_out, out, 2, (3,), OUTPUT_RATE)
    for part in range(3):
        for half, gradient in enumerate(columns(part, 2)):
            size = gradient.shape[1]
            update(new_down, down, (part, slice(None), slice(half * size, half * size + size)), gradient, RATE, DECAY)
    low = lax.broadcasted_iota(jnp.int32, (up[0].shape[0], 128), 1) < 64
    for span in range(2):
        parts = [columns(part, span) for part in range(3)]
        size = parts[0][0].shape[1]
        for half in range(2):
            for lane in range(0, size, 128):
                one, two, three = (parts[part][half][:, lane : lane + 128] for part in range(3))
                turned = pltpu.roll(two, 64, 1)
                start = 3 * ((2 * span + half) * size + lane)
                pieces = (jnp.where(low, one, turned), jnp.where(low, three, one), jnp.where(low, turned, three))
                for number, gradient in enumerate(pieces):
                    at = (slice(None), slice(start + 128 * number, start + 128 * number + 128))
                    update(new_up, up, at, gradient, RATE, DECAY)


def adam_all(line, core, total, ada, qkv, out, up, down, scale, ada_grad, head_grad, mines, others):
    steps = 4
    args = [core[None], total]
    in_specs = [SMEM, whole(total.shape)]
    out_specs = [whole(total.shape)]
    out_shape = [jax.ShapeDtypeStruct(total.shape, WIDE)]

    def by_rows(array):
        shape = array.shape[:-2] + (array.shape[-2] // steps, array.shape[-1])
        lead = (0,) * (array.ndim - 2)
        return pl.BlockSpec(shape, lambda i: lead + (i, 0))

    for group, cut in ((ada, False), (qkv, True), (out, True), (up, True), (down, True), (scale, False)):
        for array in group:
            spec = by_rows(array) if cut else whole(array.shape)
            args.append(array)
            in_specs.append(spec)
            out_specs.append(spec)
            out_shape.append(jax.ShapeDtypeStruct(array.shape, WIDE))
    args += [ada_grad, head_grad, *mines, *others]
    in_specs += [whole(ada_grad.shape), whole(head_grad.shape)] + [by_rows(m) for m in (*mines, *others)]
    return line.call(
        adam_kernel,
        args,
        in_specs,
        grid=(steps,),
        out_specs=out_specs,
        out_shape=out_shape,
        compiler_params=params(1),
        cost_estimate=cost(0, 30 << 20),
        name="adamw",
    )


def turn_kernel(shapes_ref, rates_ref, cos_ref, up_ref, down_ref, valid_ref):
    image = pl.program_id(0)
    height, width = shapes_ref[image, 0], shapes_ref[image, 1]
    shape = cos_ref.shape
    slot = lax.broadcasted_iota(jnp.int32, shape, 0)
    place = slot.astype(WIDE)
    wide = width.astype(WIDE)
    row = jnp.floor((place + 0.5) / wide)
    angle = row * rates_ref[0:1, :] + (place - row * wide) * rates_ref[1:2, :]
    lane = lax.broadcasted_iota(jnp.int32, shape, 1) % 64
    cosine, sine = jnp.cos(angle), jnp.sin(angle)
    cos_ref[...] = jnp.where(lane < 32, cosine, 1.0)
    up_ref[...] = jnp.where(lane < 16, -sine, 0.0)
    down_ref[...] = jnp.where((lane >= 16) & (lane < 32), sine, 0.0)
    valid_ref[...] = jnp.where(slot < height * width, 1.0, 0.0).astype(LOW)


def turn_tables(line, shapes, seq_len, head_dim):
    images = shapes.shape[0]
    count = head_dim // 8
    frequency = ROPE_BASE ** (-jnp.arange(count, dtype=WIDE) / count)
    none = jnp.zeros((count,), WIDE)
    blank = jnp.zeros((head_dim // 2,), WIDE)
    rates = jnp.stack(
        [
            jnp.concatenate([frequency, none, frequency, none, blank] * 2),
            jnp.concatenate([none, frequency, none, frequency, blank] * 2),
        ]
    )
    block = pl.BlockSpec((seq_len, 128), lambda i: (i, 0))
    wide = jax.ShapeDtypeStruct((images * seq_len, 128), WIDE)
    *turns, valid = line.call(
        turn_kernel,
        (shapes, rates),
        [SMEM, whole(rates.shape)],
        grid=(images,),
        out_specs=[block] * 4,
        out_shape=[wide, wide, wide, jax.ShapeDtypeStruct(wide.shape, LOW)],
        compiler_params=params(1),
        cost_estimate=cost(0, 2 << 20),
        name="turns",
    )
    return tuple(turns), valid


def head_matrices(width, head_dim):
    heads = width // head_dim
    owner = np.arange(width) // head_dim
    sums = np.zeros((2, width, 128), np.float32)
    spread = np.zeros((2, 128, width), np.float32)
    for side in range(2):
        for copy in range(2):
            sums[side, np.arange(width), side * heads + copy * 2 * heads + owner] = 1.0
            spread[side, side * heads + copy * 2 * heads + owner, np.arange(width)] = 1.0
    pick = np.zeros((heads, width), np.float32)
    pick[owner, np.arange(width)] = 1.0
    block = np.kron(np.eye(128 // head_dim), np.ones((head_dim, head_dim)))
    return tuple(jnp.asarray(m, LOW) for m in (sums, spread, pick, block))


def finish_wide(net, ada, qkv, out, up, down, scale, grad_ada, head_grad, mines, others):
    def columns(number, span):
        size = mines[0].shape[1] // 3
        mine = mines[number][:, span * size : span * size + size]
        other = others[number][:, span * size : span * size + size]
        pair = [jnp.where(net.core == 0, mine, other), jnp.where(net.core == 0, other, mine)]
        return jnp.concatenate(pair, axis=1).astype(WIDE)

    grad_up = [
        jnp.concatenate([columns(part, span) for span in range(2)], axis=1).reshape(-1, 2, 16, 64)
        for part in range(3)
    ]
    gradients = [
        jnp.concatenate([columns(3, span) for span in range(3)], axis=1),
        columns(2, 3),
        jnp.stack(grad_up, axis=3).reshape(-1, up[0].shape[1]),
        jnp.concatenate([columns(part, 2) for part in range(3)], axis=0),
    ]
    gradients = [grad_ada] + [net.split_sub(gradient) for gradient in gradients]
    total = lax.psum(sum(jnp.sum(gradient * gradient) for gradient in gradients), "fsdp")
    head_grad = head_grad[0]
    norm = jnp.sqrt(total + jnp.sum(head_grad * head_grad))
    factor = jnp.minimum(1.0, CLIP / (norm + 1e-06))
    rates = (RATE, RATE, OUTPUT_RATE, RATE, RATE)
    news = [norm]
    for group, gradient, rate in zip((ada, qkv, out, up, down), gradients, rates):
        news += adam(*group, gradient, factor, rate, DECAY)
    news += adam(*scale, head_grad, factor, SCALE_RATE, 0.0)
    return tuple(news)


def local(
    tokens,
    condition,
    shapes,
    cotangent,
    ada_weight,
    ada_first,
    ada_second,
    qkv_weight,
    qkv_first,
    qkv_second,
    out_weight,
    out_first,
    out_second,
    up_weight,
    up_first,
    up_second,
    down_weight,
    down_first,
    down_second,
    head_scale,
    scale_first,
    scale_second,
    *,
    dp_size,
    fsdp_size,
):
    net = Net(fsdp_size, dp_size)
    line = Line()
    core = net.core
    images = shapes.shape[0]
    width = tokens.shape[1]
    seq_len = tokens.shape[0] // images
    head_count = head_scale.shape[0]
    head_dim = width // head_count
    small = net.sub == 1
    even, odd = net.tables

    ada_joined = net.join_sub(ada_weight.transpose(1, 0, 2)).transpose(1, 0, 2) if net.sub > 1 else ada_weight
    half_qk, half_vo = head_parts(
        line, core, net.join_sub(qkv_weight), net.join_sub(out_weight), ada_joined
    )
    get_qk = Gather(net, line, 0, half_qk)
    down_joined = net.join_sub(down_weight).reshape(3, -1, width)
    halves = cut_parts(line, core, net.join_sub(up_weight), down_joined)
    get_qk.second()
    get_vo = Gather(net, line, 1, half_vo)
    turns, valid = turn_tables(line, shapes, seq_len, head_dim)
    sums, spread, pick, block = head_matrices(width, head_dim)
    root = jnp.repeat(jnp.sqrt(head_scale), head_dim)[None]
    get_vo.wait()
    get_qk.third()
    get_vo.second()
    get_vo.wait()
    get_qk.wait_near()
    get_vo.third()
    get_qk.fourth()
    get_mlp = [Gather(net, line, 1, halves[0])]
    get_qk.wait_last()
    get_mlp[0].second()
    get_mlp.append(Gather(net, line, 0, halves[1]))
    get_qk.finish()

    act_one, q, k, pack, scale_one = front(
        line, even, tokens, condition, get_qk.pieces, sums, spread, root, turns, images
    )
    get_mlp[0].third()
    get_vo.fourth()
    get_vo.finish()
    v, o, o_turned, lse = attend(
        line, odd, q, k, valid, tokens, scale_one, get_vo.pieces, images
    )
    get_mlp[1].second()
    get_mlp[0].fourth()
    mid, act_two, act_two_turned, scale_two = middle_block(
        line, odd, o, tokens, condition, get_vo.pieces, images
    )
    get_mlp[1].third()
    get_mlp[0].finish()
    get_mlp.append(Gather(net, line, 1, halves[2]))

    def put(parity, acts, spans):
        return Scatter(net, line, parity, *weight_halves(line, net.tables[parity], acts, spans))

    def mlp_spans(hid_turned, dgu):
        return ((act_two_turned, hid_turned), ((0, dgu, 0, 2), (0, dgu, 1, 2), (1, cotangent, 0, 1)))

    hid0, dgu0, turned0, acc = geglu_part(line, odd, act_two, cotangent, get_mlp[0].pieces, images)
    get_mlp[2].second()
    get_mlp[1].fourth()
    put0 = put(0, *mlp_spans(turned0, dgu0))
    get_mlp[2].third()
    get_mlp[1].finish()
    hid1, dgu1, turned1, acc = geglu_part(
        line, even, act_two, cotangent, get_mlp[1].pieces, images, acc
    )
    get_mlp[2].fourth()
    put0.start()
    put1 = put(1, *mlp_spans(turned1, dgu1))
    put0.first()
    get_mlp[2].finish()
    hid2, dgu2, turned2, dmid, db, do, dscale_two = geglu_part(
        line, odd, act_two, cotangent, get_mlp[2].pieces, images, acc,
        (mid, scale_two, odd, get_vo.pieces),
    )
    put0.second()
    put1.start()
    acts2, spans2 = mlp_spans(turned2, dgu2)
    put2 = put(0, acts2 + (o_turned,), spans2 + ((2, db, 0, 1),))
    put0.third()
    put1.first()
    dproj, dhead = attend_back(
        line, q, k, v, o, do, lse, valid, pack, spread, root, pick, block, turns, images
    )
    put0.fourth()
    put1.second()
    put2.start()
    put_qkv = put(1, (act_one,), tuple((0, dproj, span, 3) for span in range(3)))
    put0.finish()
    put1.third()
    put2.first()
    put_qkv.start()

    places = 2 if images % (2 * grouped(images)) == 0 else 1

    def result(place, into=None):
        return result_block(
            line, net.tables, (hid0, hid1, hid2), mid, [get.pieces for get in get_mlp], images,
            place, places, into,
        )

    qkv_pieces = get_qk.pieces + get_vo.pieces

    def to_input(place, into=None):
        return input_block(
            line, net.tables, dproj, tokens, dmid, scale_one, qkv_pieces, images, place, places, into
        )

    input_grad, dscale_one = to_input(0)
    put1.fourth()
    put2.second()
    put_qkv.first()
    if places > 1:
        input_grad, rest = to_input(1, input_grad)
        dscale_one = jnp.concatenate([dscale_one, rest], axis=0)
    put1.finish()
    put2.third()
    put_qkv.second()

    dhead = jnp.sum(dhead, axis=0)
    rows = jnp.concatenate([dscale_one[:, 0], dscale_two[:, 0], condition.astype(WIDE)], axis=1)
    if small:
        high = dhead.astype(LOW)
        rest = (dhead - high.astype(WIDE)).astype(LOW)
        heads = jnp.concatenate([high, rest, jnp.zeros((6, 128), LOW)], axis=0)
        rows = jnp.concatenate([rows.astype(LOW).reshape(1, -1, 128), heads[None]], axis=1)
        late = SmallGather(net, line, rows)
        late.step((4, 8, 12))
    block_output = result(0)
    put_qkv.third()
    put2.fourth()
    if small:
        late.step((1, 2, 3))
    if places > 1:
        block_output = result(1, block_output)
    put_qkv.fourth()
    put2.finish()
    if small:
        late.step()
        rows = late.held[:, :-8].reshape(32 * images, -1).astype(WIDE)
        dhead = jnp.sum(late.held[:, -8:-6].astype(WIDE), axis=(0, 1))[None]
    else:
        rows = lax.all_gather(rows, AXES, axis=0, tiled=True)
        dhead = lax.psum(dhead, AXES)
    own_rows = ada_weight.shape[1]
    own_start = 2 * width + lax.axis_index("fsdp") * own_rows
    cond_own = lax.dynamic_slice_in_dim(rows, own_start, own_rows, axis=1)
    grad_ada = jnp.stack(
        [jnp.dot(cond_own.T, rows[:, :width], precision=PRECISE),
         jnp.dot(cond_own.T, rows[:, width : 2 * width], precision=PRECISE)]
    )
    head_grad = dhead[:, :head_count] / (2.0 * head_scale)
    ada_square = line.pin(0.5 * jnp.sum(grad_ada * grad_ada))
    grad_ada, head_grad = line.pin(grad_ada), line.pin(head_grad)
    put_qkv.finish()
    puts = (put0, put1, put2, put_qkv)
    mines = tuple(each.mine for each in puts)
    others = tuple(each.other for each in puts)
    ada = (ada_weight, ada_first, ada_second)
    qkv = (qkv_weight, qkv_first, qkv_second)
    out = (out_weight, out_first, out_second)
    up = (up_weight, up_first, up_second)
    down = (down_weight, down_first, down_second)
    scale = (head_scale, scale_first, scale_second)
    if not small:
        return (block_output, input_grad) + finish_wide(
            net, ada, qkv, out, up, down, scale, grad_ada, head_grad, mines, others
        )
    local_squares = sum(each.square for each in puts) + ada_square
    total = net.total(local_squares)
    rows = down_weight.shape[0] // 3
    news = adam_all(
        line, core, total, ada, qkv, out, up,
        tuple(array.reshape(3, rows, width) for array in down),
        tuple(array[None] for array in scale), grad_ada, head_grad, mines, others,
    )
    return (
        block_output,
        input_grad,
        news[0][0, 0],
        *news[1:13],
        *[array.reshape(down_weight.shape) for array in news[13:16]],
        *[array[0] for array in news[16:19]],
    )


def solution(mesh):
    tokens = P(("dp", "fsdp"), None)
    ada = P(None, "fsdp", None)
    rows = P("fsdp", None)
    return jax.shard_map(
        functools.partial(local, dp_size=mesh.shape["dp"], fsdp_size=mesh.shape["fsdp"]),
        mesh=mesh,
        in_specs=(tokens,) * 4 + (ada,) * 3 + (rows,) * 12 + (P(),) * 3,
        out_specs=(tokens, tokens, P()) + (ada,) * 3 + (rows,) * 12 + (P(),) * 3,
        check_vma=False,
    )
```
